32 devices in a mesh: dp: 8 (over y, x, core), tensor: 4 (over z).
Axes of the slice: x: 2, y: 2, z: 4, core: 2. Of those that a mesh axis runs over, the one named last changes fastest.
Arguments:
- inputs: bfloat16 [2048, 768], P('dp'), may hold values from -6 to 6
- segments: int32 [8, 256], P('dp'), may hold values from 0 to 3, never falling along the last dimension, each value on 1 to 128 neighbouring positions
- buckets: int32 [511], replicated, may hold values from 0 to 31
- routes: int32 [2048], P('dp'), may hold values from 0 to 1, as said below
- capacity_slots: int32 [2048], P('dp'), may hold values from 0 to 143, as said below
- gain_attn: float32 [768], replicated, may hold values from 0.25 to 1.75
- bias_table: float32 [32, 12], P(None, 'tensor'), may hold values from -4 to 4
- query_weight: bfloat16 [768, 768], P(None, 'tensor'), may hold values from -0.0546875 to 0.0546875
- key_weight: bfloat16 [768, 768], P(None, 'tensor'), may hold values from -0.21875 to 0.21875
- value_weight: bfloat16 [768, 768], P(None, 'tensor'), may hold values from -0.21875 to 0.21875
- out_weight: bfloat16 [768, 768], P('tensor'), may hold values from -0.875 to 0.875
- gain_expert: float32 [768], replicated, may hold values from 0.25 to 1.75
- router_weight: bfloat16 [768, 2], replicated, may hold values from -0.15625 to 0.15625
- expert_up: bfloat16 [2, 768, 3072], P(None, None, 'tensor'), may hold values from -0.21875 to 0.21875
- expert_down: bfloat16 [2, 3072, 768], P(None, 'tensor'), may hold values from -0.21875 to 0.21875
- cotangent: bfloat16 [2048, 768], P('dp'), may hold values from -6 to 6
Outputs:
- output: bfloat16 [2048, 768], P('dp')
- grad_inputs: bfloat16 [2048, 768], P('dp')
- grad_gain_attn: float32 [768], P(('dp', 'tensor'))
- grad_table: float32 [32, 12], P(None, 'tensor')
- grad_query_weight: float32 [768, 768], P('dp', 'tensor')
- grad_key_weight: float32 [768, 768], P('dp', 'tensor')
- grad_value_weight: float32 [768, 768], P('dp', 'tensor')
- grad_out_weight: float32 [768, 768], P('tensor', 'dp')
- grad_gain_expert: float32 [768], P(('dp', 'tensor'))
- grad_router: float32 [768, 2], P(('dp', 'tensor'))
- grad_expert_up: float32 [2, 768, 3072], P(None, 'dp', 'tensor')
- grad_expert_down: float32 [2, 3072, 768], P(None, 'tensor', 'dp')
The draws below stay inside these ranges and needn't reach their ends.
Inputs may be any that keep to these rules, and one draw needn't show every extreme that they name: `routes`: in each sequence one expert receives exactly 144 tokens and every other fewer. `capacity_slots`: within one sequence, tokens of the same expert have distinct slots. `buckets`: the bucket of the offset j - i stands at index j - i + 255.
All inputs are finite; a program needn't handle non-finite values.
Results may differ from the reference program's by a relative error of at most 0.018.
Values may be sent and summed in bfloat16 or wider, within the bound.
No kernel may reach another device: no remote copies, remote signals or barrier semaphores. Data moves between devices by JAX's collectives and lax.ppermute only.
A program may use at most 128 MiB of HBM per device.

```python
import math
import jax
import jax.numpy as jnp
import numpy as np
from jax import lax

D = 768
HEADS = 12
HEAD_DIM = 64
FF = 3072
NUM_BUCKETS = 32
EXPERTS = 2
LEN = 256
CAP = 144
TOKENS = 2048
N_DP = 8


def shuffled_tokens(subkey):
    return jax.random.permutation(subkey, LEN).astype(jnp.int32)


def shuffled_slots(subkey):
    return jax.random.permutation(subkey, CAP).astype(jnp.int32)


def route_table(key):
    seq_count = TOKENS // LEN
    full_expert = jax.random.randint(jax.random.fold_in(key, 101), (seq_count, 1), 0, EXPERTS).astype(jnp.int32)
    token_rank = jax.vmap(shuffled_tokens)(jax.random.split(jax.random.fold_in(key, 102), seq_count))
    shift_by = jax.random.randint(jax.random.fold_in(key, 103), (seq_count, LEN), 1, EXPERTS).astype(jnp.int32)
    route_rows = jnp.where(token_rank < CAP, full_expert, (full_expert + shift_by) % EXPERTS).astype(jnp.int32)
    one_hot = (route_rows[:, :, None] == jnp.arange(EXPERTS, dtype=jnp.int32)[None, None, :]).astype(jnp.int32)
    within = jnp.sum((jnp.cumsum(one_hot, axis=1) - 1) * one_hot, axis=2).astype(jnp.int32)
    slot_order = jax.vmap(shuffled_slots)(jax.random.split(jax.random.fold_in(key, 104), seq_count * EXPERTS))
    slot_order = slot_order.reshape(seq_count, EXPERTS * CAP)
    slot_rows = jnp.take_along_axis(slot_order, route_rows * CAP + within, axis=1)
    return (route_rows.reshape(-1).astype(jnp.int32), slot_rows.reshape(-1).astype(jnp.int32))


def draw_routes(key, part):
    return route_table(key)[0]


def draw_capacity_slots(key, part):
    return route_table(key)[1]


def with_ends(drawn, key, smallest, high):
    index_at = [jax.random.randint(jax.random.fold_in(key, axis), (), 0, length) for axis, length in enumerate(drawn.shape)]
    main_axis = drawn.shape.index(max(drawn.shape))
    neighbour = index_at[:main_axis] + [(index_at[main_axis] + 1) % drawn.shape[main_axis]] + index_at[main_axis + 1:]
    return drawn.at[tuple(index_at)].set(smallest).at[tuple(neighbour)].set(high)


def raised(array, key, source, target, parts, factor):
    def block_of(dim):
        return (jnp.arange(array.shape[dim]) // (array.shape[dim] // parts)).reshape((-1,) + (1,) * (array.ndim - 1 - dim))

    first = jax.random.permutation(key, parts)[block_of(target)]
    other_side = (block_of(target) + parts // 2) % parts
    return jnp.where((block_of(source) == first) | (block_of(source) == other_side), factor * array, array)


def steps_of(rng, shape, cuts, low, high):
    level, own = 1.0, jax.random.fold_in(rng, 6)
    for dim, shards_of in cuts:
        steps = jnp.exp(jax.random.uniform(jax.random.fold_in(own, dim), (shards_of,), jnp.float32, low / len(cuts), high / len(cuts)))
        level = level * jnp.repeat(steps, shape[dim] // shards_of).reshape([-1 if axis == dim else 1 for axis in range(len(shape))])
    return level


def length_profile(amount, total, bound, lean):
    loads = [(1 << 20) // math.isqrt(standing ** lean) + 1 for standing in range(2, amount + 1)]
    rest, given = total - bound - (amount - 1), [1] * (amount - 1)
    while rest > 0:
        candidates = [i for i in range(amount - 1) if given[i] < bound]
        mass, left = sum([loads[i] for i in candidates]), rest
        for i in candidates:
            extra = min(bound - given[i], max(1, left * loads[i] // mass), rest)
            given[i] = given[i] + extra
            rest = rest - extra
    return np.array([bound] + given)


def uneven_parts(rng, number_of, total, bound, lean):
    if number_of == 2:
        one = jax.random.randint(rng, (), max(1, total - bound), min(bound, total - 1) + 1)
        return jnp.stack([one, total - one])
    lengths = jnp.asarray(length_profile(number_of, total, bound, lean), jnp.int32)
    couples = (number_of - 1) // 2
    source_of, sink = lengths[1:1 + 2 * couples:2], lengths[2:2 + 2 * couples:2]
    slack = jnp.minimum(source_of - 1, bound - sink)
    shifted = jax.random.randint(jax.random.fold_in(rng, 1), (couples,), 0, 1 << 20) % (slack + 1)
    lengths = lengths.at[1:1 + 2 * couples:2].set(source_of - shifted).at[2:2 + 2 * couples:2].set(sink + shifted)
    return lengths[jax.random.permutation(jax.random.fold_in(rng, 2), number_of)]


def bell_draw(stream_key, extent, scale, bound, cuts=(), kind=jnp.bfloat16):
    entries = jax.random.normal(stream_key, extent, jnp.float32) * scale
    if len(cuts) > 0:
        entries = steps_of(stream_key, extent, cuts, -0.22, 0.18) * entries
    return jnp.clip(entries, min=-bound, max=bound).astype(kind)


def bell_draw_with(rng, shape, scale, most, shards, heavy, kind=jnp.bfloat16):
    values = scale * jax.random.normal(rng, shape, jnp.float32)
    if shards:
        values = values * steps_of(rng, shape, shards, -0.22, 0.18)
    return jnp.clip(raised(values, jax.random.fold_in(rng, 3), *heavy), -most, most).astype(kind)


def setup_inputs(seed: int = 0) -> dict:
    key_of = jax.random.split(jax.random.key(seed), 17)
    return {
        "inputs": bell_draw_with(key_of[0], (TOKENS, D), 1.0, 6.0, ((0, 8),), (0, 1, 8, 2.0)),
        "segments": jax.vmap(lambda own: jnp.searchsorted(jnp.cumsum(uneven_parts(own, 4, LEN, LEN // 2, 0)), jnp.arange(LEN), side="right"))(jax.random.split(key_of[1], N_DP)).reshape((N_DP, LEN)).astype(jnp.int32),
        "buckets": with_ends(jax.random.randint(key_of[2], (2 * LEN - 1,), 0, NUM_BUCKETS), jax.random.fold_in(key_of[2], 1), 0, NUM_BUCKETS - 1).astype(jnp.int32),
        "routes": draw_routes(jax.random.fold_in(key_of[16], 71), 0),
        "capacity_slots": draw_capacity_slots(jax.random.fold_in(key_of[16], 71), 0),
        "gain_attn": jnp.clip(1.0 + 0.15 * jax.random.normal(key_of[5], (D,), jnp.float32), 0.25, 1.75),
        "bias_table": bell_draw(key_of[6], (NUM_BUCKETS, HEADS), 1.0, 4.0, ((1, 4),), jnp.float32),
        "query_weight": bell_draw(key_of[7], (D, HEADS * HEAD_DIM), (16 * D) ** -0.5, 0.0546875, ((1, 4),)),
        "key_weight": bell_draw(key_of[8], (D, HEADS * HEAD_DIM), D ** -0.5, 0.21875, ((1, 4),)),
        "value_weight": bell_draw(key_of[9], (D, HEADS * HEAD_DIM), D ** -0.5, 0.21875, ((1, 4),)),
        "out_weight": bell_draw(key_of[10], (HEADS * HEAD_DIM, D), (HEADS * HEAD_DIM // 16) ** -0.5, 0.875, ((0, 4),)),
        "gain_expert": jnp.clip(1.0 + 0.15 * jax.random.normal(key_of[11], (D,), jnp.float32), 0.25, 1.75),
        "router_weight": bell_draw(key_of[12], (D, EXPERTS), (2 * D) ** -0.5, 0.15625),
        "expert_up": bell_draw(key_of[13], (EXPERTS, D, FF), D ** -0.5, 0.21875, ((2, 4),)),
        "expert_down": bell_draw(key_of[14], (EXPERTS, FF, D), (FF // 4) ** -0.5, 0.21875, ((1, 4),)),
        "cotangent": bell_draw_with(key_of[15], (TOKENS, D), 1.0, 6.0, ((0, 8),), (0, 1, 8, 2.0)),
    }


highest = lax.Precision.HIGHEST

@jax.custom_vjp
def low(v):
    return lax.optimization_barrier(v.astype(jnp.bfloat16)).astype(jnp.float32)

@jax.custom_vjp
def low_back(v):
    return v

def low_keep(v):
    return (low(v), None)

def low_pass(kept, grad):
    return (grad,)

def back_keep(v):
    return (v, None)

def back_low(kept, grad):
    return (low(grad),)
low.defvjp(low_keep, low_pass)
low_back.defvjp(back_keep, back_low)

def norm_rows(values, gains):
    return values * lax.rsqrt(lax.optimization_barrier(jnp.mean(values * values, axis=-1, keepdims=True)) + 1e-06) * gains

def encoder_layer(params, inputs, segment, route_row, slot_row, buckets):
    gain_attn, bias_table, query_weight, key_weight, value_weight, out_weight, gain_expert, router_weight, expert_up, expert_down = params
    length = inputs.shape[0]
    normed = low(norm_rows(inputs, gain_attn))

    def project(weight):
        projected = jnp.dot(normed, weight, precision=highest)
        return low(low_back(projected)).reshape(length, HEADS, HEAD_DIM)
    queries, key_rows, value_rows = (project(query_weight), project(key_weight), project(value_weight))
    offsets = jnp.arange(length)[None, :] - jnp.arange(length)[:, None] + length - 1
    pos_bias = jnp.transpose(bias_table[buckets[offsets]], (2, 0, 1))
    scores = jnp.einsum('qhd,khd->hqk', queries, key_rows, precision=highest) + pos_bias
    scores = low_back(scores)
    same_doc = segment[:, None] == segment[None, :]
    scores = jnp.where(same_doc[None], scores, -1e+30)
    weights = low(jax.nn.softmax(scores, axis=-1))
    mixed = jnp.einsum('hqk,khd->qhd', weights, value_rows, precision=highest).reshape(length, HEADS * HEAD_DIM)
    mixed = low(low_back(mixed))
    attended = low_back(jnp.dot(mixed, out_weight, precision=highest))
    hidden = inputs + attended
    normed_two = low(norm_rows(hidden, gain_expert))
    logits = jnp.dot(normed_two, router_weight, precision=highest)
    router_probs = jax.nn.softmax(logits, axis=-1)
    chosen = (route_row[:, None] == jnp.arange(EXPERTS)[None, :]).astype(jnp.float32)
    gate_value = lax.optimization_barrier(jnp.sum(router_probs * chosen, axis=-1))
    where_to = route_row * CAP + slot_row
    buffer = jnp.zeros((EXPERTS * CAP, inputs.shape[1]), jnp.float32).at[where_to].set(normed_two)
    buffer = buffer.reshape(EXPERTS, CAP, inputs.shape[1])
    before = low_back(jnp.einsum('ecd,edf->ecf', buffer, expert_up, precision=highest))
    active = low(jax.nn.gelu(before))
    result = jnp.einsum('ecf,efd->ecd', active, expert_down, precision=highest).reshape(EXPERTS * CAP, inputs.shape[1])
    expert_rows = low_back(result[where_to])
    return hidden + gate_value[:, None] * expert_rows

def reference(inputs, segments, buckets, routes, capacity_slots, gain_attn, bias_table, query_weight, key_weight, value_weight, out_weight, gain_expert, router_weight, expert_up, expert_down, cotangent):
    params = tuple((argument.astype(jnp.float32) for argument in (gain_attn, bias_table, query_weight, key_weight, value_weight, out_weight, gain_expert, router_weight, expert_up, expert_down)))
    seq_count = TOKENS // LEN
    wide_inputs = inputs.astype(jnp.float32).reshape(seq_count, LEN, D)
    route_rows = routes.reshape(seq_count, LEN)
    slot_rows = capacity_slots.reshape(seq_count, LEN)
    step_layer = jax.checkpoint(encoder_layer)

    def forward(layer_inputs, layer_params):

        def per_sequence(pieces):
            block_inputs, segment, route_row, slot_row = pieces
            return step_layer(layer_params, block_inputs, segment, route_row, slot_row, buckets)
        return lax.map(per_sequence, (layer_inputs, segments, route_rows, slot_rows))
    outputs, pullback = jax.vjp(forward, wide_inputs, params)
    grad_wide, grads = pullback(cotangent.astype(jnp.float32).reshape(seq_count, LEN, D))
    return (outputs.reshape(TOKENS, D).astype(jnp.bfloat16), grad_wide.reshape(TOKENS, D).astype(jnp.bfloat16), grads[0], grads[1], grads[2], grads[3], grads[4], grads[5], grads[6], grads[7], grads[8], grads[9])
```

```python
import functools

import jax
import jax.numpy as jnp
from jax import lax
from jax.experimental import pallas as pl
from jax.experimental.pallas import tpu as pltpu
from jax.sharding import PartitionSpec as P

HEAD_DIM = 64
EXPERTS = 2
CAP = 144
EPS = 1e-06
SMALL_ROWS = 16
BF16 = jnp.bfloat16
F32 = jnp.float32
HIGHEST = lax.Precision.HIGHEST
NT = (((1,), (1,)), ((), ()))
TN = (((0,), (0,)), ((), ()))
GELU_C = 0.7978845608028654
GELU_A = 0.044715


def dot(a, b):
    return jnp.dot(a, b, preferred_element_type=F32)


def dot_nt(a, b, precision=None):
    return lax.dot_general(a, b, NT, preferred_element_type=F32, precision=precision)


def dot_tn(a, b):
    return lax.dot_general(a, b, TN, preferred_element_type=F32)


def inverse_rms(values):
    return lax.rsqrt(jnp.mean(values * values, axis=-1, keepdims=True) + EPS)


def share_of(index, rows):
    return pl.ds(pl.multiple_of(index * rows, rows), rows)


def put_shares(acc_ref, share_refs):
    me = lax.axis_index("tensor")
    for k, ref in enumerate(share_refs):
        rows = ref.shape[0]
        ref[...] = acc_ref[share_of(jnp.bitwise_xor(me, k), rows), :].astype(ref.dtype)


def assemble(full_ref, share_refs):
    me = lax.axis_index("tensor")
    for k, ref in enumerate(share_refs):
        rows = ref.shape[0]
        full_ref[share_of(jnp.bitwise_xor(me, k), rows), :] = ref[...]


def total_of(refs):
    total = refs[0][...].astype(F32)
    for ref in refs[1:]:
        total = total + ref[...].astype(F32)
    return total


def column_of(row, length):
    eye = lax.broadcasted_iota(jnp.int32, (length, length), 0) == lax.broadcasted_iota(
        jnp.int32, (length, length), 1
    )
    return jnp.sum(jnp.where(eye, row, jnp.zeros_like(row)), axis=1, keepdims=True)


def head_mask(head, width):
    lane = lax.broadcasted_iota(jnp.int32, (1, width), 1)
    return (lane >= head * HEAD_DIM) & (lane < (head + 1) * HEAD_DIM)


def masked(values, head):
    return jnp.where(head_mask(head, values.shape[1]), values, jnp.zeros_like(values))


def bucket_hot_of(buckets_ref, bucket_count):
    offsets = buckets_ref.shape[1]
    return (
        lax.broadcasted_iota(jnp.int32, (bucket_count, offsets), 0) == buckets_ref[...]
    ).astype(F32)


def attention_kernel(members, inputs, segment, buckets, gain, table, wq, wk, wv, wo, *rest):
    outs = rest[: members + 6]
    normed_o, q_o, k_o, v_o, probs_o, mixed_o = outs[members:]
    acc, offset_rows = rest[members + 6 :]
    length = inputs.shape[0]
    heads = wq.shape[1] // HEAD_DIM
    x = inputs[...].astype(F32)
    normed = (x * inverse_rms(x) * gain[...]).astype(BF16)
    normed_o[...] = normed
    q = dot(normed, wq[...]).astype(BF16)
    k = dot(normed, wk[...]).astype(BF16)
    v = dot(normed, wv[...]).astype(BF16)
    q_o[...] = q
    k_o[...] = k
    v_o[...] = v
    hot = bucket_hot_of(buckets, table.shape[0])
    seg_row = segment[...].astype(F32)
    same = column_of(seg_row, length) == seg_row
    mixed = jnp.zeros((length, wq.shape[1]), F32)
    offset_rows[...] = jnp.zeros_like(offset_rows)
    for h in range(heads):
        offset_rows[h : h + 1, 0 : hot.shape[1]] = jnp.sum(
            hot * table[:, h : h + 1], axis=0, keepdims=True
        )
    for h in range(heads):
        spread = jnp.broadcast_to(offset_rows[h : h + 1, :], (length, 2 * length))
        bias = pltpu.roll(spread, length + 1, 1, stride=1, stride_axis=0)[:, :length]
        scores = dot_nt(masked(q, h), k) + bias
        scores = jnp.where(same, scores, -1e30)
        shifted = jnp.exp(scores - jnp.max(scores, axis=-1, keepdims=True))
        probs = shifted / jnp.sum(shifted, axis=-1, keepdims=True)
        probs_o[h] = probs
        mixed = mixed + dot(probs.astype(BF16), masked(v, h))
    mixed = mixed.astype(BF16)
    mixed_o[...] = mixed
    acc[...] = dot(mixed, wo[...])
    put_shares(acc, outs[:members])


def hidden_kernel(members, inputs, gain, *rest):
    parts = rest[:members]
    hidden_o, normed_o = rest[members:]
    share = hidden_o.shape[0]
    x = inputs[share_of(lax.axis_index("tensor"), share), :].astype(F32)
    hidden = x + total_of(parts)
    hidden_o[...] = hidden
    normed_o[...] = (hidden * inverse_rms(hidden) * gain[...]).astype(BF16)


def expert_kernel(members, where_to, cotangent, router_t, up, down, *rest):
    pieces = rest[:members]
    rest = rest[members:]
    back_o, row_o = rest[:members], rest[members : 2 * members]
    buffer_o, active_o, grad_before_o, grad_expert_o, router_o = rest[2 * members : 2 * members + 5]
    normed, backs, rows, acc = rest[2 * members + 5 :]
    length = cotangent.shape[0]
    assemble(normed, pieces)
    place = (
        lax.broadcasted_iota(jnp.int32, (EXPERTS * CAP, length), 0) == where_to[...]
    ).astype(BF16)
    buffer = dot(place, normed[...]).astype(BF16)
    buffer_o[...] = buffer
    dy_buffer = dot(place, cotangent[...])
    router_rows = router_t[...].astype(F32)
    router_grad = [jnp.zeros((1, buffer.shape[1]), F32) for _ in range(EXPERTS)]
    for e in range(EXPERTS):
        slot = slice(e * CAP, (e + 1) * CAP)
        rows_in = buffer[slot]
        logits = dot_nt(rows_in, router_t[...])
        shifted = jnp.exp(logits - jnp.max(logits, axis=-1, keepdims=True))
        router_probs = shifted / jnp.sum(shifted, axis=-1, keepdims=True)
        gate = router_probs[:, e : e + 1]
        dy = dy_buffer[slot]
        grad_expert = (dy * gate).astype(BF16)
        grad_expert_o[slot, :] = grad_expert
        before = dot(rows_in, up[e])
        inner = jnp.tanh(GELU_C * (before + GELU_A * before * before * before))
        active = (0.5 * before * (1.0 + inner)).astype(BF16)
        active_o[slot, :] = active
        slope = 0.5 * (1.0 + inner) + 0.5 * before * (1.0 - inner * inner) * GELU_C * (
            1.0 + 3.0 * GELU_A * before * before
        )
        result = dot(active, down[e])
        grad_before = (dot_nt(grad_expert, down[e]) * slope).astype(BF16)
        grad_before_o[slot, :] = grad_before
        rows[slot, :] = (result * gate).astype(BF16)
        scaled = jnp.sum(dy * result, axis=-1, keepdims=True) * gate
        back = dot_nt(grad_before, up[e])
        for other in range(EXPERTS):
            own = 1.0 if other == e else 0.0
            grad_logit = scaled * (own - router_probs[:, other : other + 1])
            router_grad[other] = router_grad[other] + jnp.sum(
                grad_logit * rows_in.astype(F32), axis=0, keepdims=True
            )
            back = back + grad_logit * router_rows[other : other + 1, :]
        backs[slot, :] = back.astype(BF16)
    for other in range(EXPERTS):
        router_o[other : other + 1, :] = router_grad[other]
    acc[...] = dot_tn(place, backs[...])
    put_shares(acc, back_o)
    acc[...] = dot_tn(place, rows[...])
    put_shares(acc, row_o)


def split_rows(keep, send, chip, part):
    core = lax.rem(lax.axis_index("dp"), 2)
    return share_of(2 * chip + core, part), share_of(2 * chip + 1 - core, part)


def expert_grad_kernel(split, buffer, active, grad_before, grad_expert, *rest):
    width = buffer.shape[1]
    scratch = rest[-1]
    for e in range(EXPERTS):
        slot = slice(e * CAP, (e + 1) * CAP)
        for which in range(2):
            if which == 0:
                product = dot_tn(buffer[slot, :], grad_before[slot, :])
            else:
                product = dot_tn(grad_expert[slot, :], active[slot, :])
            hidden_units = active.shape[1]
            first = (2 * e + which) * hidden_units
            if not split:
                rest[0][:, first : first + hidden_units] = product
                continue
            keep, send = rest[0], rest[1]
            part = keep.shape[1]
            scratch[...] = product
            for chip in range(keep.shape[0]):
                mine, other = split_rows(keep, send, chip, part)
                keep[chip, :, first : first + hidden_units] = scratch[mine, :].astype(BF16)
                send[chip, :, first : first + hidden_units] = scratch[other, :].astype(BF16)


def merge_kernel(kept, came, *outs):
    chips = kept.shape[0]
    chip = lax.div(lax.axis_index("dp"), 2)
    for k in range(chips):
        there = jnp.bitwise_xor(chip, k)
        total = kept[there].astype(F32) + came[there].astype(F32)
        outs[k][...] = total.astype(outs[k].dtype)


def expert_final_kernel(chips, *refs):
    up_o, down_o = refs[chips:]
    total = total_of(refs[:chips])
    for e in range(EXPERTS):
        width = up_o.shape[2]
        first = 2 * e * width
        up_o[e] = total[:, first : first + width]
        down_o[e] = total[:, first + width : first + 2 * width].T


def output_kernel(members, hidden, *rest):
    rest[-1][...] = (hidden[...] + total_of(rest[:members])).astype(BF16)


def gather_kernel(*refs):
    assemble(refs[-1], refs[:-1])


def hidden_back_kernel(members, hidden, cotangent, gain, *rest):
    parts = rest[:members]
    grad_o, low_o, gain_o = rest[members:]
    share = hidden.shape[0]
    h = hidden[...]
    dy = cotangent[share_of(lax.axis_index("tensor"), share), :].astype(F32)
    r = inverse_rms(h)
    grad_normed = total_of(parts)
    z = grad_normed * gain[...]
    gain_o[...] = jnp.sum(grad_normed * h * r, axis=0, keepdims=True)
    grad = dy + r * z - h * (r * r * r) * jnp.mean(z * h, axis=-1, keepdims=True)
    grad_o[...] = grad
    low_o[...] = grad.astype(BF16)


def attention_back_kernel(members, inputs, probs, q, k, v, wq, wk, wv, wo, *rest):
    pieces = rest[:members]
    rest = rest[members:]
    share_o = rest[:members]
    grads_o, attended_o, scores_o, gain_o = rest[members : members + 4]
    acc = rest[members + 4]
    assemble(attended_o, pieces)
    heads = wq.shape[1] // HEAD_DIM
    grad_mixed = dot_nt(attended_o[...], wo[...]).astype(BF16)
    qv, kv, vv = q[...], k[...], v[...]
    dq = jnp.zeros(qv.shape, F32)
    dk = jnp.zeros(qv.shape, F32)
    dv = jnp.zeros(qv.shape, F32)
    for h in range(heads):
        grad_mixed_h = masked(grad_mixed, h)
        p = probs[h]
        grad_probs = dot_nt(grad_mixed_h, vv)
        inner = jnp.sum(p * grad_probs, axis=-1, keepdims=True)
        grad_scores = (p * (grad_probs - inner)).astype(BF16)
        scores_o[h] = grad_scores
        dq = dq + dot(grad_scores, masked(kv, h))
        dk = dk + dot_tn(grad_scores, masked(qv, h))
        dv = dv + dot_tn(p.astype(BF16), grad_mixed_h)
    dq, dk, dv = dq.astype(BF16), dk.astype(BF16), dv.astype(BF16)
    grads_o[0] = dq
    grads_o[1] = dk
    grads_o[2] = dv
    total = dot_nt(dq, wq[...]) + dot_nt(dk, wk[...]) + dot_nt(dv, wv[...])
    acc[...] = total
    put_shares(acc, share_o)
    x = inputs[...].astype(F32)
    gain_o[...] = jnp.sum(total * x * inverse_rms(x), axis=0, keepdims=True)


def weight_grad_kernel(
    split, normed, grads, attended, mixed, scores, buckets, gain_one, gain_two, router, *rest
):
    bucket_count = 32
    small, scratch = rest[-2:]
    length = normed.shape[0]
    cols = grads.shape[2]
    normed_v = normed[...]
    for i in range(4):
        if i < 3:
            product = dot_tn(normed_v, grads[i])
        else:
            product = dot_tn(attended[...], mixed[...])
        scratch[:, i * cols : (i + 1) * cols] = product
    small[...] = jnp.zeros_like(small)
    width = gain_one.shape[1]
    small[0:1, 0:width] = gain_one[...]
    small[1:2, 0:width] = gain_two[...]
    small[2 : 2 + EXPERTS, 0:width] = router[...]
    flip = (
        lax.broadcasted_iota(jnp.int32, (length, length), 0)
        + lax.broadcasted_iota(jnp.int32, (length, length), 1)
        == length - 1
    ).astype(BF16)
    hot = (
        lax.broadcasted_iota(jnp.int32, (bucket_count, 2 * length), 0) == buckets[...]
    ).astype(F32)
    for h in range(scores.shape[0]):
        flipped = dot(flip, scores[h])
        wide = jnp.concatenate([flipped, jnp.zeros_like(flipped)], axis=1)
        sheared = pltpu.roll(wide, 0, 1, stride=1, stride_axis=0)
        offsets = jnp.sum(sheared, axis=0, keepdims=True)
        small[2 + EXPERTS + h : 3 + EXPERTS + h, 0:bucket_count] = dot_nt(
            jnp.broadcast_to(offsets, (8, 2 * length)), hot, HIGHEST
        )[0:1]
    if not split:
        rest[0][...] = scratch[...]
        rest[1][...] = small[...]
        return
    keep, send = rest[0], rest[1]
    chips, rows, _ = keep.shape
    part = rows - SMALL_ROWS
    for chip in range(chips):
        mine, other = split_rows(keep, send, chip, part)
        keep[chip, 0:part, :] = scratch[mine, :].astype(BF16)
        send[chip, 0:part, :] = scratch[other, :].astype(BF16)
        keep[chip, part:rows, :] = small[...].astype(BF16)
        send[chip, part:rows, :] = small[...].astype(BF16)


def weight_final_kernel(chips, *refs):
    wq_o, wk_o, wv_o, wo_o, table_o, small_o = refs[chips:]
    total = total_of(refs[:chips])
    part, cols = wq_o.shape
    wq_o[...] = total[0:part, 0:cols]
    wk_o[...] = total[0:part, cols : 2 * cols]
    wv_o[...] = total[0:part, 2 * cols : 3 * cols]
    wo_o[...] = total[0:part, 3 * cols : 4 * cols].T
    small = total[part:, :]
    small_o[...] = small
    bucket_count, heads = table_o.shape
    pick = (
        lax.broadcasted_iota(jnp.int32, (bucket_count, small.shape[1]), 0)
        == lax.broadcasted_iota(jnp.int32, (bucket_count, small.shape[1]), 1)
    ).astype(F32)
    table_o[...] = dot_nt(pick, small, HIGHEST)[:, 2 + EXPERTS : 2 + EXPERTS + heads]


def small_final_kernel(members, *refs):
    one_o, two_o, router_o = refs[members:]
    total = total_of(refs[:members])
    part = router_o.shape[0]
    first = (lax.axis_index("dp") * members + lax.axis_index("tensor")) * part
    shape = (part, total.shape[1])
    pick = (
        lax.broadcasted_iota(jnp.int32, shape, 0) + first
        == lax.broadcasted_iota(jnp.int32, shape, 1)
    ).astype(F32)
    rows = dot_nt(total, pick, HIGHEST)
    one_o[...] = rows[0:1]
    two_o[...] = rows[1:2]
    router_o[...] = dot_nt(pick, total, HIGHEST)[:, 2 : 2 + EXPERTS]


def input_back_kernel(members, inputs, gain, grad_hidden, *rest):
    out = rest[-1]
    share = out.shape[0]
    x = inputs[share_of(lax.axis_index("tensor"), share), :].astype(F32)
    r = inverse_rms(x)
    z = total_of(rest[:members]) * gain[...]
    out[...] = (
        grad_hidden[...] + r * z - x * (r * r * r) * jnp.mean(z * x, axis=-1, keepdims=True)
    ).astype(BF16)


def run(kernel, outs, args, scratch=(), flops=0, name=None):
    vmem = pl.BlockSpec(memory_space=pltpu.VMEM)
    size = sum(a.size * a.dtype.itemsize for a in args)
    size += sum(o.size * o.dtype.itemsize for o in outs)
    return pl.pallas_call(
        kernel,
        out_shape=outs,
        in_specs=[vmem] * len(args),
        out_specs=[vmem] * len(outs),
        scratch_shapes=list(scratch),
        compiler_params=pltpu.CompilerParams(vmem_limit_bytes=48 * 1024 * 1024),
        cost_estimate=pl.CostEstimate(flops=flops, bytes_accessed=size, transcendentals=0),
        name=name,
    )(*args)


def sds(shape, dtype):
    return jax.ShapeDtypeStruct(tuple(shape), dtype)


def swap(values, axis, k):
    size = lax.axis_size(axis)
    return lax.ppermute(values, axis, [(i, i ^ k) for i in range(size)])


def exchange(shares):
    return [shares[0]] + [swap(s, "tensor", k) for k, s in enumerate(shares) if k > 0]


def spread(share):
    members = lax.axis_size("tensor")
    return [share] + [swap(share, "tensor", k) for k in range(1, members)]


def shards(
    inputs,
    segments,
    buckets,
    routes,
    capacity_slots,
    gain_attn,
    bias_table,
    query_weight,
    key_weight,
    value_weight,
    out_weight,
    gain_expert,
    router_weight,
    expert_up,
    expert_down,
    cotangent,
):
    length, width = inputs.shape
    members = lax.axis_size("tensor")
    dp = lax.axis_size("dp")
    share = length // members
    cols = query_weight.shape[1]
    heads = cols // HEAD_DIM
    hidden_units = expert_up.shape[2]
    bucket_count = bias_table.shape[0]
    part = width // dp
    split = dp == 8 and part % 16 == 0
    chips = dp // 2
    bind = functools.partial

    def shares_sds(dtype, own=None):
        return [sds((share, width), own or dtype)] + [
            sds((share, width), dtype) for _ in range(members - 1)
        ]

    gain_row = gain_attn.reshape(1, width)
    gain_two_row = gain_expert.reshape(1, width)
    bucket_row = buckets.reshape(1, -1)
    bucket_wide = jnp.pad(bucket_row, ((0, 0), (0, 1)), constant_values=-1)
    where_to = (routes * CAP + capacity_slots).reshape(1, length)
    router_t = router_weight.T

    outs = run(
        bind(attention_kernel, members),
        shares_sds(BF16, F32)
        + [sds((length, width), BF16)]
        + [sds((length, cols), BF16)] * 3
        + [sds((heads, length, length), F32), sds((length, cols), BF16)],
        [
            inputs,
            segments,
            bucket_row,
            gain_row,
            bias_table,
            query_weight,
            key_weight,
            value_weight,
            out_weight,
        ],
        [pltpu.VMEM((length, width), F32), pltpu.VMEM((8, 2 * length), F32)],
        name="attention",
    )
    attended = exchange(outs[:members])
    normed, q, k, v, probs, mixed = outs[members:]

    hidden, normed_two = run(
        bind(hidden_kernel, members),
        [sds((share, width), F32), sds((share, width), BF16)],
        [inputs, gain_two_row] + attended,
        name="hidden",
    )
    normed_two = spread(normed_two)

    slots = EXPERTS * CAP
    outs = run(
        bind(expert_kernel, members),
        shares_sds(BF16)
        + shares_sds(BF16)
        + [sds((slots, width), BF16)]
        + [sds((slots, hidden_units), BF16)] * 2
        + [sds((slots, width), BF16), sds((EXPERTS, width), F32)],
        [where_to, cotangent, router_t, expert_up, expert_down] + normed_two,
        [
            pltpu.VMEM((length, width), BF16),
            pltpu.VMEM((slots, width), BF16),
            pltpu.VMEM((slots, width), BF16),
            pltpu.VMEM((length, width), F32),
        ],
        name="expert",
    )
    back_rows = exchange(outs[:members])
    out_rows = outs[members : 2 * members]
    buffer, active, grad_before, grad_expert, grad_router = outs[2 * members :]

    def split_sds(rows, columns):
        return [sds((chips, rows, columns), BF16)] * 2

    expert_grads = run(
        bind(expert_grad_kernel, split),
        split_sds(part, 4 * hidden_units) if split else [sds((width, 4 * hidden_units), F32)],
        [buffer, active, grad_before, grad_expert],
        [pltpu.VMEM((width, hidden_units), F32)],
        flops=8 * CAP * width * hidden_units,
        name="expert_grads",
    )

    grad_hidden, grad_attended, grad_gain_expert = run(
        bind(hidden_back_kernel, members),
        [sds((share, width), F32), sds((share, width), BF16), sds((1, width), F32)],
        [hidden, cotangent, gain_two_row] + back_rows,
        name="hidden_back",
    )
    grad_attended = spread(grad_attended)
    out_rows = exchange(out_rows)
    (output,) = run(
        bind(output_kernel, members),
        [sds((share, width), BF16)],
        [hidden] + out_rows,
        name="output_share",
    )
    output = spread(output)
    (output,) = run(gather_kernel, [sds((length, width), BF16)], output, name="output_rows")

    outs = run(
        bind(attention_back_kernel, members),
        shares_sds(BF16, F32)
        + [
            sds((3, length, cols), BF16),
            sds((length, width), BF16),
            sds((heads, length, length), BF16),
            sds((1, width), F32),
        ],
        [inputs, probs, q, k, v, query_weight, key_weight, value_weight, out_weight]
        + grad_attended,
        [pltpu.VMEM((length, width), F32)],
        name="attention_back",
    )
    grad_normed = exchange(outs[:members])
    projections, attended_low, grad_scores, grad_gain_attn = outs[members:]

    weight_cols = 4 * cols
    weight_grads = run(
        bind(weight_grad_kernel, split),
        split_sds(part + SMALL_ROWS, weight_cols)
        if split
        else [sds((width, weight_cols), F32), sds((SMALL_ROWS, weight_cols), F32)],
        [
            normed,
            projections,
            attended_low,
            mixed,
            grad_scores,
            bucket_wide,
            grad_gain_attn,
            grad_gain_expert,
            grad_router,
        ],
        [pltpu.VMEM((SMALL_ROWS, weight_cols), F32), pltpu.VMEM((width, weight_cols), F32)],
        name="weight_grads",
    )

    (grad_inputs,) = run(
        bind(input_back_kernel, members),
        [sds((share, width), BF16)],
        [inputs, gain_row, grad_hidden] + grad_normed,
        name="input_back",
    )
    grad_inputs = spread(grad_inputs)
    (grad_inputs,) = run(
        gather_kernel, [sds((length, width), BF16)], grad_inputs, name="grad_rows"
    )

    if split:

        def over_chips(kept, sent):
            rows, columns = kept.shape[1:]
            came = swap(sent, "dp", 1)
            merged = run(
                merge_kernel,
                [sds((rows, columns), F32)] + [sds((rows, columns), BF16)] * (chips - 1),
                [kept, came],
                name="merge",
            )
            return [merged[0]] + [swap(merged[i], "dp", 2 * i) for i in range(1, chips)]

        parts = over_chips(*expert_grads)
        grad_expert_up, grad_expert_down = run(
            bind(expert_final_kernel, chips),
            [sds((EXPERTS, part, hidden_units), F32), sds((EXPERTS, hidden_units, part), F32)],
            parts,
            name="expert_final",
        )
        parts = over_chips(*weight_grads)
        (
            grad_query_weight,
            grad_key_weight,
            grad_value_weight,
            grad_out_weight,
            grad_table,
            small,
        ) = run(
            bind(weight_final_kernel, chips),
            [sds((part, cols), F32)] * 3
            + [sds((cols, part), F32), sds((bucket_count, heads), F32)]
            + [sds((SMALL_ROWS, weight_cols), F32)],
            parts,
            name="weight_final",
        )
        small = [small] + [swap(small, "tensor", i) for i in range(1, members)]
        per = part // members
        grad_gain_attn, grad_gain_expert, grad_router = run(
            bind(small_final_kernel, members),
            [sds((1, per), F32), sds((1, per), F32), sds((per, EXPERTS), F32)],
            small,
            name="small_final",
        )
        grad_gain_attn = grad_gain_attn.reshape(per)
        grad_gain_expert = grad_gain_expert.reshape(per)
    else:

        def scatter(values, axes, dimension):
            return lax.psum_scatter(values, axes, scatter_dimension=dimension, tiled=True)

        grads = expert_grads[0].reshape(width, EXPERTS, 2, hidden_units)
        grad_expert_up = scatter(grads[:, :, 0].transpose(1, 0, 2), "dp", 1)
        grad_expert_down = scatter(grads[:, :, 1].transpose(1, 2, 0), "dp", 2)
        grads, small = weight_grads
        grad_query_weight = scatter(grads[:, 0:cols], "dp", 0)
        grad_key_weight = scatter(grads[:, cols : 2 * cols], "dp", 0)
        grad_value_weight = scatter(grads[:, 2 * cols : 3 * cols], "dp", 0)
        grad_out_weight = scatter(grads[:, 3 * cols :].T, "dp", 1)
        first = 2 + EXPERTS
        grad_table = lax.psum(small[first : first + heads, :bucket_count].T, "dp")
        both = ("dp", "tensor")
        grad_gain_attn = scatter(small[0, :width], both, 0)
        grad_gain_expert = scatter(small[1, :width], both, 0)
        grad_router = scatter(small[2:first, :width].T, both, 0)
    return (
        output,
        grad_inputs,
        grad_gain_attn,
        grad_table,
        grad_query_weight,
        grad_key_weight,
        grad_value_weight,
        grad_out_weight,
        grad_gain_expert,
        grad_router,
        grad_expert_up,
        grad_expert_down,
    )


def solution(mesh):
    return jax.shard_map(
        shards,
        mesh=mesh,
        in_specs=(
            P("dp", None),
            P("dp", None),
            P(),
            P("dp"),
            P("dp"),
            P(),
            P(None, "tensor"),
            P(None, "tensor"),
            P(None, "tensor"),
            P(None, "tensor"),
            P("tensor", None),
            P(),
            P(),
            P(None, None, "tensor"),
            P(None, "tensor", None),
            P("dp", None),
        ),
        out_specs=(
            P("dp", None),
            P("dp", None),
            P(("dp", "tensor")),
            P(None, "tensor"),
            P("dp", "tensor"),
            P("dp", "tensor"),
            P("dp", "tensor"),
            P("tensor", "dp"),
            P(("dp", "tensor")),
            P(("dp", "tensor"), None),
            P(None, "dp", "tensor"),
            P(None, "tensor", "dp"),
        ),
        check_vma=False,
    )
```

```python
import functools

import jax
import jax.numpy as jnp
from jax import lax
from jax.experimental import pallas as pl
from jax.experimental.pallas import tpu as pltpu
from jax.sharding import PartitionSpec as P

HEAD_DIM = 64
EXPERTS = 2
CAP = 144
EPS = 1e-06
SMALL_ROWS = 16
TABLE_ROW = 2 + EXPERTS
WEIGHTS = {
    "expert": 5,
    "expert_grads": 400,
    "hidden_back": 1000,
    "expert_merge": 400,
    "attention_back": 1000,
    "weight_grads": 12,
    "input_back": 1000,
    "expert_final": 1,
    "weight_final": 1,
}
BF16 = jnp.bfloat16
F32 = jnp.float32
HIGHEST = lax.Precision.HIGHEST
NT = (((1,), (1,)), ((), ()))
TN = (((0,), (0,)), ((), ()))
GELU_C = 0.7978845608028654
GELU_A = 0.044715


def dot(a, b):
    return jnp.dot(a, b, preferred_element_type=F32)


def dot_nt(a, b, precision=None):
    return lax.dot_general(a, b, NT, preferred_element_type=F32, precision=precision)


def dot_tn(a, b):
    return lax.dot_general(a, b, TN, preferred_element_type=F32)


def inverse_rms(values):
    return lax.rsqrt(jnp.mean(values * values, axis=-1, keepdims=True) + EPS)


def share_of(index, rows):
    return pl.ds(pl.multiple_of(index * rows, rows), rows)


def put_shares(acc_ref, share_refs):
    me = lax.axis_index("tensor")
    for k, ref in enumerate(share_refs):
        rows = ref.shape[0]
        ref[...] = acc_ref[share_of(jnp.bitwise_xor(me, k), rows), :].astype(ref.dtype)


def assemble(full_ref, share_refs):
    me = lax.axis_index("tensor")
    for k, ref in enumerate(share_refs):
        rows = ref.shape[0]
        full_ref[share_of(jnp.bitwise_xor(me, k), rows), :] = ref[...]


def total_of(refs):
    total = refs[0][...].astype(F32)
    for ref in refs[1:]:
        total = total + ref[...].astype(F32)
    return total


def column_of(row, length):
    eye = lax.broadcasted_iota(jnp.int32, (length, length), 0) == lax.broadcasted_iota(
        jnp.int32, (length, length), 1
    )
    return jnp.sum(jnp.where(eye, row, jnp.zeros_like(row)), axis=1, keepdims=True)


def head_mask(head, width):
    lane = lax.broadcasted_iota(jnp.int32, (1, width), 1)
    return (lane >= head * HEAD_DIM) & (lane < (head + 1) * HEAD_DIM)


def masked(values, head):
    return jnp.where(head_mask(head, values.shape[1]), values, jnp.zeros_like(values))


def bucket_hot_of(buckets_ref, bucket_count):
    offsets = buckets_ref.shape[1]
    return (
        lax.broadcasted_iota(jnp.int32, (bucket_count, offsets), 0) == buckets_ref[...]
    ).astype(F32)


def attention_kernel(members, *refs):
    sources, outs = refs[:9], refs[9 : members + 15]
    normed_o, q_o, k_o, v_o, probs_o, mixed_o = outs[members:]
    acc, offset_rows = refs[members + 15 : members + 17]
    local, sems = refs[members + 17 : members + 26], refs[members + 26]
    copies = [
        pltpu.make_async_copy(source, held, sems.at[i])
        for i, (source, held) in enumerate(zip(sources, local))
    ]
    for copy in copies:
        copy.start()
    inputs, gain, wq, wk, wv, buckets, table, segment, wo = local
    length = inputs.shape[0]
    heads = wq.shape[0] // HEAD_DIM
    copies[0].wait()
    x = inputs[...].astype(F32)
    scaled = x * inverse_rms(x)
    for copy in copies[1:8]:
        copy.wait()
    normed = (scaled * gain[...].reshape(1, -1)).astype(BF16)
    normed_o[...] = normed
    q = dot_nt(normed, wq[...]).astype(BF16)
    k = dot_nt(normed, wk[...]).astype(BF16)
    v = dot_nt(normed, wv[...]).astype(BF16)
    q_o[...] = q
    k_o[...] = k
    v_o[...] = v
    hot = bucket_hot_of(buckets, table.shape[1])
    seg_row = segment[...].astype(F32)
    same = column_of(seg_row, length) == seg_row
    mixed = jnp.zeros((length, wq.shape[0]), F32)
    offset_rows[...] = jnp.zeros_like(offset_rows)
    offset_rows[0:heads, 0 : hot.shape[1]] = jnp.dot(
        table[...], hot, preferred_element_type=F32, precision=HIGHEST
    )
    for h in range(heads):
        spread = jnp.broadcast_to(offset_rows[h : h + 1, :], (length, 2 * length))
        bias = pltpu.roll(spread, length + 1, 1, stride=1, stride_axis=0)[:, :length]
        scores = dot_nt(masked(q, h), k) + bias
        scores = jnp.where(same, scores, -1e30)
        shifted = jnp.exp(scores - jnp.max(scores, axis=-1, keepdims=True))
        probs = shifted / jnp.sum(shifted, axis=-1, keepdims=True)
        probs_o[h] = probs
        mixed = mixed + dot(probs.astype(BF16), masked(v, h))
    mixed = mixed.astype(BF16)
    mixed_o[...] = mixed
    copies[8].wait()
    acc[...] = dot(mixed, wo[...])
    put_shares(acc, outs[:members])


def hidden_kernel(members, inputs, gain, *rest):
    parts = rest[:members]
    hidden_o, normed_o = rest[members:]
    share = hidden_o.shape[0]
    x = inputs[share_of(lax.axis_index("tensor"), share), :].astype(F32)
    hidden = x + total_of(parts)
    hidden_o[...] = hidden
    normed_o[...] = (hidden * inverse_rms(hidden) * gain[...]).astype(BF16)


def expert_kernel(members, where_to, cotangent, router_t, up, down, *rest):
    pieces = rest[:members]
    rest = rest[members:]
    back_o, row_o = rest[:members], rest[members : members + 2]
    buffer_o, active_o, grad_before_o, grad_expert_o, router_o = rest[members + 2 : members + 7]
    normed, backs, rows, acc = rest[members + 7 :]
    length = cotangent.shape[0]
    assemble(normed, pieces)
    place = (
        lax.broadcasted_iota(jnp.int32, (EXPERTS * CAP, length), 0) == where_to[...]
    ).astype(BF16)
    buffer = dot(place, normed[...]).astype(BF16)
    buffer_o[...] = buffer
    dy_buffer = dot(place, cotangent[...])
    router_rows = router_t[...].astype(F32)
    router_grad = [jnp.zeros((1, buffer.shape[1]), F32) for _ in range(EXPERTS)]
    for e in range(EXPERTS):
        slot = slice(e * CAP, (e + 1) * CAP)
        rows_in = buffer[slot]
        logits = dot_nt(rows_in, router_t[...])
        shifted = jnp.exp(logits - jnp.max(logits, axis=-1, keepdims=True))
        router_probs = shifted / jnp.sum(shifted, axis=-1, keepdims=True)
        gate = router_probs[:, e : e + 1]
        dy = dy_buffer[slot]
        grad_expert = (dy * gate).astype(BF16)
        grad_expert_o[slot, :] = grad_expert
        before = dot(rows_in, up[e])
        inner = jnp.tanh(GELU_C * (before + GELU_A * before * before * before))
        active = (0.5 * before * (1.0 + inner)).astype(BF16)
        active_o[slot, :] = active
        slope = 0.5 * (1.0 + inner) + 0.5 * before * (1.0 - inner * inner) * GELU_C * (
            1.0 + 3.0 * GELU_A * before * before
        )
        result = dot(active, down[e])
        grad_before = (dot_nt(grad_expert, down[e]) * slope).astype(BF16)
        grad_before_o[slot, :] = grad_before
        rows[slot, :] = (result * gate).astype(BF16)
        scaled = jnp.sum(dy * result, axis=-1, keepdims=True) * gate
        back = dot_nt(grad_before, up[e])
        for other in range(EXPERTS):
            own = 1.0 if other == e else 0.0
            grad_logit = scaled * (own - router_probs[:, other : other + 1])
            router_grad[other] = router_grad[other] + jnp.sum(
                grad_logit * rows_in.astype(F32), axis=0, keepdims=True
            )
            back = back + grad_logit * router_rows[other : other + 1, :]
        backs[slot, :] = back.astype(BF16)
    for other in range(EXPERTS):
        router_o[other : other + 1, :] = router_grad[other]
    acc[...] = dot_tn(place, backs[...])
    put_shares(acc, back_o)
    acc[...] = dot_tn(place, rows[...])
    me = lax.axis_index("tensor")
    share = back_o[0].shape[0]
    for first, ref in enumerate(row_o):
        for k in range(2):
            index = jnp.bitwise_xor(me, first + 2 * k)
            ref[k * share : (k + 1) * share, :] = acc[share_of(index, share), :].astype(BF16)


def split_rows(keep, send, chip, part):
    core = lax.rem(lax.axis_index("dp"), 2)
    return share_of(2 * chip + core, part), share_of(2 * chip + 1 - core, part)


def expert_grad_kernel(split, buffer, active, grad_before, grad_expert, *rest):
    width = buffer.shape[1]
    scratch = rest[-1]
    for e in range(EXPERTS):
        slot = slice(e * CAP, (e + 1) * CAP)
        for which in range(2):
            if which == 0:
                product = dot_tn(buffer[slot, :], grad_before[slot, :])
            else:
                product = dot_tn(grad_expert[slot, :], active[slot, :])
            hidden_units = active.shape[1]
            first = (2 * e + which) * hidden_units
            if not split:
                rest[0][:, first : first + hidden_units] = product
                continue
            keep, send = rest[0], rest[1]
            part = keep.shape[1]
            scratch[...] = product
            for chip in range(keep.shape[0]):
                mine, other = split_rows(keep, send, chip, part)
                keep[chip, :, first : first + hidden_units] = scratch[mine, :].astype(BF16)
                send[chip, :, first : first + hidden_units] = scratch[other, :].astype(BF16)


def chip_bits():
    core = lax.rem(lax.axis_index("dp"), 2)
    return 1 + core, 2 - core


def merge_kernel(kept, came, keep, send):
    chip = lax.div(lax.axis_index("dp"), 2)
    first, second = chip_bits()
    for ref, start in ((keep, chip), (send, jnp.bitwise_xor(chip, first))):
        for k, there in enumerate((start, jnp.bitwise_xor(start, second))):
            total = kept[there].astype(F32) + came[there].astype(F32)
            ref[k] = total.astype(ref.dtype)


def merge_small_kernel(kept, came, small, small_came, keep, send):
    merge_kernel(kept, came, keep, send)
    total = small[...] + small_came[...]
    first = kept.shape[1] - SMALL_ROWS
    rows = slice(first, first + TABLE_ROW)
    for ref in (keep, send):
        for k in range(2):
            ref[k, rows, 0 : total.shape[1]] = total[0:TABLE_ROW].astype(ref.dtype)


def merge_two_kernel(kept, came, keep, send):
    keep[...] = kept[0] + came[0].astype(F32)
    send[...] = (kept[1] + came[1].astype(F32)).astype(BF16)


def expert_final_kernel(*refs):
    up_o, down_o = refs[2:]
    total = total_of(refs[:2])
    for e in range(EXPERTS):
        width = up_o.shape[2]
        first = 2 * e * width
        up_o[e] = total[:, first : first + width]
        down_o[e] = total[:, first + width : first + 2 * width]


def pair_sum_kernel(kept, came, own, other):
    share = own.shape[0]
    own[...] = kept[0:share, :].astype(F32) + came[0:share, :].astype(F32)
    other[...] = (kept[share:, :].astype(F32) + came[share:, :].astype(F32)).astype(BF16)


def output_kernel(hidden, own, came, out):
    out[...] = (hidden[...] + own[...] + came[...].astype(F32)).astype(BF16)


def pair_kernel(own, came, out):
    share = own.shape[0]
    out[0:share, :] = own[...]
    out[share:, :] = came[...]


def pair_rows_kernel(own, came, out):
    me = lax.axis_index("tensor")
    share = own.shape[0] // 2
    for first, ref in enumerate((own, came)):
        for k in range(2):
            index = jnp.bitwise_xor(me, first + 2 * k)
            out[share_of(index, share), :] = ref[k * share : (k + 1) * share, :]


def gather_kernel(*refs):
    assemble(refs[-1], refs[:-1])


def hidden_back_kernel(members, hidden, cotangent, gain, *rest):
    parts = rest[:members]
    grad_o, low_o, gain_o = rest[members:]
    share = hidden.shape[0]
    h = hidden[...]
    dy = cotangent[share_of(lax.axis_index("tensor"), share), :].astype(F32)
    r = inverse_rms(h)
    grad_normed = total_of(parts)
    z = grad_normed * gain[...]
    gain_o[...] = jnp.sum(grad_normed * h * r, axis=0, keepdims=True)
    grad = dy + r * z - h * (r * r * r) * jnp.mean(z * h, axis=-1, keepdims=True)
    grad_o[...] = grad
    low_o[...] = grad.astype(BF16)


def attention_back_kernel(
    members, inputs, probs, q, k, v, wq, wk, wv, wo, gain_two, router, *rest
):
    pieces = rest[:members]
    rest = rest[members:]
    share_o = rest[:members]
    grads_o, attended_o, scores_o = rest[members : members + 3]
    acc = rest[members + 3]
    assemble(attended_o, pieces)
    heads = wq.shape[0] // HEAD_DIM
    grad_mixed = dot_nt(attended_o[...], wo[...]).astype(BF16)
    qv, kv, vv = q[...], k[...], v[...]
    dq = jnp.zeros(qv.shape, F32)
    dk = jnp.zeros(qv.shape, F32)
    dv = jnp.zeros(qv.shape, F32)
    for h in range(heads):
        grad_mixed_h = masked(grad_mixed, h)
        p = probs[h]
        grad_probs = dot_nt(grad_mixed_h, vv)
        inner = jnp.sum(p * grad_probs, axis=-1, keepdims=True)
        grad_scores = (p * (grad_probs - inner)).astype(BF16)
        scores_o[h] = grad_scores
        dq = dq + dot(grad_scores, masked(kv, h))
        dk = dk + dot_tn(grad_scores, masked(qv, h))
        dv = dv + dot_tn(p.astype(BF16), grad_mixed_h)
    dq, dk, dv = dq.astype(BF16), dk.astype(BF16), dv.astype(BF16)
    grads_o[0] = dq
    grads_o[1] = dk
    grads_o[2] = dv
    total = dot(dq, wq[...]) + dot(dk, wk[...]) + dot(dv, wv[...])
    acc[...] = total
    x = inputs[...].astype(F32)
    gain_one = jnp.sum(total * x * inverse_rms(x), axis=0, keepdims=True)
    small = jnp.concatenate(
        [
            gain_one,
            gain_two[...],
            router[...],
            jnp.zeros((SMALL_ROWS - 2 - EXPERTS, gain_one.shape[1]), F32),
        ],
        axis=0,
    )
    me = lax.axis_index("tensor")
    for k, ref in enumerate(share_o):
        share = ref.shape[0] - SMALL_ROWS
        ref[0:share, :] = acc[share_of(jnp.bitwise_xor(me, k), share), :].astype(ref.dtype)
        ref[share:, :] = small.astype(ref.dtype)


def weight_grad_kernel(
    split, normed, grads, attended, mixed, scores, buckets, *rest
):
    bucket_count = 32
    small, scratch = rest[-2:]
    length = normed.shape[0]
    cols = grads.shape[2]
    normed_v = normed[...]
    for i in range(4):
        if i < 3:
            product = dot_tn(normed_v, grads[i])
        else:
            product = dot_tn(attended[...], mixed[...])
        scratch[:, i * cols : (i + 1) * cols] = product
    small[...] = jnp.zeros_like(small)
    flip = (
        lax.broadcasted_iota(jnp.int32, (length, length), 0)
        + lax.broadcasted_iota(jnp.int32, (length, length), 1)
        == length - 1
    ).astype(BF16)
    hot = (
        lax.broadcasted_iota(jnp.int32, (bucket_count, 2 * length), 0) == buckets[...]
    ).astype(F32)
    for h in range(scores.shape[0]):
        flipped = dot(flip, scores[h])
        wide = jnp.concatenate([flipped, jnp.zeros_like(flipped)], axis=1)
        sheared = pltpu.roll(wide, 0, 1, stride=1, stride_axis=0)
        offsets = jnp.sum(sheared, axis=0, keepdims=True)
        small[TABLE_ROW + h : TABLE_ROW + h + 1, 0:bucket_count] = dot_nt(
            jnp.broadcast_to(offsets, (8, 2 * length)), hot, HIGHEST
        )[0:1]
    if not split:
        rest[0][...] = scratch[...]
        rest[1][...] = small[...]
        return
    keep, send = rest[0], rest[1]
    chips, rows, _ = keep.shape
    part = rows - SMALL_ROWS
    for chip in range(chips):
        mine, other = split_rows(keep, send, chip, part)
        keep[chip, 0:part, :] = scratch[mine, :].astype(BF16)
        send[chip, 0:part, :] = scratch[other, :].astype(BF16)
        keep[chip, part:rows, :] = small[...].astype(BF16)
        send[chip, part:rows, :] = small[...].astype(BF16)


def weight_final_kernel(members, *refs):
    wq_o, wk_o, wv_o, wo_o, table_o, one_o, two_o, router_o = refs[2:]
    total = total_of(refs[:2])
    part, cols = wq_o.shape
    wq_o[...] = total[0:part, 0:cols]
    wk_o[...] = total[0:part, cols : 2 * cols]
    wv_o[...] = total[0:part, 2 * cols : 3 * cols]
    wo_o[...] = total[0:part, 3 * cols : 4 * cols].T
    small = total[part:, :]
    heads, bucket_count = table_o.shape
    table_o[...] = small[TABLE_ROW : TABLE_ROW + heads, 0:bucket_count]
    per = one_o.shape[1]
    first = (lax.axis_index("dp") * members + lax.axis_index("tensor")) * per
    shape = (per, small.shape[1])
    pick = (
        lax.broadcasted_iota(jnp.int32, shape, 0) + first
        == lax.broadcasted_iota(jnp.int32, shape, 1)
    ).astype(F32)
    rows = dot_nt(small, pick, HIGHEST)
    one_o[...] = rows[0:1]
    two_o[...] = rows[1:2]
    router_o[...] = rows[2:TABLE_ROW]


def input_back_kernel(members, inputs, gain, grad_hidden, *rest):
    out, small_o = rest[members:]
    share = out.shape[0]
    x = inputs[share_of(lax.axis_index("tensor"), share), :].astype(F32)
    r = inverse_rms(x)
    total = total_of(rest[:members])
    small_o[...] = total[share:]
    z = total[0:share] * gain[...]
    out[...] = (
        grad_hidden[...] + r * z - x * (r * r * r) * jnp.mean(z * x, axis=-1, keepdims=True)
    ).astype(BF16)


def run(kernel, outs, args, scratch=(), name=None, after=(), space=pltpu.VMEM):
    vmem = pl.BlockSpec(memory_space=pltpu.VMEM)
    anywhere = pl.BlockSpec(memory_space=pl.ANY)
    count, extra = len(args), len(after)

    def body(*refs):
        kernel(*refs[:count], *refs[count + extra :])

    return pl.pallas_call(
        body,
        out_shape=outs,
        in_specs=[pl.BlockSpec(memory_space=space)] * count + [anywhere] * extra,
        out_specs=[vmem] * len(outs),
        scratch_shapes=list(scratch),
        compiler_params=pltpu.CompilerParams(vmem_limit_bytes=48 * 1024 * 1024),
        cost_estimate=pl.CostEstimate(
            flops=int(WEIGHTS.get(name, 0.2) * 1e9), bytes_accessed=0, transcendentals=0
        ),
        name=name,
    )(*args, *after)


def sds(shape, dtype):
    return jax.ShapeDtypeStruct(tuple(shape), dtype)


def swap(values, axis, k):
    size = lax.axis_size(axis)
    return lax.ppermute(values, axis, [(i, i ^ k) for i in range(size)])


def swap_chips(values, even, odd):
    size = lax.axis_size("dp")
    pairs = [(i, i ^ (odd if i % 2 else even)) for i in range(size)]
    return lax.ppermute(values, "dp", pairs)


def exchange(shares):
    return [shares[0]] + [swap(s, "tensor", k) for k, s in enumerate(shares) if k > 0]


def spread(share):
    members = lax.axis_size("tensor")
    return [share] + [swap(share, "tensor", k) for k in range(1, members)]


def shards(
    inputs,
    segments,
    buckets,
    routes,
    capacity_slots,
    gain_attn,
    bias_table,
    query_weight,
    key_weight,
    value_weight,
    out_weight,
    gain_expert,
    router_weight,
    expert_up,
    expert_down,
    cotangent,
):
    length, width = inputs.shape
    members = lax.axis_size("tensor")
    dp = lax.axis_size("dp")
    share = length // members
    cols = query_weight.shape[1]
    heads = cols // HEAD_DIM
    hidden_units = expert_up.shape[2]
    bucket_count = bias_table.shape[0]
    part = width // dp
    split = dp == 8 and part % 16 == 0
    chips = dp // 2
    bind = functools.partial

    def shares_sds(dtype, own=None):
        return [sds((share, width), own or dtype)] + [
            sds((share, width), dtype) for _ in range(members - 1)
        ]

    gain_row = gain_attn.reshape(1, width)
    gain_two_row = gain_expert.reshape(1, width)
    bucket_row = buckets.reshape(1, -1)
    bucket_wide = jnp.pad(bucket_row, ((0, 0), (0, 1)), constant_values=-1)
    where_to = (routes * CAP + capacity_slots).reshape(1, length)
    router_t = router_weight.T
    query_t, key_t, value_t = query_weight.T, key_weight.T, value_weight.T

    attention_args = [
        inputs,
        gain_attn,
        query_t,
        key_t,
        value_t,
        bucket_row,
        bias_table.T,
        segments,
        out_weight,
    ]
    attention_args = [pltpu.with_memory_space_constraint(a, pltpu.HBM) for a in attention_args]
    outs = run(
        bind(attention_kernel, members),
        shares_sds(BF16, F32)
        + [sds((length, width), BF16)]
        + [sds((length, cols), BF16)] * 3
        + [sds((heads, length, length), F32), sds((length, cols), BF16)],
        attention_args,
        [pltpu.VMEM((length, width), F32), pltpu.VMEM((8, 2 * length), F32)]
        + [pltpu.VMEM(a.shape, a.dtype) for a in attention_args]
        + [pltpu.SemaphoreType.DMA((len(attention_args),))],
        name="attention",
        space=pltpu.HBM,
    )
    attended = exchange(outs[:members])
    normed, q, k, v, probs, mixed = outs[members:]

    hidden, normed_two = run(
        bind(hidden_kernel, members),
        [sds((share, width), F32), sds((share, width), BF16)],
        [inputs, gain_two_row] + attended,
        name="hidden",
    )
    normed_two = spread(normed_two)

    slots = EXPERTS * CAP
    outs = run(
        bind(expert_kernel, members),
        shares_sds(BF16)
        + [sds((2 * share, width), BF16)] * 2
        + [sds((slots, width), BF16)]
        + [sds((slots, hidden_units), BF16)] * 2
        + [sds((slots, width), BF16), sds((EXPERTS, width), F32)],
        [where_to, cotangent, router_t, expert_up, expert_down] + normed_two,
        [
            pltpu.VMEM((length, width), BF16),
            pltpu.VMEM((slots, width), BF16),
            pltpu.VMEM((slots, width), BF16),
            pltpu.VMEM((length, width), F32),
        ],
        name="expert",
    )
    back_rows = exchange(outs[:members])
    rows_kept, rows_sent = outs[members : members + 2]
    buffer, active, grad_before, grad_expert, grad_router = outs[members + 2 :]

    def split_sds(rows, columns):
        return [sds((chips, rows, columns), BF16)] * 2

    def merge_sds(rows, columns):
        return [sds((2, rows, columns), F32), sds((2, rows, columns), BF16)]

    def merge_two(merged, name, after=()):
        rows, columns = merged[0].shape[1:]
        return run(
            merge_two_kernel,
            [sds((rows, columns), F32), sds((rows, columns), BF16)],
            [merged[0], swap_chips(merged[1], 2, 4)],
            name=name,
            after=after,
        )

    expert_grads = run(
        bind(expert_grad_kernel, split),
        split_sds(part, 4 * hidden_units) if split else [sds((width, 4 * hidden_units), F32)],
        [buffer, active, grad_before, grad_expert],
        [pltpu.VMEM((width, hidden_units), F32)],
        name="expert_grads",
    )

    own_rows, other_rows = run(
        pair_sum_kernel,
        [sds((share, width), F32), sds((share, width), BF16)],
        [rows_kept, swap(rows_sent, "tensor", 1)],
        name="pair_sum",
    )
    grad_hidden, grad_attended, grad_gain_expert = run(
        bind(hidden_back_kernel, members),
        [sds((share, width), F32), sds((share, width), BF16), sds((1, width), F32)],
        [hidden, cotangent, gain_two_row] + back_rows,
        name="hidden_back",
        after=[own_rows, *expert_grads[-1:]],
    )
    grad_attended = spread(grad_attended)

    (output_share,) = run(
        output_kernel,
        [sds((share, width), BF16)],
        [hidden, own_rows, swap(other_rows, "tensor", 2)],
        name="output_share",
    )
    expert_merged = []
    if split:
        expert_merged = run(
            merge_kernel,
            merge_sds(part, 4 * hidden_units),
            [expert_grads[0], swap(expert_grads[1], "dp", 1)],
            name="expert_merge",
        )
    expert_halves = []

    def tall_sds(dtype):
        return sds((share + SMALL_ROWS, width), dtype)

    outs = run(
        bind(attention_back_kernel, members),
        [tall_sds(F32)]
        + [tall_sds(BF16)] * (members - 1)
        + [
            sds((3, length, cols), BF16),
            sds((length, width), BF16),
            sds((heads, length, length), BF16),
        ],
        [inputs, probs, q, k, v, query_t, key_t, value_t, out_weight]
        + [grad_gain_expert, grad_router]
        + grad_attended,
        [pltpu.VMEM((length, width), F32)],
        name="attention_back",
        after=expert_merged[:1],
    )
    grad_normed = exchange(outs[:members])
    projections, attended_low, grad_scores = outs[members:]

    weight_cols = 4 * cols
    weight_grads = run(
        bind(weight_grad_kernel, split),
        split_sds(part + SMALL_ROWS, weight_cols)
        if split
        else [sds((width, weight_cols), F32), sds((SMALL_ROWS, weight_cols), F32)],
        [normed, projections, attended_low, mixed, grad_scores, bucket_wide],
        [pltpu.VMEM((SMALL_ROWS, weight_cols), F32), pltpu.VMEM((width, weight_cols), F32)],
        name="weight_grads",
    )

    if split:
        expert_halves = merge_two(expert_merged, "expert_merge_two")
    grad_inputs, small = run(
        bind(input_back_kernel, members),
        [sds((share, width), BF16), sds((SMALL_ROWS, width), F32)],
        [inputs, gain_row, grad_hidden] + grad_normed,
        name="input_back",
        after=[output_share, *weight_grads[-1:], *expert_halves[:1]],
    )
    (output_pair,) = run(
        pair_kernel,
        [sds((2 * share, width), BF16)],
        [output_share, swap(output_share, "tensor", 2)],
        name="output_pair",
    )
    (output,) = run(
        pair_rows_kernel,
        [sds((length, width), BF16)],
        [output_pair, swap(output_pair, "tensor", 1)],
        name="output_rows",
    )


    input_parts = spread(grad_inputs)
    (grad_inputs,) = run(
        gather_kernel, [sds((length, width), BF16)], input_parts, name="grad_rows"
    )

    if split:
        grad_expert_up, grad_expert_down = run(
            expert_final_kernel,
            [sds((EXPERTS, part, hidden_units), F32), sds((EXPERTS, part, hidden_units), F32)],
            [expert_halves[0], swap_chips(expert_halves[1], 4, 2)],
            name="expert_final",
        )
        grad_expert_down = grad_expert_down.transpose(0, 2, 1)
        merged = run(
            merge_small_kernel,
            merge_sds(part + SMALL_ROWS, weight_cols),
            [
                weight_grads[0],
                swap(weight_grads[1], "dp", 1),
                small,
                swap(small, "dp", 1),
            ],
            name="weight_merge",
            after=[output_pair, input_parts[1]],
        )
        merged = merge_two(merged, "weight_merge_two", after=input_parts[2:])
        per = part // members
        (
            grad_query_weight,
            grad_key_weight,
            grad_value_weight,
            grad_out_weight,
            grad_table,
            grad_gain_attn,
            grad_gain_expert,
            grad_router,
        ) = run(
            bind(weight_final_kernel, members),
            [sds((part, cols), F32)] * 3
            + [sds((cols, part), F32), sds((heads, bucket_count), F32)]
            + [sds((1, per), F32), sds((1, per), F32), sds((EXPERTS, per), F32)],
            [merged[0], swap_chips(merged[1], 4, 2)],
            name="weight_final",
        )
        grad_table = grad_table.T
        grad_router = grad_router.T
        grad_gain_attn = grad_gain_attn.reshape(per)
        grad_gain_expert = grad_gain_expert.reshape(per)
    else:

        def scatter(values, axes, dimension):
            return lax.psum_scatter(values, axes, scatter_dimension=dimension, tiled=True)

        def pick(values):
            at = lax.axis_index("tensor") * (part // members)
            return lax.dynamic_slice_in_dim(scatter(values, "dp", 0), at, part // members)

        grads = expert_grads[0].reshape(width, EXPERTS, 2, hidden_units)
        grad_expert_up = scatter(grads[:, :, 0].transpose(1, 0, 2), "dp", 1)
        grad_expert_down = scatter(grads[:, :, 1].transpose(1, 2, 0), "dp", 2)
        grads, table_rows = weight_grads
        grad_query_weight = scatter(grads[:, 0:cols], "dp", 0)
        grad_key_weight = scatter(grads[:, cols : 2 * cols], "dp", 0)
        grad_value_weight = scatter(grads[:, 2 * cols : 3 * cols], "dp", 0)
        grad_out_weight = scatter(grads[:, 3 * cols :].T, "dp", 1)
        grad_table = lax.psum(table_rows[TABLE_ROW : TABLE_ROW + heads, :bucket_count].T, "dp")
        grad_gain_attn = pick(small[0])
        grad_gain_expert = pick(small[1])
        grad_router = pick(small[2:TABLE_ROW].T)
    return (
        output,
        grad_inputs,
        grad_gain_attn,
        grad_table,
        grad_query_weight,
        grad_key_weight,
        grad_value_weight,
        grad_out_weight,
        grad_gain_expert,
        grad_router,
        grad_expert_up,
        grad_expert_down,
    )


def solution(mesh):
    return jax.shard_map(
        shards,
        mesh=mesh,
        in_specs=(
            P("dp", None),
            P("dp", None),
            P(),
            P("dp"),
            P("dp"),
            P(),
            P(None, "tensor"),
            P(None, "tensor"),
            P(None, "tensor"),
            P(None, "tensor"),
            P("tensor", None),
            P(),
            P(),
            P(None, None, "tensor"),
            P(None, "tensor", None),
            P("dp", None),
        ),
        out_specs=(
            P("dp", None),
            P("dp", None),
            P(("dp", "tensor")),
            P(None, "tensor"),
            P("dp", "tensor"),
            P("dp", "tensor"),
            P("dp", "tensor"),
            P("tensor", "dp"),
            P(("dp", "tensor")),
            P(("dp", "tensor"), None),
            P(None, "dp", "tensor"),
            P(None, "tensor", "dp"),
        ),
        check_vma=False,
    )
```

```python
import functools
import math

import jax
import jax.numpy as jnp
from jax import lax
from jax.experimental import pallas as pl
from jax.experimental.pallas import tpu as pltpu
from jax.sharding import PartitionSpec as P

HEAD_DIM = 64
EXPERTS = 2
CAP = 144
EPS = 1e-06
SMALL_ROWS = 16
TABLE_ROW = 2 + EXPERTS
WEIGHTS = {
    "fetch": 20,
    "expert": 5,
    "expert_grads": 20,
    "hidden_back": 60,
    "expert_merge": 20,
    "attention_back": 60,
    "weight_grads": 4,
    "output_share": 8,
    "input_back": 60,
    "expert_final": 1,
    "weight_final": 1,
}
BF16 = jnp.bfloat16
F32 = jnp.float32
HIGHEST = lax.Precision.HIGHEST
NT = (((1,), (1,)), ((), ()))
TN = (((0,), (0,)), ((), ()))
GELU_C = 0.7978845608028654
GELU_A = 0.044715


def dot(a, b):
    return jnp.dot(a, b, preferred_element_type=F32)


def dot_nt(a, b, precision=None):
    return lax.dot_general(a, b, NT, preferred_element_type=F32, precision=precision)


def dot_tn(a, b):
    return lax.dot_general(a, b, TN, preferred_element_type=F32)


def inverse_rms(values):
    return lax.rsqrt(jnp.mean(values * values, axis=-1, keepdims=True) + EPS)


def share_of(index, rows):
    return pl.ds(pl.multiple_of(index * rows, rows), rows)


def put_shares(acc_ref, share_refs):
    me = lax.axis_index("tensor")
    for k, ref in enumerate(share_refs):
        rows = ref.shape[0]
        ref[...] = acc_ref[share_of(jnp.bitwise_xor(me, k), rows), :].astype(ref.dtype)


def assemble(full_ref, share_refs):
    me = lax.axis_index("tensor")
    for k, ref in enumerate(share_refs):
        rows = ref.shape[0]
        full_ref[share_of(jnp.bitwise_xor(me, k), rows), :] = ref[...]


def total_of(refs):
    total = refs[0][...].astype(F32)
    for ref in refs[1:]:
        total = total + ref[...].astype(F32)
    return total


def column_of(row, length):
    eye = lax.broadcasted_iota(jnp.int32, (length, length), 0) == lax.broadcasted_iota(
        jnp.int32, (length, length), 1
    )
    return jnp.sum(jnp.where(eye, row, jnp.zeros_like(row)), axis=1, keepdims=True)


def head_mask(head, width):
    lane = lax.broadcasted_iota(jnp.int32, (1, width), 1)
    return (lane >= head * HEAD_DIM) & (lane < (head + 1) * HEAD_DIM)


def masked(values, head):
    return jnp.where(head_mask(head, values.shape[1]), values, jnp.zeros_like(values))


def bucket_hot_of(buckets_ref, bucket_count):
    offsets = buckets_ref.shape[1]
    return (
        lax.broadcasted_iota(jnp.int32, (bucket_count, offsets), 0) == buckets_ref[...]
    ).astype(F32)


def attention_kernel(members, *refs):
    sources, outs = refs[:9], refs[9 : members + 15]
    normed_o, q_o, k_o, v_o, probs_o, mixed_o = outs[members:]
    acc, offset_rows = refs[members + 15 : members + 17]
    local, sems = refs[members + 17 : members + 26], refs[members + 26]
    copies = [
        pltpu.make_async_copy(source, held, sems.at[i])
        for i, (source, held) in enumerate(zip(sources, local))
    ]
    for copy in copies:
        copy.start()
    inputs, gain, wq, wk, wv, buckets, table, segment, wo = local
    length = inputs.shape[0]
    heads = wq.shape[0] // HEAD_DIM
    copies[0].wait()
    x = inputs[...].astype(F32)
    scaled = x * inverse_rms(x)
    for copy in copies[1:8]:
        copy.wait()
    normed = (scaled * gain[...].reshape(1, -1)).astype(BF16)
    normed_o[...] = normed
    q = dot_nt(normed, wq[...]).astype(BF16)
    k = dot_nt(normed, wk[...]).astype(BF16)
    v = dot_nt(normed, wv[...]).astype(BF16)
    q_o[...] = q
    k_o[...] = k
    v_o[...] = v
    hot = bucket_hot_of(buckets, table.shape[1])
    seg_row = segment[...].astype(F32)
    same = column_of(seg_row, length) == seg_row
    mixed = jnp.zeros((length, wq.shape[0]), F32)
    offset_rows[...] = jnp.zeros_like(offset_rows)
    offset_rows[0:heads, 0 : hot.shape[1]] = jnp.dot(
        table[...], hot, preferred_element_type=F32, precision=HIGHEST
    )
    for h in range(heads):
        spread = jnp.broadcast_to(offset_rows[h : h + 1, :], (length, 2 * length))
        bias = pltpu.roll(spread, length + 1, 1, stride=1, stride_axis=0)[:, :length]
        scores = dot_nt(masked(q, h), k) + bias
        scores = jnp.where(same, scores, -1e30)
        shifted = jnp.exp(scores - jnp.max(scores, axis=-1, keepdims=True))
        probs = shifted / jnp.sum(shifted, axis=-1, keepdims=True)
        probs_o[h] = probs
        mixed = mixed + dot(probs.astype(BF16), masked(v, h))
    mixed = mixed.astype(BF16)
    mixed_o[...] = mixed
    copies[8].wait()
    acc[...] = dot(mixed, wo[...])
    put_shares(acc, outs[:members])
    own = share_of(lax.axis_index("tensor"), outs[0].shape[0])
    outs[0][...] += inputs[own, :].astype(F32)


def hidden_kernel(members, gain, *rest):
    hidden_o, normed_o = rest[members:]
    hidden = total_of(rest[:members])
    hidden_o[...] = hidden
    normed_o[...] = (hidden * inverse_rms(hidden) * gain[...]).astype(BF16)


def fetch_kernel(up, down, up_o, down_o, sems):
    copies = [
        pltpu.make_async_copy(up, up_o, sems.at[0]),
        pltpu.make_async_copy(down, down_o, sems.at[1]),
    ]
    for copy in copies:
        copy.start()
    for copy in copies:
        copy.wait()


def expert_kernel(members, where_to, cotangent, router_t, up, down, *rest):
    pieces = rest[:members]
    rest = rest[members:]
    back_o, row_o = rest[:members], rest[members : members + 2]
    buffer_o, active_o, grad_before_o, grad_expert_o, router_o, dy_o = rest[
        members + 2 : members + 8
    ]
    normed, backs, rows, acc = rest[members + 8 :]
    length = cotangent.shape[0]
    assemble(normed, pieces)
    dy_o[...] = cotangent[share_of(lax.axis_index("tensor"), dy_o.shape[0]), :]
    place = (
        lax.broadcasted_iota(jnp.int32, (EXPERTS * CAP, length), 0) == where_to[...]
    ).astype(BF16)
    buffer = dot(place, normed[...]).astype(BF16)
    buffer_o[...] = buffer
    dy_buffer = dot(place, cotangent[...])
    router_rows = router_t[...].astype(F32)
    router_grad = [jnp.zeros((1, buffer.shape[1]), F32) for _ in range(EXPERTS)]
    for e in range(EXPERTS):
        slot = slice(e * CAP, (e + 1) * CAP)
        rows_in = buffer[slot]
        logits = dot_nt(rows_in, router_t[...])
        shifted = jnp.exp(logits - jnp.max(logits, axis=-1, keepdims=True))
        router_probs = shifted / jnp.sum(shifted, axis=-1, keepdims=True)
        gate = router_probs[:, e : e + 1]
        dy = dy_buffer[slot]
        grad_expert = (dy * gate).astype(BF16)
        grad_expert_o[slot, :] = grad_expert
        before = dot(rows_in, up[e])
        inner = jnp.tanh(GELU_C * (before + GELU_A * before * before * before))
        active = (0.5 * before * (1.0 + inner)).astype(BF16)
        active_o[slot, :] = active
        slope = 0.5 * (1.0 + inner) + 0.5 * before * (1.0 - inner * inner) * GELU_C * (
            1.0 + 3.0 * GELU_A * before * before
        )
        result = dot(active, down[e])
        grad_before = (dot_nt(grad_expert, down[e]) * slope).astype(BF16)
        grad_before_o[slot, :] = grad_before
        rows[slot, :] = (result * gate).astype(BF16)
        scaled = jnp.sum(dy * result, axis=-1, keepdims=True) * gate
        back = dot_nt(grad_before, up[e])
        for other in range(EXPERTS):
            own = 1.0 if other == e else 0.0
            grad_logit = scaled * (own - router_probs[:, other : other + 1])
            router_grad[other] = router_grad[other] + jnp.sum(
                grad_logit * rows_in.astype(F32), axis=0, keepdims=True
            )
            back = back + grad_logit * router_rows[other : other + 1, :]
        backs[slot, :] = back.astype(BF16)
    for other in range(EXPERTS):
        router_o[other : other + 1, :] = router_grad[other]
    acc[...] = dot_tn(place, backs[...])
    put_shares(acc, back_o)
    acc[...] = dot_tn(place, rows[...])
    me = lax.axis_index("tensor")
    share = back_o[0].shape[0]
    for first, ref in enumerate(row_o):
        for k in range(2):
            index = jnp.bitwise_xor(me, first + 2 * k)
            ref[k * share : (k + 1) * share, :] = acc[share_of(index, share), :].astype(BF16)


def split_rows(keep, send, chip, part):
    core = lax.rem(lax.axis_index("dp"), 2)
    return share_of(2 * chip + core, part), share_of(2 * chip + 1 - core, part)


def expert_grad_kernel(split, buffer, active, grad_before, grad_expert, *rest):
    width = buffer.shape[1]
    scratch = rest[-1]
    for e in range(EXPERTS):
        slot = slice(e * CAP, (e + 1) * CAP)
        for which in range(2):
            if which == 0:
                product = dot_tn(buffer[slot, :], grad_before[slot, :])
            else:
                product = dot_tn(grad_expert[slot, :], active[slot, :])
            hidden_units = active.shape[1]
            first = (2 * e + which) * hidden_units
            if not split:
                rest[0][:, first : first + hidden_units] = product
                continue
            keep, send = rest[0], rest[1]
            part = keep.shape[1]
            scratch[...] = product
            for chip in range(keep.shape[0]):
                mine, other = split_rows(keep, send, chip, part)
                keep[chip, :, first : first + hidden_units] = scratch[mine, :].astype(BF16)
                send[chip, :, first : first + hidden_units] = scratch[other, :].astype(BF16)


def chip_bits():
    core = lax.rem(lax.axis_index("dp"), 2)
    return 1 + core, 2 - core


def merge_kernel(kept, came, keep, send):
    chip = lax.div(lax.axis_index("dp"), 2)
    first, second = chip_bits()
    for ref, start in ((keep, chip), (send, jnp.bitwise_xor(chip, first))):
        for k, there in enumerate((start, jnp.bitwise_xor(start, second))):
            total = kept[there].astype(F32) + came[there].astype(F32)
            ref[k] = total.astype(ref.dtype)


def add_kernel(one, other, out):
    out[...] = one[...] + other[...]


def cross_kernel(kept, came, weight_kept, weight_came, own, send, weight_keep):
    rows, columns = own.shape
    own[...] = kept[0] + came[0].astype(F32)
    send[0:rows, :] = (kept[1] + came[1].astype(F32)).astype(BF16)
    chip = lax.div(lax.axis_index("dp"), 2)
    second, first = chip_bits()
    width = weight_keep.shape[2]
    half = rows // 2
    for k in range(2):
        mine = jnp.bitwise_xor(chip, k * second)
        weight_keep[k] = weight_kept[mine].astype(F32) + weight_came[mine].astype(F32)
        there = jnp.bitwise_xor(mine, first)
        total = (weight_kept[there].astype(F32) + weight_came[there].astype(F32)).astype(BF16)
        for i in range(2):
            at = (2 * k + i) * width
            send[rows : rows + half, at : at + width] = total[i * half : (i + 1) * half]


def weight_cross_kernel(kept, came, own, send):
    rows, width = own.shape
    half = rows // 2
    for k, ref in enumerate((own, send)):
        for i in range(2):
            at = (2 * k + i) * width
            arrived = came[rows : rows + half, at : at + width].astype(F32)
            part = slice(i * half, (i + 1) * half)
            ref[part, :] = (kept[k, part, :] + arrived).astype(ref.dtype)


def expert_final_kernel(*refs):
    up_o, down_o = refs[2:]
    total = refs[0][...] + refs[1][0 : refs[0].shape[0], :].astype(F32)
    for e in range(EXPERTS):
        width = up_o.shape[2]
        first = 2 * e * width
        up_o[e] = total[:, first : first + width]
        down_o[e] = total[:, first + width : first + 2 * width]


def pair_sum_kernel(kept, came, own, other):
    share = own.shape[0]
    own[...] = kept[0:share, :].astype(F32) + came[0:share, :].astype(F32)
    other[...] = (kept[share:, :].astype(F32) + came[share:, :].astype(F32)).astype(BF16)


def output_kernel(hidden, own, came, out):
    out[...] = (hidden[...] + own[...] + came[...].astype(F32)).astype(BF16)


def pair_kernel(own, came, out):
    share = own.shape[0]
    out[0:share, :] = own[...]
    out[share:, :] = came[...]


def pair_rows_kernel(own, came, out):
    me = lax.axis_index("tensor")
    share = own.shape[0] // 2
    for first, ref in enumerate((own, came)):
        for k in range(2):
            index = jnp.bitwise_xor(me, first + 2 * k)
            out[share_of(index, share), :] = ref[k * share : (k + 1) * share, :]


def gather_kernel(*refs):
    assemble(refs[-1], refs[:-1])


def hidden_back_kernel(members, hidden, cotangent, gain, rows, *rest):
    parts = rest[:members]
    grad_o, low_o, gain_o, rows_o = rest[members:]
    rows_o[...] = rows[...]
    h = hidden[...]
    dy = cotangent[...].astype(F32)
    r = inverse_rms(h)
    grad_normed = total_of(parts)
    z = grad_normed * gain[...]
    gain_o[...] = jnp.sum(grad_normed * h * r, axis=0, keepdims=True)
    grad = dy + r * z - h * (r * r * r) * jnp.mean(z * h, axis=-1, keepdims=True)
    grad_o[...] = grad
    low_o[...] = grad.astype(BF16)


def attention_back_kernel(
    members, inputs, probs, q, k, v, wq, wk, wv, wo, gain_two, router, *rest
):
    pieces = rest[:members]
    rest = rest[members:]
    share_o = rest[:members]
    grads_o, attended_o, scores_o = rest[members : members + 3]
    acc = rest[members + 3]
    assemble(attended_o, pieces)
    heads = wq.shape[0] // HEAD_DIM
    grad_mixed = dot_nt(attended_o[...], wo[...]).astype(BF16)
    qv, kv, vv = q[...], k[...], v[...]
    dq = jnp.zeros(qv.shape, F32)
    dk = jnp.zeros(qv.shape, F32)
    dv = jnp.zeros(qv.shape, F32)
    for h in range(heads):
        grad_mixed_h = masked(grad_mixed, h)
        p = probs[h]
        grad_probs = dot_nt(grad_mixed_h, vv)
        inner = jnp.sum(p * grad_probs, axis=-1, keepdims=True)
        grad_scores = (p * (grad_probs - inner)).astype(BF16)
        scores_o[h] = grad_scores
        dq = dq + dot(grad_scores, masked(kv, h))
        dk = dk + dot_tn(grad_scores, masked(qv, h))
        dv = dv + dot_tn(p.astype(BF16), grad_mixed_h)
    dq, dk, dv = dq.astype(BF16), dk.astype(BF16), dv.astype(BF16)
    grads_o[0] = dq
    grads_o[1] = dk
    grads_o[2] = dv
    total = dot(dq, wq[...]) + dot(dk, wk[...]) + dot(dv, wv[...])
    acc[...] = total
    x = inputs[...].astype(F32)
    gain_one = jnp.sum(total * x * inverse_rms(x), axis=0, keepdims=True)
    small = jnp.concatenate(
        [
            gain_one,
            gain_two[...],
            router[...],
            jnp.zeros((SMALL_ROWS - 2 - EXPERTS, gain_one.shape[1]), F32),
        ],
        axis=0,
    )
    me = lax.axis_index("tensor")
    for k, ref in enumerate(share_o):
        share = ref.shape[0] - SMALL_ROWS
        ref[0:share, :] = acc[share_of(jnp.bitwise_xor(me, k), share), :].astype(ref.dtype)
        ref[share:, :] = small.astype(ref.dtype)


def weight_grad_kernel(
    split, normed, grads, attended, mixed, scores, buckets, *rest
):
    bucket_count = 32
    small, scratch = rest[-2:]
    length = normed.shape[0]
    cols = grads.shape[2]
    normed_v = normed[...]
    for i in range(4):
        if i < 3:
            product = dot_tn(normed_v, grads[i])
        else:
            product = dot_tn(attended[...], mixed[...])
        scratch[:, i * cols : (i + 1) * cols] = product
    small[...] = jnp.zeros_like(small)
    flip = (
        lax.broadcasted_iota(jnp.int32, (length, length), 0)
        + lax.broadcasted_iota(jnp.int32, (length, length), 1)
        == length - 1
    ).astype(BF16)
    hot = (
        lax.broadcasted_iota(jnp.int32, (bucket_count, 2 * length), 0) == buckets[...]
    ).astype(F32)
    for h in range(scores.shape[0]):
        flipped = dot(flip, scores[h])
        wide = jnp.concatenate([flipped, jnp.zeros_like(flipped)], axis=1)
        sheared = pltpu.roll(wide, 0, 1, stride=1, stride_axis=0)
        offsets = jnp.sum(sheared, axis=0, keepdims=True)
        small[TABLE_ROW + h : TABLE_ROW + h + 1, 0:bucket_count] = dot_nt(
            jnp.broadcast_to(offsets, (8, 2 * length)), hot, HIGHEST
        )[0:1]
    if not split:
        rest[0][...] = scratch[...]
        return
    keep, send = rest[0], rest[1]
    chips, part, _ = keep.shape
    for chip in range(chips):
        mine, other = split_rows(keep, send, chip, part)
        keep[chip] = scratch[mine, :].astype(BF16)
        send[chip] = scratch[other, :].astype(BF16)


def weight_final_kernel(*refs):
    wq_o, wk_o, wv_o, wo_o = refs[2:]
    total = total_of(refs[:2])
    part, cols = wq_o.shape
    wq_o[...] = total[0:part, 0:cols]
    wk_o[...] = total[0:part, cols : 2 * cols]
    wv_o[...] = total[0:part, 2 * cols : 3 * cols]
    wo_o[...] = total[0:part, 3 * cols : 4 * cols].T


def small_final_kernel(members, one, other, one_o, two_o, router_o, table_o):
    small = one[...] + other[...]
    per = one_o.shape[1]
    first = (lax.axis_index("dp") * members + lax.axis_index("tensor")) * per
    shape = (per, small.shape[1])
    pick = (
        lax.broadcasted_iota(jnp.int32, shape, 0) + first
        == lax.broadcasted_iota(jnp.int32, shape, 1)
    ).astype(F32)
    rows = dot_nt(small, pick, HIGHEST)
    one_o[...] = rows[0:1]
    two_o[...] = rows[1:2]
    router_o[...] = rows[2:TABLE_ROW]
    heads, bucket_count = table_o.shape
    table_o[...] = small[TABLE_ROW : TABLE_ROW + heads, 0:bucket_count]


def input_back_kernel(members, inputs, gain, grad_hidden, table, *rest):
    out, small_o = rest[members:]
    share = out.shape[0]
    x = inputs[share_of(lax.axis_index("tensor"), share), :].astype(F32)
    r = inverse_rms(x)
    total = total_of(rest[:members])
    small_o[...] = total[share : share + small_o.shape[0]] + table[...]
    z = total[0:share] * gain[...]
    out[...] = (
        grad_hidden[...] + r * z - x * (r * r * r) * jnp.mean(z * x, axis=-1, keepdims=True)
    ).astype(BF16)


def run(kernel, outs, args, scratch=(), name=None, after=(), space=pltpu.VMEM, out=pltpu.VMEM):
    vmem = pl.BlockSpec(memory_space=pltpu.VMEM)
    anywhere = pl.BlockSpec(memory_space=pl.ANY)
    count, extra = len(args), len(after)
    held = [*args, *outs, *(x for x in scratch if x.memory_space == pltpu.VMEM)]
    size = sum(math.prod(x.shape) * jnp.dtype(x.dtype).itemsize for x in held)

    def body(*refs):
        kernel(*refs[:count], *refs[count + extra :])

    return pl.pallas_call(
        body,
        out_shape=[out(o.shape, o.dtype) for o in outs] if out else outs,
        in_specs=[pl.BlockSpec(memory_space=space)] * count + [anywhere] * extra,
        out_specs=[vmem] * len(outs),
        scratch_shapes=list(scratch),
        compiler_params=pltpu.CompilerParams(vmem_limit_bytes=size + size // 4 + 4 * 1024 * 1024),
        cost_estimate=pl.CostEstimate(
            flops=int(WEIGHTS.get(name, 0.2) * 1e9), bytes_accessed=0, transcendentals=0
        ),
        name=name,
    )(*args, *after)


def sds(shape, dtype):
    return jax.ShapeDtypeStruct(tuple(shape), dtype)


def swap(values, axis, k):
    size = lax.axis_size(axis)
    return lax.ppermute(values, axis, [(i, i ^ k) for i in range(size)])


def swap_chips(values, even, odd):
    size = lax.axis_size("dp")
    pairs = [(i, i ^ (odd if i % 2 else even)) for i in range(size)]
    return lax.ppermute(values, "dp", pairs)


def exchange(shares):
    return [shares[0]] + [swap(s, "tensor", k) for k, s in enumerate(shares) if k > 0]


def spread(share):
    members = lax.axis_size("tensor")
    return [share] + [swap(share, "tensor", k) for k in range(1, members)]


def shards(
    inputs,
    segments,
    buckets,
    routes,
    capacity_slots,
    gain_attn,
    bias_table,
    query_weight,
    key_weight,
    value_weight,
    out_weight,
    gain_expert,
    router_weight,
    expert_up,
    expert_down,
    cotangent,
):
    length, width = inputs.shape
    members = lax.axis_size("tensor")
    dp = lax.axis_size("dp")
    share = length // members
    cols = query_weight.shape[1]
    heads = cols // HEAD_DIM
    hidden_units = expert_up.shape[2]
    bucket_count = bias_table.shape[0]
    part = width // dp
    split = dp == 8 and part % 16 == 0
    chips = dp // 2
    bind = functools.partial

    def shares_sds(dtype, own=None):
        return [sds((share, width), own or dtype)] + [
            sds((share, width), dtype) for _ in range(members - 1)
        ]

    gain_row = gain_attn.reshape(1, width)
    gain_two_row = gain_expert.reshape(1, width)
    bucket_row = buckets.reshape(1, -1)
    bucket_wide = jnp.pad(bucket_row, ((0, 0), (0, 1)), constant_values=-1)
    where_to = (routes * CAP + capacity_slots).reshape(1, length)
    router_t = router_weight.T
    query_t, key_t, value_t = query_weight.T, key_weight.T, value_weight.T

    attention_args = [
        inputs,
        gain_attn,
        query_t,
        key_t,
        value_t,
        bucket_row,
        bias_table.T,
        segments,
        out_weight,
    ]
    attention_args = [pltpu.with_memory_space_constraint(a, pltpu.HBM) for a in attention_args]
    outs = run(
        bind(attention_kernel, members),
        shares_sds(BF16, F32)
        + [sds((length, width), BF16)]
        + [sds((length, cols), BF16)] * 3
        + [sds((heads, length, length), F32), sds((length, cols), BF16)],
        attention_args,
        [pltpu.VMEM((length, width), F32), pltpu.VMEM((8, 2 * length), F32)]
        + [pltpu.VMEM(a.shape, a.dtype) for a in attention_args]
        + [pltpu.SemaphoreType.DMA((len(attention_args),))],
        name="attention",
        space=pltpu.HBM,
    )
    attended = exchange(outs[:members])
    normed, q, k, v, probs, mixed = outs[members:]

    hidden, normed_two = run(
        bind(hidden_kernel, members),
        [sds((share, width), F32), sds((share, width), BF16)],
        [gain_two_row] + attended,
        name="hidden",
    )
    up, down = run(
        fetch_kernel,
        [sds(expert_up.shape, BF16), sds(expert_down.shape, BF16)],
        [pltpu.with_memory_space_constraint(a, pltpu.HBM) for a in (expert_up, expert_down)],
        [pltpu.SemaphoreType.DMA((2,))],
        name="fetch",
        space=pltpu.HBM,
        after=[normed_two],
    )
    normed_two = spread(normed_two)

    slots = EXPERTS * CAP
    outs = run(
        bind(expert_kernel, members),
        shares_sds(BF16)
        + [sds((2 * share, width), BF16)] * 2
        + [sds((slots, width), BF16)]
        + [sds((slots, hidden_units), BF16)] * 2
        + [sds((slots, width), BF16), sds((EXPERTS, width), F32), sds((share, width), BF16)],
        [where_to, cotangent, router_t, up, down] + normed_two,
        [
            pltpu.VMEM((length, width), BF16),
            pltpu.VMEM((slots, width), BF16),
            pltpu.VMEM((slots, width), BF16),
            pltpu.VMEM((length, width), F32),
        ],
        name="expert",
    )
    back_rows = exchange(outs[:members])
    rows_kept, rows_sent = outs[members : members + 2]
    buffer, active, grad_before, grad_expert, grad_router, dy_share = outs[members + 2 :]

    def split_sds(rows, columns):
        return [sds((chips, rows, columns), BF16)] * 2

    def merge_sds(rows, columns):
        return [sds((2, rows, columns), F32), sds((2, rows, columns), BF16)]

    expert_grads = run(
        bind(expert_grad_kernel, split),
        split_sds(part, 4 * hidden_units) if split else [sds((width, 4 * hidden_units), F32)],
        [buffer, active, grad_before, grad_expert],
        [pltpu.VMEM((width, hidden_units), F32)],
        name="expert_grads",
    )

    grad_hidden, grad_attended, grad_gain_expert, rows_sent = run(
        bind(hidden_back_kernel, members),
        [sds((share, width), F32), sds((share, width), BF16), sds((1, width), F32)]
        + [sds((2 * share, width), BF16)],
        [hidden, dy_share, gain_two_row, rows_sent] + back_rows,
        name="hidden_back",
        after=expert_grads[-1:],
    )
    grad_attended = spread(grad_attended)

    own_rows, other_rows = run(
        pair_sum_kernel,
        [sds((share, width), F32), sds((share, width), BF16)],
        [rows_kept, swap(rows_sent, "tensor", 1)],
        name="pair_sum",
        after=[grad_attended[0]],
    )
    expert_merged = []
    if split:
        expert_merged = run(
            merge_kernel,
            merge_sds(part, 4 * hidden_units),
            [expert_grads[0], swap(expert_grads[1], "dp", 1)],
            name="expert_merge",
        )
    crossed = []

    def tall_sds(dtype):
        return sds((share + SMALL_ROWS, width), dtype)

    outs = run(
        bind(attention_back_kernel, members),
        [tall_sds(F32)]
        + [tall_sds(BF16)] * (members - 1)
        + [
            sds((3, length, cols), BF16),
            sds((length, width), BF16),
            sds((heads, length, length), BF16),
        ],
        [inputs, probs, q, k, v, query_t, key_t, value_t, out_weight]
        + [grad_gain_expert, grad_router]
        + grad_attended,
        [pltpu.VMEM((length, width), F32)],
        name="attention_back",
        after=[own_rows, *expert_merged[:1]],
    )
    grad_normed = exchange(outs[:members])
    projections, attended_low, grad_scores = outs[members:]

    weight_cols = 4 * cols
    weight_grads = run(
        bind(weight_grad_kernel, split),
        (split_sds(part, weight_cols) if split else [sds((width, weight_cols), F32)])
        + [sds((8, width), F32)],
        [normed, projections, attended_low, mixed, grad_scores, bucket_wide],
        [pltpu.VMEM((width, weight_cols), F32)],
        name="weight_grads",
    )

    (output_share,) = run(
        output_kernel,
        [sds((share, width), BF16)],
        [hidden, own_rows, swap(other_rows, "tensor", 2)],
        name="output_share",
        after=weight_grads[-1:],
    )
    if split:
        expert_own, crossing, weight_kept = run(
            cross_kernel,
            [
                sds((part, 4 * hidden_units), F32),
                sds((part + part // 2, 4 * hidden_units), BF16),
                sds((2, part, weight_cols), F32),
            ],
            [
                expert_merged[0],
                swap_chips(expert_merged[1], 2, 4),
                weight_grads[0],
                swap(weight_grads[1], "dp", 1),
            ],
            name="cross",
            after=[output_share],
        )
        crossed = [expert_own]
    grad_inputs, small = run(
        bind(input_back_kernel, members),
        [sds((share, width), BF16), sds((8, width), F32)],
        [inputs, gain_row, grad_hidden, weight_grads[-1]] + grad_normed,
        name="input_back",
        after=crossed,
    )
    (output_pair,) = run(
        pair_kernel,
        [sds((2 * share, width), BF16)],
        [output_share, swap(output_share, "tensor", 2)],
        name="output_pair",
        after=[small],
    )
    (output,) = run(
        pair_rows_kernel,
        [sds((length, width), BF16)],
        [output_pair, swap(output_pair, "tensor", 1)],
        name="output_rows",
        out=None,
    )


    input_parts = spread(grad_inputs)
    (grad_inputs,) = run(
        gather_kernel, [sds((length, width), BF16)], input_parts, name="grad_rows", out=None
    )

    if split:
        crossing = swap_chips(crossing, 4, 2)
        grad_expert_up, grad_expert_down = run(
            expert_final_kernel,
            [sds((EXPERTS, part, hidden_units), F32), sds((EXPERTS, part, hidden_units), F32)],
            [expert_own, crossing],
            name="expert_final", out=None,
        )
        grad_expert_down = grad_expert_down.transpose(0, 2, 1)
        weight_own, weight_sent = run(
            weight_cross_kernel,
            [sds((part, weight_cols), F32), sds((part, weight_cols), BF16)],
            [weight_kept, crossing],
            name="weight_cross",
        )
        (grad_query_weight, grad_key_weight, grad_value_weight, grad_out_weight) = run(
            weight_final_kernel,
            [sds((part, cols), F32)] * 3 + [sds((cols, part), F32)],
            [weight_own, swap_chips(weight_sent, 2, 4)],
            name="weight_final", out=None,
        )
        for step in range(2):
            came = swap(small, "dp", 1) if step == 0 else swap_chips(small, 2, 4)
            (small,) = run(
                add_kernel,
                [sds(small.shape, F32)],
                [small, came],
                name="small_sum",
                after=input_parts[2:] if step == 1 else input_parts[1:2],
            )
        per = part // members
        grad_gain_attn, grad_gain_expert, grad_router, grad_table = run(
            bind(small_final_kernel, members),
            [sds((1, per), F32), sds((1, per), F32), sds((EXPERTS, per), F32)]
            + [sds((heads, bucket_count), F32)],
            [small, swap_chips(small, 4, 2)],
            name="small_final", out=None,
        )
        grad_table = grad_table.T
        grad_router = grad_router.T
        grad_gain_attn = grad_gain_attn.reshape(per)
        grad_gain_expert = grad_gain_expert.reshape(per)
    else:

        def scatter(values, axes, dimension):
            return lax.psum_scatter(values, axes, scatter_dimension=dimension, tiled=True)

        def pick(values):
            at = lax.axis_index("tensor") * (part // members)
            return lax.dynamic_slice_in_dim(scatter(values, "dp", 0), at, part // members)

        grads = expert_grads[0].reshape(width, EXPERTS, 2, hidden_units)
        grad_expert_up = scatter(grads[:, :, 0].transpose(1, 0, 2), "dp", 1)
        grad_expert_down = scatter(grads[:, :, 1].transpose(1, 2, 0), "dp", 2)
        grads = weight_grads[0]
        grad_query_weight = scatter(grads[:, 0:cols], "dp", 0)
        grad_key_weight = scatter(grads[:, cols : 2 * cols], "dp", 0)
        grad_value_weight = scatter(grads[:, 2 * cols : 3 * cols], "dp", 0)
        grad_out_weight = scatter(grads[:, 3 * cols :].T, "dp", 1)
        grad_table = lax.psum(small[TABLE_ROW : TABLE_ROW + heads, :bucket_count].T, "dp")
        grad_gain_attn = pick(small[0])
        grad_gain_expert = pick(small[1])
        grad_router = pick(small[2:TABLE_ROW].T)
    return (
        output,
        grad_inputs,
        grad_gain_attn,
        grad_table,
        grad_query_weight,
        grad_key_weight,
        grad_value_weight,
        grad_out_weight,
        grad_gain_expert,
        grad_router,
        grad_expert_up,
        grad_expert_down,
    )


def solution(mesh):
    return jax.shard_map(
        shards,
        mesh=mesh,
        in_specs=(
            P("dp", None),
            P("dp", None),
            P(),
            P("dp"),
            P("dp"),
            P(),
            P(None, "tensor"),
            P(None, "tensor"),
            P(None, "tensor"),
            P(None, "tensor"),
            P("tensor", None),
            P(),
            P(),
            P(None, None, "tensor"),
            P(None, "tensor", None),
            P("dp", None),
        ),
        out_specs=(
            P("dp", None),
            P("dp", None),
            P(("dp", "tensor")),
            P(None, "tensor"),
            P("dp", "tensor"),
            P("dp", "tensor"),
            P("dp", "tensor"),
            P("tensor", "dp"),
            P(("dp", "tensor")),
            P(("dp", "tensor"), None),
            P(None, "dp", "tensor"),
            P(None, "tensor", "dp"),
        ),
        check_vma=False,
    )
```

```python
import functools
import math

import jax
import jax.numpy as jnp
from jax import lax
from jax.experimental import pallas as pl
from jax.experimental.pallas import tpu as pltpu
from jax.sharding import PartitionSpec as P

HEAD_DIM = 64
EXPERTS = 2
CAP = 144
EPS = 1e-06
SMALL_ROWS = 16
GAIN_ROWS = 8
TABLE_ROW = 2 + EXPERTS
WEIGHTS = {
    "fetch": 20,
    "expert": 5,
    "expert_grads": 20,
    "hidden_back": 60,
    "expert_merge": 20,
    "attention_back": 5,
    "pair_sum": 8,
    "weight_grads": 4,
    "expert_cross": 8,
    "input_back": 60,
    "expert_final": 0.001,
    "weight_final": 0.001,
    "small_sum": 0.001,
    "weight_cross": 0.001,
}
BF16 = jnp.bfloat16
F32 = jnp.float32
HIGHEST = lax.Precision.HIGHEST
NT = (((1,), (1,)), ((), ()))
TN = (((0,), (0,)), ((), ()))
GELU_C = 0.7978845608028654
GELU_A = 0.044715


def dot(a, b):
    return jnp.dot(a, b, preferred_element_type=F32)


def dot_nt(a, b, precision=None):
    return lax.dot_general(a, b, NT, preferred_element_type=F32, precision=precision)


def dot_tn(a, b):
    return lax.dot_general(a, b, TN, preferred_element_type=F32)


def inverse_rms(values):
    return lax.rsqrt(jnp.mean(values * values, axis=-1, keepdims=True) + EPS)


def share_of(index, rows):
    return pl.ds(pl.multiple_of(index * rows, rows), rows)


def distance(place, members):
    return (members - place) % members


def member_at(place, members):
    return jnp.bitwise_xor(lax.axis_index("tensor"), distance(place, members))


def put_shares(acc_ref, share_refs):
    for i, ref in enumerate(share_refs):
        there = share_of(member_at(i, len(share_refs)), ref.shape[0])
        ref[...] = acc_ref[there, :].astype(ref.dtype)


def assemble(full_ref, share_refs):
    for i, ref in enumerate(share_refs):
        full_ref[share_of(member_at(i, len(share_refs)), ref.shape[0]), :] = ref[...]


def total_of(refs):
    total = refs[0][...].astype(F32)
    for ref in refs[1:]:
        total = total + ref[...].astype(F32)
    return total


def column_of(row, length):
    eye = lax.broadcasted_iota(jnp.int32, (length, length), 0) == lax.broadcasted_iota(
        jnp.int32, (length, length), 1
    )
    return jnp.sum(jnp.where(eye, row, jnp.zeros_like(row)), axis=1, keepdims=True)


def head_mask(head, width):
    lane = lax.broadcasted_iota(jnp.int32, (1, width), 1)
    return (lane >= head * HEAD_DIM) & (lane < (head + 1) * HEAD_DIM)


def masked(values, head):
    return jnp.where(head_mask(head, values.shape[1]), values, jnp.zeros_like(values))


def bucket_hot_of(buckets_ref, bucket_count):
    offsets = buckets_ref.shape[1]
    return (
        lax.broadcasted_iota(jnp.int32, (bucket_count, offsets), 0) == buckets_ref[...]
    ).astype(F32)


def attention_kernel(members, *refs):
    sources, outs = refs[:9], refs[9 : members + 15]
    normed_o, q_o, k_o, v_o, probs_o, mixed_o = outs[members:]
    acc, offset_rows = refs[members + 15 : members + 17]
    local, sems = refs[members + 17 : members + 26], refs[members + 26]
    copies = [
        pltpu.make_async_copy(source, held, sems.at[i])
        for i, (source, held) in enumerate(zip(sources, local))
    ]
    for copy in copies:
        copy.start()
    inputs, gain, wq, wk, wv, buckets, table, segment, wo = local
    length = inputs.shape[0]
    heads = wq.shape[0] // HEAD_DIM
    copies[0].wait()
    x = inputs[...].astype(F32)
    scaled = x * inverse_rms(x)
    for copy in copies[1:8]:
        copy.wait()
    normed = (scaled * gain[...].reshape(1, -1)).astype(BF16)
    normed_o[...] = normed
    q = dot_nt(normed, wq[...]).astype(BF16)
    k = dot_nt(normed, wk[...]).astype(BF16)
    v = dot_nt(normed, wv[...]).astype(BF16)
    q_o[...] = q
    k_o[...] = k
    v_o[...] = v
    hot = bucket_hot_of(buckets, table.shape[1])
    seg_row = segment[...].astype(F32)
    same = column_of(seg_row, length) == seg_row
    mixed = jnp.zeros((length, wq.shape[0]), F32)
    offset_rows[...] = jnp.zeros_like(offset_rows)
    offset_rows[0:heads, 0 : hot.shape[1]] = jnp.dot(
        table[...], hot, preferred_element_type=F32, precision=HIGHEST
    )
    for h in range(heads):
        spread = jnp.broadcast_to(offset_rows[h : h + 1, :], (length, 2 * length))
        bias = pltpu.roll(spread, length + 1, 1, stride=1, stride_axis=0)[:, :length]
        scores = dot_nt(masked(q, h), k) + bias
        scores = jnp.where(same, scores, -1e30)
        shifted = jnp.exp(scores - jnp.max(scores, axis=-1, keepdims=True))
        probs = shifted / jnp.sum(shifted, axis=-1, keepdims=True)
        probs_o[h] = probs
        mixed = mixed + dot(probs.astype(BF16), masked(v, h))
    mixed = mixed.astype(BF16)
    mixed_o[...] = mixed
    copies[8].wait()
    acc[...] = dot(mixed, wo[...])
    put_shares(acc, outs[:members])
    own = share_of(lax.axis_index("tensor"), outs[0].shape[0])
    outs[0][...] += inputs[own, :].astype(F32)


def hidden_kernel(members, gain, *rest):
    hidden_o, normed_o = rest[members:]
    hidden = total_of(rest[:members])
    hidden_o[...] = hidden
    normed_o[...] = (hidden * inverse_rms(hidden) * gain[...]).astype(BF16)


def fetch_kernel(up, down, up_o, down_o, sems):
    copies = [
        pltpu.make_async_copy(up, up_o, sems.at[0]),
        pltpu.make_async_copy(down, down_o, sems.at[1]),
    ]
    for copy in copies:
        copy.start()
    for copy in copies:
        copy.wait()


def expert_kernel(members, where_to, cotangent, router_t, up, down, *rest):
    pieces = rest[:members]
    rest = rest[members:]
    back_o, row_o = rest[:members], rest[members : members + 2]
    buffer_o, active_o, grad_before_o, grad_expert_o, router_o, dy_o = rest[
        members + 2 : members + 8
    ]
    normed, backs, rows, acc = rest[members + 8 :]
    length = cotangent.shape[0]
    assemble(normed, pieces)
    dy_o[...] = cotangent[share_of(lax.axis_index("tensor"), dy_o.shape[0]), :]
    place = (
        lax.broadcasted_iota(jnp.int32, (EXPERTS * CAP, length), 0) == where_to[...]
    ).astype(BF16)
    buffer = dot(place, normed[...]).astype(BF16)
    buffer_o[...] = buffer
    dy_buffer = dot(place, cotangent[...])
    router_rows = router_t[...].astype(F32)
    router_grad = [jnp.zeros((1, buffer.shape[1]), F32) for _ in range(EXPERTS)]
    for e in range(EXPERTS):
        slot = slice(e * CAP, (e + 1) * CAP)
        rows_in = buffer[slot]
        logits = dot_nt(rows_in, router_t[...])
        shifted = jnp.exp(logits - jnp.max(logits, axis=-1, keepdims=True))
        router_probs = shifted / jnp.sum(shifted, axis=-1, keepdims=True)
        gate = router_probs[:, e : e + 1]
        dy = dy_buffer[slot]
        grad_expert = (dy * gate).astype(BF16)
        grad_expert_o[slot, :] = grad_expert
        before = dot(rows_in, up[e])
        inner = jnp.tanh(GELU_C * (before + GELU_A * before * before * before))
        active = (0.5 * before * (1.0 + inner)).astype(BF16)
        active_o[slot, :] = active
        slope = 0.5 * (1.0 + inner) + 0.5 * before * (1.0 - inner * inner) * GELU_C * (
            1.0 + 3.0 * GELU_A * before * before
        )
        result = dot(active, down[e])
        grad_before = (dot_nt(grad_expert, down[e]) * slope).astype(BF16)
        grad_before_o[slot, :] = grad_before
        rows[slot, :] = (result * gate).astype(BF16)
        scaled = jnp.sum(dy * result, axis=-1, keepdims=True) * gate
        back = dot_nt(grad_before, up[e])
        for other in range(EXPERTS):
            own = 1.0 if other == e else 0.0
            grad_logit = scaled * (own - router_probs[:, other : other + 1])
            router_grad[other] = router_grad[other] + jnp.sum(
                grad_logit * rows_in.astype(F32), axis=0, keepdims=True
            )
            back = back + grad_logit * router_rows[other : other + 1, :]
        backs[slot, :] = back.astype(BF16)
    for other in range(EXPERTS):
        router_o[other : other + 1, :] = router_grad[other]
    acc[...] = dot_tn(place, backs[...])
    put_shares(acc, back_o)
    acc[...] = dot_tn(place, rows[...])
    me = lax.axis_index("tensor")
    share = back_o[0].shape[0]
    for first, ref in enumerate(row_o):
        for k in range(2):
            index = jnp.bitwise_xor(me, first + 2 * k)
            ref[k * share : (k + 1) * share, :] = acc[share_of(index, share), :].astype(BF16)


def split_rows(keep, send, chip, part):
    core = lax.rem(lax.axis_index("dp"), 2)
    return share_of(2 * chip + core, part), share_of(2 * chip + 1 - core, part)


def expert_grad_kernel(split, buffer, active, grad_before, grad_expert, rows, *rest):
    scratch, rows_o = rest[-1], rest[-2]
    rows_o[...] = rows[...]
    for e in range(EXPERTS):
        slot = slice(e * CAP, (e + 1) * CAP)
        for which in range(2):
            if which == 0:
                product = dot_tn(buffer[slot, :], grad_before[slot, :])
            else:
                product = dot_tn(grad_expert[slot, :], active[slot, :])
            hidden_units = active.shape[1]
            first = (2 * e + which) * hidden_units
            if not split:
                rest[0][:, first : first + hidden_units] = product
                continue
            keep, send = rest[0], rest[1]
            part = keep.shape[1]
            scratch[...] = product
            for chip in range(keep.shape[0]):
                mine, other = split_rows(keep, send, chip, part)
                keep[chip, :, first : first + hidden_units] = scratch[mine, :].astype(BF16)
                send[chip, :, first : first + hidden_units] = scratch[other, :].astype(BF16)


def chip_bits():
    core = lax.rem(lax.axis_index("dp"), 2)
    return 1 + core, 2 - core


def merge_kernel(kept, came, keep, send):
    chip = lax.div(lax.axis_index("dp"), 2)
    first, second = chip_bits()
    for ref, start in ((keep, chip), (send, jnp.bitwise_xor(chip, first))):
        for k, there in enumerate((start, jnp.bitwise_xor(start, second))):
            total = kept[there].astype(F32) + came[there].astype(F32)
            ref[k] = total.astype(ref.dtype)


def add_kernel(one, other, out):
    out[...] = one[...] + other[...]


def expert_cross_kernel(kept, came, own, send):
    own[...] = kept[0] + came[0].astype(F32)
    send[...] = (kept[1] + came[1].astype(F32)).astype(BF16)


def cross_kernel(expert_send, weight_kept, weight_came, send, weight_keep):
    rows = expert_send.shape[0]
    send[0:rows, :] = expert_send[...]
    chip = lax.div(lax.axis_index("dp"), 2)
    second, first = chip_bits()
    width = weight_keep.shape[2]
    half = rows // 2
    for k in range(2):
        mine = jnp.bitwise_xor(chip, k * second)
        weight_keep[k] = weight_kept[mine].astype(F32) + weight_came[mine].astype(F32)
        there = jnp.bitwise_xor(mine, first)
        total = (weight_kept[there].astype(F32) + weight_came[there].astype(F32)).astype(BF16)
        for i in range(2):
            at = (2 * k + i) * width
            send[rows : rows + half, at : at + width] = total[i * half : (i + 1) * half]


def weight_cross_kernel(kept, came, small, small_came, own, send):
    width = own.shape[1]
    rows = kept.shape[1]
    half = rows // 2
    total = jnp.concatenate([small[...] + small_came[...], jnp.zeros_like(small)], axis=0)
    for k, ref in enumerate((own, send)):
        for i in range(2):
            at = (2 * k + i) * width
            arrived = came[rows : rows + half, at : at + width].astype(F32)
            part = slice(i * half, (i + 1) * half)
            ref[part, :] = (kept[k, part, :] + arrived).astype(ref.dtype)
        ref[rows:, :] = total.astype(ref.dtype)


def expert_final_kernel(*refs):
    up_o, down_o = refs[2:]
    total = refs[0][...] + refs[1][0 : refs[0].shape[0], :].astype(F32)
    for e in range(EXPERTS):
        width = up_o.shape[2]
        first = 2 * e * width
        up_o[e] = total[:, first : first + width]
        down_o[e] = total[:, first + width : first + 2 * width]


def pair_sum_kernel(kept, came, own, other):
    share = own.shape[0]
    own[...] = kept[0:share, :].astype(F32) + came[0:share, :].astype(F32)
    other[...] = (kept[share:, :].astype(F32) + came[share:, :].astype(F32)).astype(BF16)


def rows_kernel(*refs):
    shares, (output, grad_inputs) = refs[:-2], refs[-2:]
    for i, ref in enumerate(shares):
        rows = ref.shape[0] // 2
        there = share_of(member_at(i, len(shares)), rows)
        grad_inputs[there, :] = ref[0:rows, :]
        output[there, :] = ref[rows:, :]


def hidden_back_kernel(members, hidden, cotangent, gain, *rest):
    parts = rest[:members]
    grad_o, low_o, gain_o = rest[members:]
    h = hidden[...]
    dy = cotangent[...].astype(F32)
    r = inverse_rms(h)
    grad_normed = total_of(parts)
    z = grad_normed * gain[...]
    gain_o[...] = jnp.sum(grad_normed * h * r, axis=0, keepdims=True)
    grad = dy + r * z - h * (r * r * r) * jnp.mean(z * h, axis=-1, keepdims=True)
    grad_o[...] = grad
    low_o[...] = grad.astype(BF16)


def attention_back_kernel(
    members, inputs, probs, q, k, v, wq, wk, wv, wo, gain_two, router, *rest
):
    pieces = rest[:members]
    rest = rest[members:]
    share_o = rest[:members]
    grads_o, attended_o, scores_o = rest[members : members + 3]
    acc = rest[members + 3]
    assemble(attended_o, pieces)
    heads = wq.shape[0] // HEAD_DIM
    grad_mixed = dot_nt(attended_o[...], wo[...]).astype(BF16)
    qv, kv, vv = q[...], k[...], v[...]
    dq = jnp.zeros(qv.shape, F32)
    dk = jnp.zeros(qv.shape, F32)
    dv = jnp.zeros(qv.shape, F32)
    for h in range(heads):
        grad_mixed_h = masked(grad_mixed, h)
        p = probs[h]
        grad_probs = dot_nt(grad_mixed_h, vv)
        inner = jnp.sum(p * grad_probs, axis=-1, keepdims=True)
        grad_scores = (p * (grad_probs - inner)).astype(BF16)
        scores_o[h] = grad_scores
        dq = dq + dot(grad_scores, masked(kv, h))
        dk = dk + dot_tn(grad_scores, masked(qv, h))
        dv = dv + dot_tn(p.astype(BF16), grad_mixed_h)
    dq, dk, dv = dq.astype(BF16), dk.astype(BF16), dv.astype(BF16)
    grads_o[0] = dq
    grads_o[1] = dk
    grads_o[2] = dv
    total = dot(dq, wq[...]) + dot(dk, wk[...]) + dot(dv, wv[...])
    acc[...] = total
    x = inputs[...].astype(F32)
    gain_one = jnp.sum(total * x * inverse_rms(x), axis=0, keepdims=True)
    small = jnp.concatenate(
        [
            gain_one,
            gain_two[...],
            router[...],
            jnp.zeros((GAIN_ROWS - TABLE_ROW, gain_one.shape[1]), F32),
        ],
        axis=0,
    )
    for i, ref in enumerate(share_o):
        share = ref.shape[0] - GAIN_ROWS
        ref[0:share, :] = acc[share_of(member_at(i, members), share), :].astype(ref.dtype)
        ref[share:, :] = small.astype(ref.dtype)


def weight_grad_kernel(
    split, normed, grads, attended, mixed, scores, buckets, *rest
):
    bucket_count = 32
    small, scratch = rest[-2:]
    length = normed.shape[0]
    cols = grads.shape[2]
    normed_v = normed[...]
    for i in range(4):
        if i < 3:
            product = dot_tn(normed_v, grads[i])
        else:
            product = dot_tn(attended[...], mixed[...])
        scratch[:, i * cols : (i + 1) * cols] = product
    small[...] = jnp.zeros_like(small)
    flip = (
        lax.broadcasted_iota(jnp.int32, (length, length), 0)
        + lax.broadcasted_iota(jnp.int32, (length, length), 1)
        == length - 1
    ).astype(BF16)
    hot = (
        lax.broadcasted_iota(jnp.int32, (bucket_count, 2 * length), 0) == buckets[...]
    ).astype(F32)
    for h in range(scores.shape[0]):
        flipped = dot(flip, scores[h])
        wide = jnp.concatenate([flipped, jnp.zeros_like(flipped)], axis=1)
        sheared = pltpu.roll(wide, 0, 1, stride=1, stride_axis=0)
        offsets = jnp.sum(sheared, axis=0, keepdims=True)
        small[TABLE_ROW + h : TABLE_ROW + h + 1, 0:bucket_count] = dot_nt(
            jnp.broadcast_to(offsets, (8, 2 * length)), hot, HIGHEST
        )[0:1]
    if not split:
        rest[0][...] = scratch[...]
        return
    keep, send = rest[0], rest[1]
    chips, part, _ = keep.shape
    for chip in range(chips):
        mine, other = split_rows(keep, send, chip, part)
        keep[chip] = scratch[mine, :].astype(BF16)
        send[chip] = scratch[other, :].astype(BF16)


def weight_final_kernel(members, own, came, *outs):
    wq_o, wk_o, wv_o, wo_o, one_o, two_o, router_o, table_o = outs
    total = total_of((own, came))
    part, cols = wq_o.shape
    wq_o[...] = total[0:part, 0:cols]
    wk_o[...] = total[0:part, cols : 2 * cols]
    wv_o[...] = total[0:part, 2 * cols : 3 * cols]
    wo_o[...] = total[0:part, 3 * cols : 4 * cols].T
    small = total[part:]
    heads, bucket_count = table_o.shape
    table_o[...] = small[TABLE_ROW : TABLE_ROW + heads, 0:bucket_count]
    per = one_o.shape[1]
    first = (lax.axis_index("dp") * members + lax.axis_index("tensor")) * per
    shape = (per, small.shape[1])
    pick = (
        lax.broadcasted_iota(jnp.int32, shape, 0) + first
        == lax.broadcasted_iota(jnp.int32, shape, 1)
    ).astype(F32)
    rows = dot_nt(small, pick, HIGHEST)
    one_o[...] = rows[0:1]
    two_o[...] = rows[1:2]
    router_o[...] = rows[2:TABLE_ROW]


def output_kernel(hidden, own, came, out):
    out[...] = (hidden[...] + own[...] + came[...].astype(F32)).astype(BF16)


def input_back_kernel(members, inputs, gain, grad_hidden, table, output, *rest):
    out, small_o = rest[members:]
    share = output.shape[0]
    x = inputs[share_of(lax.axis_index("tensor"), share), :].astype(F32)
    r = inverse_rms(x)
    total = total_of(rest[:members])
    small_o[...] = total[share:] + table[...]
    z = total[0:share] * gain[...]
    out[0:share, :] = (
        grad_hidden[...] + r * z - x * (r * r * r) * jnp.mean(z * x, axis=-1, keepdims=True)
    ).astype(BF16)
    out[share:, :] = output[...]


def run(kernel, outs, args, scratch=(), name=None, after=(), space=pltpu.VMEM, out=pltpu.VMEM):
    vmem = pl.BlockSpec(memory_space=pltpu.VMEM)
    anywhere = pl.BlockSpec(memory_space=pl.ANY)
    count, extra = len(args), len(after)
    held = [*args, *outs, *(x for x in scratch if x.memory_space == pltpu.VMEM)]
    size = sum(math.prod(x.shape) * jnp.dtype(x.dtype).itemsize for x in held)

    def body(*refs):
        kernel(*refs[:count], *refs[count + extra :])

    return pl.pallas_call(
        body,
        out_shape=[out(o.shape, o.dtype) for o in outs] if out else outs,
        in_specs=[pl.BlockSpec(memory_space=space)] * count + [anywhere] * extra,
        out_specs=[vmem] * len(outs),
        scratch_shapes=list(scratch),
        compiler_params=pltpu.CompilerParams(vmem_limit_bytes=size + size // 4 + 4 * 1024 * 1024),
        cost_estimate=pl.CostEstimate(
            flops=int(WEIGHTS.get(name, 0.2) * 1e9), bytes_accessed=0, transcendentals=0
        ),
        name=name,
    )(*args, *after)


def sds(shape, dtype):
    return jax.ShapeDtypeStruct(tuple(shape), dtype)


def swap(values, axis, k):
    size = lax.axis_size(axis)
    return lax.ppermute(values, axis, [(i, i ^ k) for i in range(size)])


def swap_chips(values, even, odd):
    size = lax.axis_size("dp")
    pairs = [(i, i ^ (odd if i % 2 else even)) for i in range(size)]
    return lax.ppermute(values, "dp", pairs)


def exchange(shares):
    members = len(shares)
    sent = [swap(s, "tensor", distance(i, members)) for i, s in enumerate(shares) if i > 0]
    return [shares[0]] + sent


def spread(share):
    return exchange([share] * lax.axis_size("tensor"))


def shards(
    inputs,
    segments,
    buckets,
    routes,
    capacity_slots,
    gain_attn,
    bias_table,
    query_weight,
    key_weight,
    value_weight,
    out_weight,
    gain_expert,
    router_weight,
    expert_up,
    expert_down,
    cotangent,
):
    length, width = inputs.shape
    members = lax.axis_size("tensor")
    dp = lax.axis_size("dp")
    share = length // members
    cols = query_weight.shape[1]
    heads = cols // HEAD_DIM
    hidden_units = expert_up.shape[2]
    bucket_count = bias_table.shape[0]
    part = width // dp
    split = dp == 8 and part % 16 == 0
    chips = dp // 2
    bind = functools.partial

    def shares_sds(dtype, own=None):
        return [sds((share, width), own or dtype)] + [
            sds((share, width), dtype) for _ in range(members - 1)
        ]

    gain_row = gain_attn.reshape(1, width)
    gain_two_row = gain_expert.reshape(1, width)
    bucket_row = buckets.reshape(1, -1)
    bucket_wide = jnp.pad(bucket_row, ((0, 0), (0, 1)), constant_values=-1)
    where_to = (routes * CAP + capacity_slots).reshape(1, length)
    router_t = router_weight.T
    query_t, key_t, value_t = query_weight.T, key_weight.T, value_weight.T

    attention_args = [
        inputs,
        gain_attn,
        query_t,
        key_t,
        value_t,
        bucket_row,
        bias_table.T,
        segments,
        out_weight,
    ]
    attention_args = [pltpu.with_memory_space_constraint(a, pltpu.HBM) for a in attention_args]
    outs = run(
        bind(attention_kernel, members),
        shares_sds(BF16, F32)
        + [sds((length, width), BF16)]
        + [sds((length, cols), BF16)] * 3
        + [sds((heads, length, length), F32), sds((length, cols), BF16)],
        attention_args,
        [pltpu.VMEM((length, width), F32), pltpu.VMEM((8, 2 * length), F32)]
        + [pltpu.VMEM(a.shape, a.dtype) for a in attention_args]
        + [pltpu.SemaphoreType.DMA((len(attention_args),))],
        name="attention",
        space=pltpu.HBM,
    )
    attended = exchange(outs[:members])
    normed, q, k, v, probs, mixed = outs[members:]

    hidden, normed_two = run(
        bind(hidden_kernel, members),
        [sds((share, width), F32), sds((share, width), BF16)],
        [gain_two_row] + attended,
        name="hidden",
    )
    up, down = run(
        fetch_kernel,
        [sds(expert_up.shape, BF16), sds(expert_down.shape, BF16)],
        [pltpu.with_memory_space_constraint(a, pltpu.HBM) for a in (expert_up, expert_down)],
        [pltpu.SemaphoreType.DMA((2,))],
        name="fetch",
        space=pltpu.HBM,
        after=[normed_two],
    )
    normed_two = spread(normed_two)

    slots = EXPERTS * CAP
    outs = run(
        bind(expert_kernel, members),
        shares_sds(BF16)
        + [sds((2 * share, width), BF16)] * 2
        + [sds((slots, width), BF16)]
        + [sds((slots, hidden_units), BF16)] * 2
        + [sds((slots, width), BF16), sds((EXPERTS, width), F32), sds((share, width), BF16)],
        [where_to, cotangent, router_t, up, down] + normed_two,
        [
            pltpu.VMEM((length, width), BF16),
            pltpu.VMEM((slots, width), BF16),
            pltpu.VMEM((slots, width), BF16),
            pltpu.VMEM((length, width), F32),
        ],
        name="expert",
    )
    back_rows = exchange(outs[:members])
    rows_kept, rows_sent = outs[members : members + 2]
    buffer, active, grad_before, grad_expert, grad_router, dy_share = outs[members + 2 :]

    def split_sds(rows, columns):
        return [sds((chips, rows, columns), BF16)] * 2

    def merge_sds(rows, columns):
        return [sds((2, rows, columns), F32), sds((2, rows, columns), BF16)]

    expert_grads = run(
        bind(expert_grad_kernel, split),
        (split_sds(part, 4 * hidden_units) if split else [sds((width, 4 * hidden_units), F32)])
        + [sds(rows_sent.shape, BF16)],
        [buffer, active, grad_before, grad_expert, rows_sent],
        [pltpu.VMEM((width, hidden_units), F32)],
        name="expert_grads",
    )

    rows_sent = expert_grads[-1]
    grad_hidden, grad_attended, grad_gain_expert = run(
        bind(hidden_back_kernel, members),
        [sds((share, width), F32), sds((share, width), BF16), sds((1, width), F32)],
        [hidden, dy_share, gain_two_row] + back_rows,
        name="hidden_back",
        after=expert_grads[-1:],
    )
    grad_attended = spread(grad_attended)

    expert_merged = []
    if split:
        expert_merged = run(
            merge_kernel,
            merge_sds(part, 4 * hidden_units),
            [expert_grads[0], swap(expert_grads[1], "dp", 1)],
            name="expert_merge",
        )
    own_rows, other_rows = run(
        pair_sum_kernel,
        [sds((share, width), F32), sds((share, width), BF16)],
        [rows_kept, swap(rows_sent, "tensor", 1)],
        name="pair_sum",
        after=grad_attended[1:] + list(expert_merged[:1]),
    )
    crossed = []

    def tall_sds(dtype):
        return sds((share + GAIN_ROWS, width), dtype)

    outs = run(
        bind(attention_back_kernel, members),
        [tall_sds(F32)]
        + [tall_sds(BF16)] * (members - 1)
        + [
            sds((3, length, cols), BF16),
            sds((length, width), BF16),
            sds((heads, length, length), BF16),
        ],
        [inputs, probs, q, k, v, query_t, key_t, value_t, out_weight]
        + [grad_gain_expert, grad_router]
        + grad_attended,
        [pltpu.VMEM((length, width), F32)],
        name="attention_back",
        after=[own_rows, *expert_merged[:1]],
    )
    grad_normed = exchange(outs[:members])
    projections, attended_low, grad_scores = outs[members:]

    (output_share,) = run(
        output_kernel,
        [sds((share, width), BF16)],
        [hidden, own_rows, swap(other_rows, "tensor", 2)],
        name="output_share",
    )
    weight_cols = 4 * cols
    weight_grads = run(
        bind(weight_grad_kernel, split),
        (split_sds(part, weight_cols) if split else [sds((width, weight_cols), F32)])
        + [sds((8, width), F32)],
        [normed, projections, attended_low, mixed, grad_scores, bucket_wide],
        [pltpu.VMEM((width, weight_cols), F32)],
        name="weight_grads",
        after=[output_share],
    )

    if split:
        expert_own, expert_sent = run(
            expert_cross_kernel,
            [sds((part, 4 * hidden_units), F32), sds((part, 4 * hidden_units), BF16)],
            [expert_merged[0], swap_chips(expert_merged[1], 2, 4)],
            name="expert_cross",
            after=weight_grads[-1:],
        )
        crossing, weight_kept = run(
            cross_kernel,
            [
                sds((part + part // 2, 4 * hidden_units), BF16),
                sds((2, part, weight_cols), F32),
            ],
            [expert_sent, weight_grads[0], swap(weight_grads[1], "dp", 1)],
            name="cross",
        )
        crossed = [weight_kept]
    both_rows, small = run(
        bind(input_back_kernel, members),
        [sds((2 * share, width), BF16), sds((8, width), F32)],
        [inputs, gain_row, grad_hidden, weight_grads[-1]]
        + [output_share]
        + grad_normed,
        name="input_back",
        after=crossed,
    )
    row_parts = spread(both_rows)
    if split:
        (small,) = run(
            add_kernel,
            [sds(small.shape, F32)],
            [small, swap(small, "dp", 1)],
            name="small_sum",
        )
    if split:
        crossing = swap_chips(crossing, 4, 2)
        grad_expert_up, grad_expert_down = run(
            expert_final_kernel,
            [sds((EXPERTS, part, hidden_units), F32), sds((EXPERTS, part, hidden_units), F32)],
            [expert_own, crossing],
            name="expert_final", out=None,
        )
        grad_expert_down = grad_expert_down.transpose(0, 2, 1)
        weight_own, weight_sent = run(
            weight_cross_kernel,
            [
                sds((part + SMALL_ROWS, weight_cols), F32),
                sds((part + SMALL_ROWS, weight_cols), BF16),
            ],
            [weight_kept, crossing, small, swap_chips(small, 4, 2)],
            name="weight_cross",
        )
        per = part // members
        (
            grad_query_weight,
            grad_key_weight,
            grad_value_weight,
            grad_out_weight,
            grad_gain_attn,
            grad_gain_expert,
            grad_router,
            grad_table,
        ) = run(
            bind(weight_final_kernel, members),
            [sds((part, cols), F32)] * 3
            + [sds((cols, part), F32), sds((1, per), F32), sds((1, per), F32)]
            + [sds((EXPERTS, per), F32), sds((heads, bucket_count), F32)],
            [weight_own, swap_chips(weight_sent, 2, 4)],
            name="weight_final",
            out=None,
        )
        grad_table = grad_table.T
        grad_router = grad_router.T
        grad_gain_attn = grad_gain_attn.reshape(per)
        grad_gain_expert = grad_gain_expert.reshape(per)
        done = [grad_expert_up]
    else:

        def scatter(values, axes, dimension):
            return lax.psum_scatter(values, axes, scatter_dimension=dimension, tiled=True)

        def pick(values):
            at = lax.axis_index("tensor") * (part // members)
            return lax.dynamic_slice_in_dim(scatter(values, "dp", 0), at, part // members)

        grads = expert_grads[0].reshape(width, EXPERTS, 2, hidden_units)
        grad_expert_up = scatter(grads[:, :, 0].transpose(1, 0, 2), "dp", 1)
        grad_expert_down = scatter(grads[:, :, 1].transpose(1, 2, 0), "dp", 2)
        grads = weight_grads[0]
        grad_query_weight = scatter(grads[:, 0:cols], "dp", 0)
        grad_key_weight = scatter(grads[:, cols : 2 * cols], "dp", 0)
        grad_value_weight = scatter(grads[:, 2 * cols : 3 * cols], "dp", 0)
        grad_out_weight = scatter(grads[:, 3 * cols :].T, "dp", 1)
        grad_table = lax.psum(small[TABLE_ROW : TABLE_ROW + heads, :bucket_count].T, "dp")
        grad_gain_attn = pick(small[0])
        grad_gain_expert = pick(small[1])
        grad_router = pick(small[2:TABLE_ROW].T)
        done = []
    output, grad_inputs = run(
        rows_kernel,
        [sds((length, width), BF16), sds((length, width), BF16)],
        row_parts,
        name="rows",
        out=None,
        after=done,
    )
    return (
        output,
        grad_inputs,
        grad_gain_attn,
        grad_table,
        grad_query_weight,
        grad_key_weight,
        grad_value_weight,
        grad_out_weight,
        grad_gain_expert,
        grad_router,
        grad_expert_up,
        grad_expert_down,
    )


def solution(mesh):
    return jax.shard_map(
        shards,
        mesh=mesh,
        in_specs=(
            P("dp", None),
            P("dp", None),
            P(),
            P("dp"),
            P("dp"),
            P(),
            P(None, "tensor"),
            P(None, "tensor"),
            P(None, "tensor"),
            P(None, "tensor"),
            P("tensor", None),
            P(),
            P(),
            P(None, None, "tensor"),
            P(None, "tensor", None),
            P("dp", None),
        ),
        out_specs=(
            P("dp", None),
            P("dp", None),
            P(("dp", "tensor")),
            P(None, "tensor"),
            P("dp", "tensor"),
            P("dp", "tensor"),
            P("dp", "tensor"),
            P("tensor", "dp"),
            P(("dp", "tensor")),
            P(("dp", "tensor"), None),
            P(None, "dp", "tensor"),
            P(None, "tensor", "dp"),
        ),
        check_vma=False,
    )
```

```python
import functools
import math

import jax
import jax.numpy as jnp
from jax import lax
from jax.experimental import pallas as pl
from jax.experimental.pallas import tpu as pltpu
from jax.sharding import PartitionSpec as P

HEAD_DIM = 64
EXPERTS = 2
CAP = 144
EPS = 1e-06
SMALL_ROWS = 16
GAIN_ROWS = 8
TABLE_ROW = 2 + EXPERTS
WEIGHTS = {
    "fetch": 20,
    "expert": 5,
    "expert_grads": 20,
    "hidden_back": 60,
    "expert_merge": 20,
    "attention_back": 5,
    "pair_sum": 8,
    "weight_grads": 4,
    "expert_cross": 8,
    "input_back": 60,
    "expert_final": 0.001,
    "finish": 0.001,
    "small_sum": 0.001,
    "weight_cross": 0.001,
}
BF16 = jnp.bfloat16
F32 = jnp.float32
HIGHEST = lax.Precision.HIGHEST
NT = (((1,), (1,)), ((), ()))
TN = (((0,), (0,)), ((), ()))
GELU_C = 0.7978845608028654
GELU_A = 0.044715


def dot(a, b):
    return jnp.dot(a, b, preferred_element_type=F32)


def dot_nt(a, b, precision=None):
    return lax.dot_general(a, b, NT, preferred_element_type=F32, precision=precision)


def dot_tn(a, b):
    return lax.dot_general(a, b, TN, preferred_element_type=F32)


def inverse_rms(values):
    return lax.rsqrt(jnp.mean(values * values, axis=-1, keepdims=True) + EPS)


def share_of(index, rows):
    return pl.ds(pl.multiple_of(index * rows, rows), rows)


def distance(place, members):
    return (members - place) % members


def member_at(place, members):
    return jnp.bitwise_xor(lax.axis_index("tensor"), distance(place, members))


def put_shares(acc_ref, share_refs):
    for i, ref in enumerate(share_refs):
        there = share_of(member_at(i, len(share_refs)), ref.shape[0])
        ref[...] = acc_ref[there, :].astype(ref.dtype)


def assemble(full_ref, share_refs):
    for i, ref in enumerate(share_refs):
        full_ref[share_of(member_at(i, len(share_refs)), ref.shape[0]), :] = ref[...]


def total_of(refs):
    total = refs[0][...].astype(F32)
    for ref in refs[1:]:
        total = total + ref[...].astype(F32)
    return total


def column_of(row, length):
    eye = lax.broadcasted_iota(jnp.int32, (length, length), 0) == lax.broadcasted_iota(
        jnp.int32, (length, length), 1
    )
    return jnp.sum(jnp.where(eye, row, jnp.zeros_like(row)), axis=1, keepdims=True)


def head_mask(head, width):
    lane = lax.broadcasted_iota(jnp.int32, (1, width), 1)
    return (lane >= head * HEAD_DIM) & (lane < (head + 1) * HEAD_DIM)


def masked(values, head):
    return jnp.where(head_mask(head, values.shape[1]), values, jnp.zeros_like(values))


def bucket_hot_of(buckets_ref, bucket_count):
    offsets = buckets_ref.shape[1]
    return (
        lax.broadcasted_iota(jnp.int32, (bucket_count, offsets), 0) == buckets_ref[...]
    ).astype(F32)


def attention_kernel(members, *refs):
    sources, outs = refs[:9], refs[9 : members + 15]
    normed_o, q_o, k_o, v_o, probs_o, mixed_o = outs[members:]
    acc, offset_rows = refs[members + 15 : members + 17]
    local, sems = refs[members + 17 : members + 26], refs[members + 26]
    copies = [
        pltpu.make_async_copy(source, held, sems.at[i])
        for i, (source, held) in enumerate(zip(sources, local))
    ]
    for copy in copies:
        copy.start()
    buckets, table, segment, inputs, gain, wq, wk, wv, wo = local
    length = inputs.shape[0]
    heads = wq.shape[0] // HEAD_DIM
    for copy in copies[:3]:
        copy.wait()
    hot = bucket_hot_of(buckets, table.shape[1])
    seg_row = segment[...].astype(F32)
    same = column_of(seg_row, length) == seg_row
    offset_rows[...] = jnp.zeros_like(offset_rows)
    offset_rows[0:heads, 0 : hot.shape[1]] = jnp.dot(
        table[...], hot, preferred_element_type=F32, precision=HIGHEST
    )
    for h in range(heads):
        spread = jnp.broadcast_to(offset_rows[h : h + 1, :], (length, 2 * length))
        bias = pltpu.roll(spread, length + 1, 1, stride=1, stride_axis=0)[:, :length]
        probs_o[h] = jnp.where(same, bias, -1e30)
    copies[3].wait()
    x = inputs[...].astype(F32)
    scaled = x * inverse_rms(x)
    for copy in copies[4:8]:
        copy.wait()
    normed = (scaled * gain[...].reshape(1, -1)).astype(BF16)
    normed_o[...] = normed
    q = dot_nt(normed, wq[...]).astype(BF16)
    k = dot_nt(normed, wk[...]).astype(BF16)
    v = dot_nt(normed, wv[...]).astype(BF16)
    q_o[...] = q
    k_o[...] = k
    v_o[...] = v
    mixed = jnp.zeros((length, wq.shape[0]), F32)
    for h in range(heads):
        scores = dot_nt(masked(q, h), k) + probs_o[h]
        shifted = jnp.exp(scores - jnp.max(scores, axis=-1, keepdims=True))
        probs = shifted / jnp.sum(shifted, axis=-1, keepdims=True)
        probs_o[h] = probs
        mixed = mixed + dot(probs.astype(BF16), masked(v, h))
    mixed = mixed.astype(BF16)
    mixed_o[...] = mixed
    copies[8].wait()
    acc[...] = dot(mixed, wo[...])
    put_shares(acc, outs[:members])
    own = share_of(lax.axis_index("tensor"), outs[0].shape[0])
    outs[0][...] += inputs[own, :].astype(F32)


def hidden_kernel(members, gain, *rest):
    hidden_o, normed_o = rest[members:]
    hidden = total_of(rest[:members])
    hidden_o[...] = hidden
    normed_o[...] = (hidden * inverse_rms(hidden) * gain[...]).astype(BF16)


def place_of(where_to):
    slots = lax.broadcasted_iota(jnp.int32, (EXPERTS * CAP, where_to.shape[1]), 0)
    return (slots == where_to[...]).astype(BF16)


def fetch_kernel(up, down, up_o, down_o, sems):
    copies = [
        pltpu.make_async_copy(up, up_o, sems.at[0]),
        pltpu.make_async_copy(down, down_o, sems.at[1]),
    ]
    for copy in copies:
        copy.start()
    for copy in copies:
        copy.wait()


def expert_kernel(members, where_to, cotangent, router_t, up, down, *rest):
    pieces = rest[:members]
    rest = rest[members:]
    back_o, rows = rest[:members], rest[members]
    buffer_o, active_o, grad_before_o, grad_expert_o, router_o, dy_o = rest[
        members + 1 : members + 7
    ]
    normed, backs, acc = rest[members + 7 :]
    length = cotangent.shape[0]
    assemble(normed, pieces)
    dy_o[...] = cotangent[share_of(lax.axis_index("tensor"), dy_o.shape[0]), :]
    place = place_of(where_to)
    buffer = dot(place, normed[...]).astype(BF16)
    buffer_o[...] = buffer
    dy_buffer = dot(place, cotangent[...])
    router_rows = router_t[...].astype(F32)
    router_grad = [jnp.zeros((1, buffer.shape[1]), F32) for _ in range(EXPERTS)]
    for e in range(EXPERTS):
        slot = slice(e * CAP, (e + 1) * CAP)
        rows_in = buffer[slot]
        logits = dot_nt(rows_in, router_t[...])
        shifted = jnp.exp(logits - jnp.max(logits, axis=-1, keepdims=True))
        router_probs = shifted / jnp.sum(shifted, axis=-1, keepdims=True)
        gate = router_probs[:, e : e + 1]
        dy = dy_buffer[slot]
        grad_expert = (dy * gate).astype(BF16)
        grad_expert_o[slot, :] = grad_expert
        before = dot(rows_in, up[e])
        inner = jnp.tanh(GELU_C * (before + GELU_A * before * before * before))
        active = (0.5 * before * (1.0 + inner)).astype(BF16)
        active_o[slot, :] = active
        slope = 0.5 * (1.0 + inner) + 0.5 * before * (1.0 - inner * inner) * GELU_C * (
            1.0 + 3.0 * GELU_A * before * before
        )
        result = dot(active, down[e])
        grad_before = (dot_nt(grad_expert, down[e]) * slope).astype(BF16)
        grad_before_o[slot, :] = grad_before
        rows[slot, :] = (result * gate).astype(BF16)
        scaled = jnp.sum(dy * result, axis=-1, keepdims=True) * gate
        back = dot_nt(grad_before, up[e])
        for other in range(EXPERTS):
            own = 1.0 if other == e else 0.0
            grad_logit = scaled * (own - router_probs[:, other : other + 1])
            router_grad[other] = router_grad[other] + jnp.sum(
                grad_logit * rows_in.astype(F32), axis=0, keepdims=True
            )
            back = back + grad_logit * router_rows[other : other + 1, :]
        backs[slot, :] = back.astype(BF16)
    for other in range(EXPERTS):
        router_o[other : other + 1, :] = router_grad[other]
    acc[...] = dot_tn(place, backs[...])
    put_shares(acc, back_o)


def split_rows(keep, send, chip, part):
    core = lax.rem(lax.axis_index("dp"), 2)
    return share_of(2 * chip + core, part), share_of(2 * chip + 1 - core, part)


def expert_grad_kernel(split, where_to, buffer, active, grad_before, grad_expert, rows, *rest):
    row_o, scratch, acc = rest[-4:-2], rest[-2], rest[-1]
    place = place_of(where_to)
    acc[...] = dot_tn(place, rows[...])
    me = lax.axis_index("tensor")
    share = row_o[0].shape[0] // 2
    for first, ref in enumerate(row_o):
        for k in range(2):
            index = jnp.bitwise_xor(me, first + 2 * k)
            ref[k * share : (k + 1) * share, :] = acc[share_of(index, share), :].astype(BF16)
    for e in range(EXPERTS):
        slot = slice(e * CAP, (e + 1) * CAP)
        for which in range(2):
            if which == 0:
                product = dot_tn(buffer[slot, :], grad_before[slot, :])
            else:
                product = dot_tn(grad_expert[slot, :], active[slot, :])
            hidden_units = active.shape[1]
            first = (2 * e + which) * hidden_units
            if not split:
                rest[0][:, first : first + hidden_units] = product
                continue
            keep, send = rest[0], rest[1]
            part = keep.shape[1]
            scratch[...] = product
            for chip in range(keep.shape[0]):
                mine, other = split_rows(keep, send, chip, part)
                keep[chip, :, first : first + hidden_units] = scratch[mine, :].astype(BF16)
                send[chip, :, first : first + hidden_units] = scratch[other, :].astype(BF16)


def chip_bits():
    core = lax.rem(lax.axis_index("dp"), 2)
    return 1 + core, 2 - core


def merge_kernel(kept, came, keep, send):
    chip = lax.div(lax.axis_index("dp"), 2)
    first, second = chip_bits()
    for ref, start in ((keep, chip), (send, jnp.bitwise_xor(chip, first))):
        for k, there in enumerate((start, jnp.bitwise_xor(start, second))):
            total = kept[there].astype(F32) + came[there].astype(F32)
            ref[k] = total.astype(ref.dtype)


def add_kernel(one, other, out):
    out[...] = one[...] + other[...]


def expert_cross_kernel(kept, came, own, send):
    own[...] = kept[0] + came[0].astype(F32)
    send[...] = (kept[1] + came[1].astype(F32)).astype(BF16)


def cross_kernel(expert_send, weight_kept, weight_came, send, weight_keep):
    rows = expert_send.shape[0]
    send[0:rows, :] = expert_send[...]
    chip = lax.div(lax.axis_index("dp"), 2)
    second, first = chip_bits()
    width = weight_keep.shape[2]
    half = rows // 2
    for k in range(2):
        mine = jnp.bitwise_xor(chip, k * second)
        weight_keep[k] = weight_kept[mine].astype(F32) + weight_came[mine].astype(F32)
        there = jnp.bitwise_xor(mine, first)
        total = (weight_kept[there].astype(F32) + weight_came[there].astype(F32)).astype(BF16)
        for i in range(2):
            at = (2 * k + i) * width
            send[rows : rows + half, at : at + width] = total[i * half : (i + 1) * half]


def weight_cross_kernel(kept, came, small, small_came, own, send):
    width = own.shape[1]
    rows = kept.shape[1]
    half = rows // 2
    total = jnp.concatenate([small[...] + small_came[...], jnp.zeros_like(small)], axis=0)
    for k, ref in enumerate((own, send)):
        for i in range(2):
            at = (2 * k + i) * width
            arrived = came[rows : rows + half, at : at + width].astype(F32)
            part = slice(i * half, (i + 1) * half)
            ref[part, :] = (kept[k, part, :] + arrived).astype(ref.dtype)
        ref[rows:, :] = total.astype(ref.dtype)


def expert_final_kernel(*refs):
    up_o, down_o = refs[2:]
    total = refs[0][...] + refs[1][0 : refs[0].shape[0], :].astype(F32)
    for e in range(EXPERTS):
        width = up_o.shape[2]
        first = 2 * e * width
        up_o[e] = total[:, first : first + width]
        down_o[e] = total[:, first + width : first + 2 * width]


def pair_sum_kernel(kept, came, own, other):
    share = own.shape[0]
    own[...] = kept[0:share, :].astype(F32) + came[0:share, :].astype(F32)
    other[...] = (kept[share:, :].astype(F32) + came[share:, :].astype(F32)).astype(BF16)


def pair_kernel(own, came, out):
    share = own.shape[0]
    out[0:share, :] = own[...]
    out[share:, :] = came[...]


def rows_kernel(*refs):
    shares, pairs, (output, grad_inputs) = refs[:-4], refs[-4:-2], refs[-2:]
    assemble(grad_inputs, shares)
    me = lax.axis_index("tensor")
    rows = output.shape[0] // len(shares)
    for near, ref in enumerate(pairs):
        for k in range(2):
            there = jnp.bitwise_xor(me, near + 2 * k)
            output[share_of(there, rows), :] = ref[k * rows : (k + 1) * rows, :]


def hidden_back_kernel(members, hidden, cotangent, gain, *rest):
    parts = rest[:members]
    grad_o, low_o, gain_o = rest[members:]
    h = hidden[...]
    dy = cotangent[...].astype(F32)
    r = inverse_rms(h)
    grad_normed = total_of(parts)
    z = grad_normed * gain[...]
    gain_o[...] = jnp.sum(grad_normed * h * r, axis=0, keepdims=True)
    grad = dy + r * z - h * (r * r * r) * jnp.mean(z * h, axis=-1, keepdims=True)
    grad_o[...] = grad
    low_o[...] = grad.astype(BF16)


def attention_back_kernel(
    members, inputs, probs, q, k, v, wq, wk, wv, wo, gain_two, router, *rest
):
    pieces = rest[:members]
    rest = rest[members:]
    share_o = rest[:members]
    grads_o, attended_o, scores_o = rest[members : members + 3]
    acc = rest[members + 3]
    assemble(attended_o, pieces)
    heads = wq.shape[0] // HEAD_DIM
    grad_mixed = dot_nt(attended_o[...], wo[...]).astype(BF16)
    qv, kv, vv = q[...], k[...], v[...]
    dq = jnp.zeros(qv.shape, F32)
    dk = jnp.zeros(qv.shape, F32)
    dv = jnp.zeros(qv.shape, F32)
    for h in range(heads):
        grad_mixed_h = masked(grad_mixed, h)
        p = probs[h]
        grad_probs = dot_nt(grad_mixed_h, vv)
        inner = jnp.sum(p * grad_probs, axis=-1, keepdims=True)
        grad_scores = (p * (grad_probs - inner)).astype(BF16)
        scores_o[h] = grad_scores
        dq = dq + dot(grad_scores, masked(kv, h))
        dk = dk + dot_tn(grad_scores, masked(qv, h))
        dv = dv + dot_tn(p.astype(BF16), grad_mixed_h)
    dq, dk, dv = dq.astype(BF16), dk.astype(BF16), dv.astype(BF16)
    grads_o[0] = dq
    grads_o[1] = dk
    grads_o[2] = dv
    total = dot(dq, wq[...]) + dot(dk, wk[...]) + dot(dv, wv[...])
    acc[...] = total
    x = inputs[...].astype(F32)
    gain_one = jnp.sum(total * x * inverse_rms(x), axis=0, keepdims=True)
    small = jnp.concatenate(
        [
            gain_one,
            gain_two[...],
            router[...],
            jnp.zeros((GAIN_ROWS - TABLE_ROW, gain_one.shape[1]), F32),
        ],
        axis=0,
    )
    for i, ref in enumerate(share_o):
        share = ref.shape[0] - GAIN_ROWS
        ref[0:share, :] = acc[share_of(member_at(i, members), share), :].astype(ref.dtype)
        ref[share:, :] = small.astype(ref.dtype)


def weight_grad_kernel(
    split, normed, grads, attended, mixed, scores, buckets, *rest
):
    bucket_count = 32
    small, scratch = rest[-2:]
    length = normed.shape[0]
    cols = grads.shape[2]
    normed_v = normed[...]
    for i in range(4):
        if i < 3:
            product = dot_tn(normed_v, grads[i])
        else:
            product = dot_tn(attended[...], mixed[...])
        scratch[:, i * cols : (i + 1) * cols] = product
    small[...] = jnp.zeros_like(small)
    flip = (
        lax.broadcasted_iota(jnp.int32, (length, length), 0)
        + lax.broadcasted_iota(jnp.int32, (length, length), 1)
        == length - 1
    ).astype(BF16)
    hot = (
        lax.broadcasted_iota(jnp.int32, (bucket_count, 2 * length), 0) == buckets[...]
    ).astype(F32)
    for h in range(scores.shape[0]):
        flipped = dot(flip, scores[h])
        wide = jnp.concatenate([flipped, jnp.zeros_like(flipped)], axis=1)
        sheared = pltpu.roll(wide, 0, 1, stride=1, stride_axis=0)
        offsets = jnp.sum(sheared, axis=0, keepdims=True)
        small[TABLE_ROW + h : TABLE_ROW + h + 1, 0:bucket_count] = dot_nt(
            jnp.broadcast_to(offsets, (8, 2 * length)), hot, HIGHEST
        )[0:1]
    if not split:
        rest[0][...] = scratch[...]
        return
    keep, send = rest[0], rest[1]
    chips, part, _ = keep.shape
    for chip in range(chips):
        mine, other = split_rows(keep, send, chip, part)
        keep[chip] = scratch[mine, :].astype(BF16)
        send[chip] = scratch[other, :].astype(BF16)


def weight_final_kernel(members, own, came, *outs):
    wq_o, wk_o, wv_o, wo_o, one_o, two_o, router_o, table_o = outs
    total = total_of((own, came))
    part, cols = wq_o.shape
    wq_o[...] = total[0:part, 0:cols]
    wk_o[...] = total[0:part, cols : 2 * cols]
    wv_o[...] = total[0:part, 2 * cols : 3 * cols]
    wo_o[...] = total[0:part, 3 * cols : 4 * cols].T
    small = total[part:]
    heads, bucket_count = table_o.shape
    table_o[...] = small[TABLE_ROW : TABLE_ROW + heads, 0:bucket_count]
    per = one_o.shape[1]
    first = (lax.axis_index("dp") * members + lax.axis_index("tensor")) * per
    shape = (per, small.shape[1])
    pick = (
        lax.broadcasted_iota(jnp.int32, shape, 0) + first
        == lax.broadcasted_iota(jnp.int32, shape, 1)
    ).astype(F32)
    rows = dot_nt(small, pick, HIGHEST)
    one_o[...] = rows[0:1]
    two_o[...] = rows[1:2]
    router_o[...] = rows[2:TABLE_ROW]


def output_kernel(hidden, own, came, out):
    out[...] = (hidden[...] + own[...] + came[...].astype(F32)).astype(BF16)


def finish_kernel(members, *refs):
    weight_in, row_in, outs = refs[:2], refs[2 : members + 4], refs[members + 4 :]
    weight_final_kernel(members, *weight_in, *outs[2:])
    rows_kernel(*row_in, *outs[:2])


def input_back_kernel(members, inputs, gain, grad_hidden, table, *rest):
    out, small_o = rest[members:]
    share = out.shape[0]
    x = inputs[share_of(lax.axis_index("tensor"), share), :].astype(F32)
    r = inverse_rms(x)
    total = total_of(rest[:members])
    small_o[...] = total[share:] + table[...]
    z = total[0:share] * gain[...]
    out[...] = (
        grad_hidden[...] + r * z - x * (r * r * r) * jnp.mean(z * x, axis=-1, keepdims=True)
    ).astype(BF16)


def run(kernel, outs, args, scratch=(), name=None, after=(), space=pltpu.VMEM, out=pltpu.VMEM):
    vmem = pl.BlockSpec(memory_space=pltpu.VMEM)
    anywhere = pl.BlockSpec(memory_space=pl.ANY)
    count, extra = len(args), len(after)
    held = [*args, *outs, *(x for x in scratch if x.memory_space == pltpu.VMEM)]
    size = sum(math.prod(x.shape) * jnp.dtype(x.dtype).itemsize for x in held)

    def body(*refs):
        kernel(*refs[:count], *refs[count + extra :])

    return pl.pallas_call(
        body,
        out_shape=[out(o.shape, o.dtype) for o in outs] if out else outs,
        in_specs=[pl.BlockSpec(memory_space=space)] * count + [anywhere] * extra,
        out_specs=[vmem] * len(outs),
        scratch_shapes=list(scratch),
        compiler_params=pltpu.CompilerParams(vmem_limit_bytes=size + size // 4 + 4 * 1024 * 1024),
        cost_estimate=pl.CostEstimate(
            flops=int(WEIGHTS.get(name, 0.2) * 1e9), bytes_accessed=0, transcendentals=0
        ),
        name=name,
    )(*args, *after)


def sds(shape, dtype):
    return jax.ShapeDtypeStruct(tuple(shape), dtype)


def swap(values, axis, k):
    size = lax.axis_size(axis)
    return lax.ppermute(values, axis, [(i, i ^ k) for i in range(size)])


def swap_chips(values, even, odd):
    size = lax.axis_size("dp")
    pairs = [(i, i ^ (odd if i % 2 else even)) for i in range(size)]
    return lax.ppermute(values, "dp", pairs)


def exchange(shares):
    members = len(shares)
    sent = [swap(s, "tensor", distance(i, members)) for i, s in enumerate(shares) if i > 0]
    return [shares[0]] + sent


def spread(share):
    return exchange([share] * lax.axis_size("tensor"))


def shards(
    inputs,
    segments,
    buckets,
    routes,
    capacity_slots,
    gain_attn,
    bias_table,
    query_weight,
    key_weight,
    value_weight,
    out_weight,
    gain_expert,
    router_weight,
    expert_up,
    expert_down,
    cotangent,
):
    length, width = inputs.shape
    members = lax.axis_size("tensor")
    dp = lax.axis_size("dp")
    share = length // members
    cols = query_weight.shape[1]
    heads = cols // HEAD_DIM
    hidden_units = expert_up.shape[2]
    bucket_count = bias_table.shape[0]
    part = width // dp
    split = dp == 8 and part % 16 == 0
    chips = dp // 2
    bind = functools.partial

    def shares_sds(dtype, own=None):
        return [sds((share, width), own or dtype)] + [
            sds((share, width), dtype) for _ in range(members - 1)
        ]

    gain_row = gain_attn.reshape(1, width)
    gain_two_row = gain_expert.reshape(1, width)
    bucket_row = buckets.reshape(1, -1)
    bucket_wide = jnp.pad(bucket_row, ((0, 0), (0, 1)), constant_values=-1)
    where_to = (routes * CAP + capacity_slots).reshape(1, length)
    router_t = router_weight.T
    query_t, key_t, value_t = query_weight.T, key_weight.T, value_weight.T

    attention_args = [
        bucket_row,
        bias_table.T,
        segments,
        inputs,
        gain_attn,
        query_t,
        key_t,
        value_t,
        out_weight,
    ]
    attention_args = [pltpu.with_memory_space_constraint(a, pltpu.HBM) for a in attention_args]
    outs = run(
        bind(attention_kernel, members),
        shares_sds(BF16, F32)
        + [sds((length, width), BF16)]
        + [sds((length, cols), BF16)] * 3
        + [sds((heads, length, length), F32), sds((length, cols), BF16)],
        attention_args,
        [pltpu.VMEM((length, width), F32), pltpu.VMEM((8, 2 * length), F32)]
        + [pltpu.VMEM(a.shape, a.dtype) for a in attention_args]
        + [pltpu.SemaphoreType.DMA((len(attention_args),))],
        name="attention",
        space=pltpu.HBM,
    )
    attended = exchange(outs[:members])
    normed, q, k, v, probs, mixed = outs[members:]

    hidden, normed_two = run(
        bind(hidden_kernel, members),
        [sds((share, width), F32), sds((share, width), BF16)],
        [gain_two_row] + attended,
        name="hidden",
    )
    up, down = run(
        fetch_kernel,
        [sds(expert_up.shape, BF16), sds(expert_down.shape, BF16)],
        [pltpu.with_memory_space_constraint(a, pltpu.HBM) for a in (expert_up, expert_down)],
        [pltpu.SemaphoreType.DMA((2,))],
        name="fetch",
        space=pltpu.HBM,
        after=[normed_two],
    )
    normed_two = spread(normed_two)

    slots = EXPERTS * CAP
    outs = run(
        bind(expert_kernel, members),
        shares_sds(BF16)
        + [sds((slots, width), BF16)] * 2
        + [sds((slots, hidden_units), BF16)] * 2
        + [sds((slots, width), BF16), sds((EXPERTS, width), F32), sds((share, width), BF16)],
        [where_to, cotangent, router_t, up, down] + normed_two,
        [
            pltpu.VMEM((length, width), BF16),
            pltpu.VMEM((slots, width), BF16),
            pltpu.VMEM((length, width), F32),
        ],
        name="expert",
    )
    back_rows = exchange(outs[:members])
    slot_rows, buffer, active, grad_before, grad_expert, grad_router, dy_share = outs[members:]

    def split_sds(rows, columns):
        return [sds((chips, rows, columns), BF16)] * 2

    def merge_sds(rows, columns):
        return [sds((2, rows, columns), F32), sds((2, rows, columns), BF16)]

    expert_grads = run(
        bind(expert_grad_kernel, split),
        (split_sds(part, 4 * hidden_units) if split else [sds((width, 4 * hidden_units), F32)])
        + [sds((2 * share, width), BF16)] * 2,
        [where_to, buffer, active, grad_before, grad_expert, slot_rows],
        [pltpu.VMEM((width, hidden_units), F32), pltpu.VMEM((length, width), F32)],
        name="expert_grads",
    )

    rows_kept, rows_sent = expert_grads[-2:]
    grad_hidden, grad_attended, grad_gain_expert = run(
        bind(hidden_back_kernel, members),
        [sds((share, width), F32), sds((share, width), BF16), sds((1, width), F32)],
        [hidden, dy_share, gain_two_row] + back_rows,
        name="hidden_back",
        after=expert_grads[-1:],
    )
    grad_attended = spread(grad_attended)

    expert_merged = []
    if split:
        expert_merged = run(
            merge_kernel,
            merge_sds(part, 4 * hidden_units),
            [expert_grads[0], swap(expert_grads[1], "dp", 1)],
            name="expert_merge",
        )
    own_rows, other_rows = run(
        pair_sum_kernel,
        [sds((share, width), F32), sds((share, width), BF16)],
        [rows_kept, swap(rows_sent, "tensor", 1)],
        name="pair_sum",
        after=grad_attended[1:] + list(expert_merged[:1]),
    )
    crossed = []

    def tall_sds(dtype):
        return sds((share + GAIN_ROWS, width), dtype)

    outs = run(
        bind(attention_back_kernel, members),
        [tall_sds(F32)]
        + [tall_sds(BF16)] * (members - 1)
        + [
            sds((3, length, cols), BF16),
            sds((length, width), BF16),
            sds((heads, length, length), BF16),
        ],
        [inputs, probs, q, k, v, query_t, key_t, value_t, out_weight]
        + [grad_gain_expert, grad_router]
        + grad_attended,
        [pltpu.VMEM((length, width), F32)],
        name="attention_back",
        after=[own_rows, *expert_merged[:1]],
    )
    grad_normed = exchange(outs[:members])
    projections, attended_low, grad_scores = outs[members:]

    (output_share,) = run(
        output_kernel,
        [sds((share, width), BF16)],
        [hidden, own_rows, swap(other_rows, "tensor", 2)],
        name="output_share",
    )
    weight_cols = 4 * cols
    weight_grads = run(
        bind(weight_grad_kernel, split),
        (split_sds(part, weight_cols) if split else [sds((width, weight_cols), F32)])
        + [sds((8, width), F32)],
        [normed, projections, attended_low, mixed, grad_scores, bucket_wide],
        [pltpu.VMEM((width, weight_cols), F32)],
        name="weight_grads",
        after=[output_share],
    )

    if split:
        expert_own, expert_sent = run(
            expert_cross_kernel,
            [sds((part, 4 * hidden_units), F32), sds((part, 4 * hidden_units), BF16)],
            [expert_merged[0], swap_chips(expert_merged[1], 2, 4)],
            name="expert_cross",
            after=weight_grads[-1:],
        )
        crossing, weight_kept = run(
            cross_kernel,
            [
                sds((part + part // 2, 4 * hidden_units), BF16),
                sds((2, part, weight_cols), F32),
            ],
            [expert_sent, weight_grads[0], swap(weight_grads[1], "dp", 1)],
            name="cross",
        )
        crossed = [weight_kept]
    grad_share, small = run(
        bind(input_back_kernel, members),
        [sds((share, width), BF16), sds((8, width), F32)],
        [inputs, gain_row, grad_hidden, weight_grads[-1]]
        + grad_normed,
        name="input_back",
        after=crossed,
    )
    row_parts = spread(grad_share)
    (output_pair,) = run(
        pair_kernel,
        [sds((2 * share, width), BF16)],
        [output_share, swap(output_share, "tensor", 2)],
        name="output_pair",
        after=[small],
    )
    row_parts += [output_pair, swap(output_pair, "tensor", 1)]
    if split:
        (small,) = run(
            add_kernel,
            [sds(small.shape, F32)],
            [small, swap(small, "dp", 1)],
            name="small_sum",
        )
    if split:
        crossing = swap_chips(crossing, 4, 2)
        grad_expert_up, grad_expert_down = run(
            expert_final_kernel,
            [sds((EXPERTS, part, hidden_units), F32), sds((EXPERTS, part, hidden_units), F32)],
            [expert_own, crossing],
            name="expert_final", out=None,
        )
        grad_expert_down = grad_expert_down.transpose(0, 2, 1)
        weight_own, weight_sent = run(
            weight_cross_kernel,
            [
                sds((part + SMALL_ROWS, weight_cols), F32),
                sds((part + SMALL_ROWS, weight_cols), BF16),
            ],
            [weight_kept, crossing, small, swap_chips(small, 4, 2)],
            name="weight_cross",
            after=row_parts[1:members],
        )
        per = part // members
        done = [pltpu.with_memory_space_constraint(grad_expert_up, pltpu.HBM)]
        (
            output,
            grad_inputs,
            grad_query_weight,
            grad_key_weight,
            grad_value_weight,
            grad_out_weight,
            grad_gain_attn,
            grad_gain_expert,
            grad_router,
            grad_table,
        ) = run(
            bind(finish_kernel, members),
            [sds((length, width), BF16)] * 2
            + [sds((part, cols), F32)] * 3
            + [sds((cols, part), F32), sds((1, per), F32), sds((1, per), F32)]
            + [sds((EXPERTS, per), F32), sds((heads, bucket_count), F32)],
            [weight_own, swap_chips(weight_sent, 2, 4)] + row_parts,
            name="finish",
            out=None,
            after=done,
        )
        grad_table = grad_table.T
        grad_router = grad_router.T
        grad_gain_attn = grad_gain_attn.reshape(per)
        grad_gain_expert = grad_gain_expert.reshape(per)
    else:

        def scatter(values, axes, dimension):
            return lax.psum_scatter(values, axes, scatter_dimension=dimension, tiled=True)

        def pick(values):
            at = lax.axis_index("tensor") * (part // members)
            return lax.dynamic_slice_in_dim(scatter(values, "dp", 0), at, part // members)

        grads = expert_grads[0].reshape(width, EXPERTS, 2, hidden_units)
        grad_expert_up = scatter(grads[:, :, 0].transpose(1, 0, 2), "dp", 1)
        grad_expert_down = scatter(grads[:, :, 1].transpose(1, 2, 0), "dp", 2)
        grads = weight_grads[0]
        grad_query_weight = scatter(grads[:, 0:cols], "dp", 0)
        grad_key_weight = scatter(grads[:, cols : 2 * cols], "dp", 0)
        grad_value_weight = scatter(grads[:, 2 * cols : 3 * cols], "dp", 0)
        grad_out_weight = scatter(grads[:, 3 * cols :].T, "dp", 1)
        grad_table = lax.psum(small[TABLE_ROW : TABLE_ROW + heads, :bucket_count].T, "dp")
        grad_gain_attn = pick(small[0])
        grad_gain_expert = pick(small[1])
        grad_router = pick(small[2:TABLE_ROW].T)
        output, grad_inputs = run(
            rows_kernel, [sds((length, width), BF16)] * 2, row_parts, name="rows", out=None
        )
    return (
        output,
        grad_inputs,
        grad_gain_attn,
        grad_table,
        grad_query_weight,
        grad_key_weight,
        grad_value_weight,
        grad_out_weight,
        grad_gain_expert,
        grad_router,
        grad_expert_up,
        grad_expert_down,
    )


def solution(mesh):
    return jax.shard_map(
        shards,
        mesh=mesh,
        in_specs=(
            P("dp", None),
            P("dp", None),
            P(),
            P("dp"),
            P("dp"),
            P(),
            P(None, "tensor"),
            P(None, "tensor"),
            P(None, "tensor"),
            P(None, "tensor"),
            P("tensor", None),
            P(),
            P(),
            P(None, None, "tensor"),
            P(None, "tensor", None),
            P("dp", None),
        ),
        out_specs=(
            P("dp", None),
            P("dp", None),
            P(("dp", "tensor")),
            P(None, "tensor"),
            P("dp", "tensor"),
            P("dp", "tensor"),
            P("dp", "tensor"),
            P("tensor", "dp"),
            P(("dp", "tensor")),
            P(("dp", "tensor"), None),
            P(None, "dp", "tensor"),
            P(None, "tensor", "dp"),
        ),
        check_vma=False,
    )
```

```python
import functools
import math

import jax
import jax.numpy as jnp
from jax import lax
from jax.experimental import pallas as pl
from jax.experimental.pallas import tpu as pltpu
from jax.sharding import PartitionSpec as P

HEAD_DIM = 64
EXPERTS = 2
CAP = 144
EPS = 1e-06
SMALL_ROWS = 16
GAIN_ROWS = 8
TABLE_ROW = 2 + EXPERTS
WEIGHTS = {
    "fetch": 20,
    "expert": 5,
    "expert_grads": 20,
    "hidden_back": 60,
    "expert_merge": 20,
    "attention_back": 5,
    "pair_sum": 8,
    "weight_grads": 4,
    "expert_cross": 8,
    "input_back": 60,
    "expert_final": 0.001,
    "finish": 0.001,
    "small_sum": 0.001,
    "weight_cross": 0.001,
}
BF16 = jnp.bfloat16
F32 = jnp.float32
HIGHEST = lax.Precision.HIGHEST
NT = (((1,), (1,)), ((), ()))
TN = (((0,), (0,)), ((), ()))
GELU_C = 0.7978845608028654
GELU_A = 0.044715


def dot(a, b):
    return jnp.dot(a, b, preferred_element_type=F32)


def dot_nt(a, b, precision=None):
    return lax.dot_general(a, b, NT, preferred_element_type=F32, precision=precision)


def dot_tn(a, b):
    return lax.dot_general(a, b, TN, preferred_element_type=F32)


def inverse_rms(values):
    return lax.rsqrt(jnp.mean(values * values, axis=-1, keepdims=True) + EPS)


def share_of(index, rows):
    return pl.ds(pl.multiple_of(index * rows, rows), rows)


def distance(place, members):
    return (members - place) % members


def member_at(place, members):
    return jnp.bitwise_xor(lax.axis_index("tensor"), distance(place, members))


def put_shares(acc_ref, share_refs):
    for i, ref in enumerate(share_refs):
        there = share_of(member_at(i, len(share_refs)), ref.shape[0])
        ref[...] = acc_ref[there, :].astype(ref.dtype)


def assemble(full_ref, share_refs):
    for i, ref in enumerate(share_refs):
        full_ref[share_of(member_at(i, len(share_refs)), ref.shape[0]), :] = ref[...]


def total_of(refs):
    total = refs[0][...].astype(F32)
    for ref in refs[1:]:
        total = total + ref[...].astype(F32)
    return total


def column_of(row, length):
    eye = lax.broadcasted_iota(jnp.int32, (length, length), 0) == lax.broadcasted_iota(
        jnp.int32, (length, length), 1
    )
    return jnp.sum(jnp.where(eye, row, jnp.zeros_like(row)), axis=1, keepdims=True)


def head_mask(head, width):
    lane = lax.broadcasted_iota(jnp.int32, (1, width), 1)
    return (lane >= head * HEAD_DIM) & (lane < (head + 1) * HEAD_DIM)


def masked(values, head):
    return jnp.where(head_mask(head, values.shape[1]), values, jnp.zeros_like(values))


def bucket_hot_of(buckets_ref, bucket_count):
    offsets = buckets_ref.shape[1]
    return (
        lax.broadcasted_iota(jnp.int32, (bucket_count, offsets), 0) == buckets_ref[...]
    ).astype(F32)


def attention_kernel(members, *refs):
    sources, outs = refs[:9], refs[9 : members + 15]
    normed_o, q_o, k_o, v_o, probs_o, mixed_o = outs[members:]
    acc, offset_rows = refs[members + 15 : members + 17]
    local, sems = refs[members + 17 : members + 26], refs[members + 26]
    copies = [
        pltpu.make_async_copy(source, held, sems.at[i])
        for i, (source, held) in enumerate(zip(sources, local))
    ]
    for copy in copies:
        copy.start()
    buckets, table, segment, inputs, gain, wq, wk, wv, wo = local
    length = inputs.shape[0]
    heads = wq.shape[0] // HEAD_DIM
    for copy in copies[:3]:
        copy.wait()
    hot = bucket_hot_of(buckets, table.shape[1])
    seg_row = segment[...].astype(F32)
    same = column_of(seg_row, length) == seg_row
    offset_rows[...] = jnp.zeros_like(offset_rows)
    offset_rows[0:heads, 0 : hot.shape[1]] = jnp.dot(
        table[...], hot, preferred_element_type=F32, precision=HIGHEST
    )
    for h in range(heads):
        spread = jnp.broadcast_to(offset_rows[h : h + 1, :], (length, 2 * length))
        bias = pltpu.roll(spread, length + 1, 1, stride=1, stride_axis=0)[:, :length]
        probs_o[h] = jnp.where(same, bias, -1e30)
    copies[3].wait()
    x = inputs[...].astype(F32)
    scaled = x * inverse_rms(x)
    for copy in copies[4:8]:
        copy.wait()
    normed = (scaled * gain[...].reshape(1, -1)).astype(BF16)
    normed_o[...] = normed
    q = dot_nt(normed, wq[...]).astype(BF16)
    k = dot_nt(normed, wk[...]).astype(BF16)
    v = dot_nt(normed, wv[...]).astype(BF16)
    q_o[...] = q
    k_o[...] = k
    v_o[...] = v
    mixed = jnp.zeros((length, wq.shape[0]), F32)
    for h in range(heads):
        scores = dot_nt(masked(q, h), k) + probs_o[h]
        shifted = jnp.exp(scores - jnp.max(scores, axis=-1, keepdims=True))
        probs = shifted / jnp.sum(shifted, axis=-1, keepdims=True)
        probs_o[h] = probs
        mixed = mixed + dot(probs.astype(BF16), masked(v, h))
    mixed = mixed.astype(BF16)
    mixed_o[...] = mixed
    copies[8].wait()
    acc[...] = dot(mixed, wo[...])
    put_shares(acc, outs[:members])
    own = share_of(lax.axis_index("tensor"), outs[0].shape[0])
    outs[0][...] += inputs[own, :].astype(F32)


def hidden_kernel(members, gain, *rest):
    hidden_o, normed_o = rest[members:]
    hidden = total_of(rest[:members])
    hidden_o[...] = hidden
    normed_o[...] = (hidden * inverse_rms(hidden) * gain[...]).astype(BF16)


def place_of(where_to):
    slots = lax.broadcasted_iota(jnp.int32, (EXPERTS * CAP, where_to.shape[1]), 0)
    return (slots == where_to[...]).astype(BF16)


def fetch_kernel(up, down, up_o, down_o, sems):
    copies = [
        pltpu.make_async_copy(up, up_o, sems.at[0]),
        pltpu.make_async_copy(down, down_o, sems.at[1]),
    ]
    for copy in copies:
        copy.start()
    for copy in copies:
        copy.wait()


def expert_kernel(members, where_to, cotangent, router_t, up, down, *rest):
    pieces = rest[:members]
    rest = rest[members:]
    back_o, rows = rest[:members], rest[members]
    buffer_o, active_o, grad_before_o, grad_expert_o, router_o, dy_o = rest[
        members + 1 : members + 7
    ]
    normed, backs, acc = rest[members + 7 :]
    length = cotangent.shape[0]
    assemble(normed, pieces)
    dy_o[...] = cotangent[share_of(lax.axis_index("tensor"), dy_o.shape[0]), :]
    place = place_of(where_to)
    buffer = dot(place, normed[...]).astype(BF16)
    buffer_o[...] = buffer
    dy_buffer = dot(place, cotangent[...])
    router_rows = router_t[...].astype(F32)
    router_grad = [jnp.zeros((1, buffer.shape[1]), F32) for _ in range(EXPERTS)]
    for e in range(EXPERTS):
        slot = slice(e * CAP, (e + 1) * CAP)
        rows_in = buffer[slot]
        logits = dot_nt(rows_in, router_t[...])
        shifted = jnp.exp(logits - jnp.max(logits, axis=-1, keepdims=True))
        router_probs = shifted / jnp.sum(shifted, axis=-1, keepdims=True)
        gate = router_probs[:, e : e + 1]
        dy = dy_buffer[slot]
        grad_expert = (dy * gate).astype(BF16)
        grad_expert_o[slot, :] = grad_expert
        before = dot(rows_in, up[e])
        inner = jnp.tanh(GELU_C * (before + GELU_A * before * before * before))
        active = (0.5 * before * (1.0 + inner)).astype(BF16)
        active_o[slot, :] = active
        slope = 0.5 * (1.0 + inner) + 0.5 * before * (1.0 - inner * inner) * GELU_C * (
            1.0 + 3.0 * GELU_A * before * before
        )
        result = dot(active, down[e])
        grad_before = (dot_nt(grad_expert, down[e]) * slope).astype(BF16)
        grad_before_o[slot, :] = grad_before
        rows[slot, :] = (result * gate).astype(BF16)
        scaled = jnp.sum(dy * result, axis=-1, keepdims=True) * gate
        back = dot_nt(grad_before, up[e])
        for other in range(EXPERTS):
            own = 1.0 if other == e else 0.0
            grad_logit = scaled * (own - router_probs[:, other : other + 1])
            router_grad[other] = router_grad[other] + jnp.sum(
                grad_logit * rows_in.astype(F32), axis=0, keepdims=True
            )
            back = back + grad_logit * router_rows[other : other + 1, :]
        backs[slot, :] = back.astype(BF16)
    for other in range(EXPERTS):
        router_o[other : other + 1, :] = router_grad[other]
    acc[...] = dot_tn(place, backs[...])
    put_shares(acc, back_o)


def split_rows(keep, send, chip, part):
    core = lax.rem(lax.axis_index("dp"), 2)
    return share_of(2 * chip + core, part), share_of(2 * chip + 1 - core, part)


def expert_grad_kernel(split, where_to, buffer, active, grad_before, grad_expert, rows, *rest):
    row_o, scratch, acc = rest[-4:-2], rest[-2], rest[-1]
    place = place_of(where_to)
    acc[...] = dot_tn(place, rows[...])
    me = lax.axis_index("tensor")
    share = row_o[0].shape[0] // 2
    for first, ref in enumerate(row_o):
        for k in range(2):
            index = jnp.bitwise_xor(me, first + 2 * k)
            ref[k * share : (k + 1) * share, :] = acc[share_of(index, share), :].astype(BF16)
    for e in range(EXPERTS):
        slot = slice(e * CAP, (e + 1) * CAP)
        for which in range(2):
            if which == 0:
                product = dot_tn(buffer[slot, :], grad_before[slot, :])
            else:
                product = dot_tn(grad_expert[slot, :], active[slot, :])
            hidden_units = active.shape[1]
            first = (2 * e + which) * hidden_units
            if not split:
                rest[0][:, first : first + hidden_units] = product
                continue
            keep, send = rest[0], rest[1]
            part = keep.shape[1]
            scratch[...] = product
            for chip in range(keep.shape[0]):
                mine, other = split_rows(keep, send, chip, part)
                keep[chip, :, first : first + hidden_units] = scratch[mine, :].astype(BF16)
                send[chip, :, first : first + hidden_units] = scratch[other, :].astype(BF16)


def chip_bits():
    core = lax.rem(lax.axis_index("dp"), 2)
    return 1 + core, 2 - core


def merge_kernel(kept, came, keep, send):
    chip = lax.div(lax.axis_index("dp"), 2)
    first, second = chip_bits()
    for ref, start in ((keep, chip), (send, jnp.bitwise_xor(chip, first))):
        for k, there in enumerate((start, jnp.bitwise_xor(start, second))):
            total = kept[there].astype(F32) + came[there].astype(F32)
            ref[k] = total.astype(ref.dtype)


def add_kernel(one, other, out):
    out[...] = one[...] + other[...]


def expert_cross_kernel(kept, came, own, send):
    own[...] = kept[0] + came[0].astype(F32)
    send[...] = (kept[1] + came[1].astype(F32)).astype(BF16)


def cross_kernel(expert_send, weight_kept, weight_came, send, weight_keep):
    rows = expert_send.shape[0]
    send[0:rows, :] = expert_send[...]
    chip = lax.div(lax.axis_index("dp"), 2)
    second, first = chip_bits()
    width = weight_keep.shape[2]
    half = rows // 2
    for k in range(2):
        mine = jnp.bitwise_xor(chip, k * second)
        weight_keep[k] = weight_kept[mine].astype(F32) + weight_came[mine].astype(F32)
        there = jnp.bitwise_xor(mine, first)
        total = (weight_kept[there].astype(F32) + weight_came[there].astype(F32)).astype(BF16)
        for i in range(2):
            at = (2 * k + i) * width
            send[rows : rows + half, at : at + width] = total[i * half : (i + 1) * half]


def weight_cross_kernel(kept, came, small, small_came, own, send):
    width = own.shape[1]
    rows = kept.shape[1]
    half = rows // 2
    total = jnp.concatenate([small[...] + small_came[...], jnp.zeros_like(small)], axis=0)
    for k, ref in enumerate((own, send)):
        for i in range(2):
            at = (2 * k + i) * width
            arrived = came[rows : rows + half, at : at + width].astype(F32)
            part = slice(i * half, (i + 1) * half)
            ref[part, :] = (kept[k, part, :] + arrived).astype(ref.dtype)
        ref[rows:, :] = total.astype(ref.dtype)


def expert_final_kernel(*refs):
    up_o, down_o = refs[2:]
    total = refs[0][...] + refs[1][0 : refs[0].shape[0], :].astype(F32)
    for e in range(EXPERTS):
        width = up_o.shape[2]
        first = 2 * e * width
        up_o[e] = total[:, first : first + width]
        down_o[e] = total[:, first + width : first + 2 * width]


def pair_sum_kernel(kept, came, own, other):
    share = own.shape[0]
    own[...] = kept[0:share, :].astype(F32) + came[0:share, :].astype(F32)
    other[...] = (kept[share:, :].astype(F32) + came[share:, :].astype(F32)).astype(BF16)


def pair_kernel(own, came, out):
    share = own.shape[0]
    out[0:share, :] = own[...]
    out[share:, :] = came[...]


def rows_kernel(*refs):
    shares, pairs, (output, grad_inputs) = refs[:-4], refs[-4:-2], refs[-2:]
    assemble(grad_inputs, shares)
    me = lax.axis_index("tensor")
    rows = output.shape[0] // len(shares)
    for near, ref in enumerate(pairs):
        for k in range(2):
            there = jnp.bitwise_xor(me, near + 2 * k)
            output[share_of(there, rows), :] = ref[k * rows : (k + 1) * rows, :]


def hidden_back_kernel(members, hidden, cotangent, gain, *rest):
    parts = rest[:members]
    grad_o, low_o, gain_o = rest[members:]
    h = hidden[...]
    dy = cotangent[...].astype(F32)
    r = inverse_rms(h)
    grad_normed = total_of(parts)
    z = grad_normed * gain[...]
    gain_o[...] = jnp.sum(grad_normed * h * r, axis=0, keepdims=True)
    grad = dy + r * z - h * (r * r * r) * jnp.mean(z * h, axis=-1, keepdims=True)
    grad_o[...] = grad
    low_o[...] = grad.astype(BF16)


def attention_back_kernel(
    members, inputs, probs, q, k, v, wq, wk, wv, wo, gain_two, router, *rest
):
    pieces = rest[:members]
    rest = rest[members:]
    share_o = rest[:members]
    grads_o, attended_o, scores_o = rest[members : members + 3]
    acc = rest[members + 3]
    assemble(attended_o, pieces)
    heads = wq.shape[0] // HEAD_DIM
    grad_mixed = dot_nt(attended_o[...], wo[...]).astype(BF16)
    qv, kv, vv = q[...], k[...], v[...]
    dq = jnp.zeros(qv.shape, F32)
    dk = jnp.zeros(qv.shape, F32)
    dv = jnp.zeros(qv.shape, F32)
    for h in range(heads):
        grad_mixed_h = masked(grad_mixed, h)
        p = probs[h]
        grad_probs = dot_nt(grad_mixed_h, vv)
        inner = jnp.sum(p * grad_probs, axis=-1, keepdims=True)
        grad_scores = (p * (grad_probs - inner)).astype(BF16)
        scores_o[h] = grad_scores
        dq = dq + dot(grad_scores, masked(kv, h))
        dk = dk + dot_tn(grad_scores, masked(qv, h))
        dv = dv + dot_tn(p.astype(BF16), grad_mixed_h)
    dq, dk, dv = dq.astype(BF16), dk.astype(BF16), dv.astype(BF16)
    grads_o[0] = dq
    grads_o[1] = dk
    grads_o[2] = dv
    total = dot(dq, wq[...]) + dot(dk, wk[...]) + dot(dv, wv[...])
    acc[...] = total
    x = inputs[...].astype(F32)
    gain_one = jnp.sum(total * x * inverse_rms(x), axis=0, keepdims=True)
    small = jnp.concatenate(
        [
            gain_one,
            gain_two[...],
            router[...],
            jnp.zeros((GAIN_ROWS - TABLE_ROW, gain_one.shape[1]), F32),
        ],
        axis=0,
    )
    for i, ref in enumerate(share_o):
        share = ref.shape[0] - GAIN_ROWS
        ref[0:share, :] = acc[share_of(member_at(i, members), share), :].astype(ref.dtype)
        ref[share:, :] = small.astype(ref.dtype)


def weight_grad_kernel(
    split, normed, grads, attended, mixed, scores, buckets, *rest
):
    bucket_count = 32
    small, scratch = rest[-2:]
    length = normed.shape[0]
    cols = grads.shape[2]
    normed_v = normed[...]
    for i in range(4):
        if i < 3:
            product = dot_tn(normed_v, grads[i])
        else:
            product = dot_tn(attended[...], mixed[...])
        scratch[:, i * cols : (i + 1) * cols] = product
    small[...] = jnp.zeros_like(small)
    flip = (
        lax.broadcasted_iota(jnp.int32, (length, length), 0)
        + lax.broadcasted_iota(jnp.int32, (length, length), 1)
        == length - 1
    ).astype(BF16)
    hot = (
        lax.broadcasted_iota(jnp.int32, (bucket_count, 2 * length), 0) == buckets[...]
    ).astype(F32)
    for h in range(scores.shape[0]):
        flipped = dot(flip, scores[h])
        wide = jnp.concatenate([flipped, jnp.zeros_like(flipped)], axis=1)
        sheared = pltpu.roll(wide, 0, 1, stride=1, stride_axis=0)
        offsets = jnp.sum(sheared, axis=0, keepdims=True)
        small[TABLE_ROW + h : TABLE_ROW + h + 1, 0:bucket_count] = dot_nt(
            jnp.broadcast_to(offsets, (8, 2 * length)), hot, HIGHEST
        )[0:1]
    if not split:
        rest[0][...] = scratch[...]
        return
    keep, send = rest[0], rest[1]
    chips, part, _ = keep.shape
    for chip in range(chips):
        mine, other = split_rows(keep, send, chip, part)
        keep[chip] = scratch[mine, :].astype(BF16)
        send[chip] = scratch[other, :].astype(BF16)


def weight_final_kernel(members, own, came, *outs):
    wq_o, wk_o, wv_o, wo_o, one_o, two_o, router_o, table_o = outs
    total = total_of((own, came))
    part, cols = wq_o.shape
    wq_o[...] = total[0:part, 0:cols]
    wk_o[...] = total[0:part, cols : 2 * cols]
    wv_o[...] = total[0:part, 2 * cols : 3 * cols]
    wo_o[...] = total[0:part, 3 * cols : 4 * cols].T
    small = total[part:]
    heads, bucket_count = table_o.shape
    table_o[...] = small[TABLE_ROW : TABLE_ROW + heads, 0:bucket_count]
    per = one_o.shape[1]
    first = (lax.axis_index("dp") * members + lax.axis_index("tensor")) * per
    shape = (per, small.shape[1])
    pick = (
        lax.broadcasted_iota(jnp.int32, shape, 0) + first
        == lax.broadcasted_iota(jnp.int32, shape, 1)
    ).astype(F32)
    rows = dot_nt(small, pick, HIGHEST)
    one_o[...] = rows[0:1]
    two_o[...] = rows[1:2]
    router_o[...] = rows[2:TABLE_ROW]


def output_kernel(hidden, own, came, out):
    out[...] = (hidden[...] + own[...] + came[...].astype(F32)).astype(BF16)


def finish_kernel(members, *refs):
    weight_in, row_in, outs = refs[:2], refs[2 : members + 4], refs[members + 4 :]
    weight_final_kernel(members, *weight_in, *outs[2:])
    rows_kernel(*row_in, *outs[:2])


def input_back_kernel(members, inputs, gain, grad_hidden, table, *rest):
    out, small_o = rest[members:]
    share = out.shape[0]
    x = inputs[share_of(lax.axis_index("tensor"), share), :].astype(F32)
    r = inverse_rms(x)
    total = total_of(rest[:members])
    small_o[...] = total[share:] + table[...]
    z = total[0:share] * gain[...]
    out[...] = (
        grad_hidden[...] + r * z - x * (r * r * r) * jnp.mean(z * x, axis=-1, keepdims=True)
    ).astype(BF16)


def run(kernel, outs, args, scratch=(), name=None, after=(), space=pltpu.VMEM, out=pltpu.VMEM):
    vmem = pl.BlockSpec(memory_space=pltpu.VMEM)
    anywhere = pl.BlockSpec(memory_space=pl.ANY)
    count, extra = len(args), len(after)
    held = [*args, *outs, *(x for x in scratch if x.memory_space == pltpu.VMEM)]
    size = sum(math.prod(x.shape) * jnp.dtype(x.dtype).itemsize for x in held)

    def body(*refs):
        kernel(*refs[:count], *refs[count + extra :])

    return pl.pallas_call(
        body,
        out_shape=[out(o.shape, o.dtype) for o in outs] if out else outs,
        in_specs=[pl.BlockSpec(memory_space=space)] * count + [anywhere] * extra,
        out_specs=[vmem] * len(outs),
        scratch_shapes=list(scratch),
        compiler_params=pltpu.CompilerParams(vmem_limit_bytes=size + size // 4 + 4 * 1024 * 1024),
        cost_estimate=pl.CostEstimate(
            flops=int(WEIGHTS.get(name, 0.2) * 1e9), bytes_accessed=0, transcendentals=0
        ),
        name=name,
    )(*args, *after)


def sds(shape, dtype):
    return jax.ShapeDtypeStruct(tuple(shape), dtype)


def swap(values, axis, k):
    size = lax.axis_size(axis)
    return lax.ppermute(values, axis, [(i, i ^ k) for i in range(size)])


def swap_chips(values, even, odd):
    size = lax.axis_size("dp")
    pairs = [(i, i ^ (odd if i % 2 else even)) for i in range(size)]
    return lax.ppermute(values, "dp", pairs)


def exchange(shares):
    members = len(shares)
    sent = [swap(s, "tensor", distance(i, members)) for i, s in enumerate(shares) if i > 0]
    return [shares[0]] + sent


def spread(share):
    return exchange([share] * lax.axis_size("tensor"))


def shards(
    inputs,
    segments,
    buckets,
    routes,
    capacity_slots,
    gain_attn,
    bias_table,
    query_weight,
    key_weight,
    value_weight,
    out_weight,
    gain_expert,
    router_weight,
    expert_up,
    expert_down,
    cotangent,
):
    length, width = inputs.shape
    members = lax.axis_size("tensor")
    dp = lax.axis_size("dp")
    share = length // members
    cols = query_weight.shape[1]
    heads = cols // HEAD_DIM
    hidden_units = expert_up.shape[2]
    bucket_count = bias_table.shape[0]
    part = width // dp
    split = dp == 8 and part % 16 == 0
    chips = dp // 2
    bind = functools.partial

    def shares_sds(dtype, own=None):
        return [sds((share, width), own or dtype)] + [
            sds((share, width), dtype) for _ in range(members - 1)
        ]

    gain_row = gain_attn.reshape(1, width)
    gain_two_row = gain_expert.reshape(1, width)
    bucket_row = buckets.reshape(1, -1)
    bucket_wide = jnp.pad(bucket_row, ((0, 0), (0, 1)), constant_values=-1)
    where_to = (routes * CAP + capacity_slots).reshape(1, length)
    router_t = router_weight.T
    query_t, key_t, value_t = query_weight.T, key_weight.T, value_weight.T

    attention_args = [
        bucket_row,
        bias_table.T,
        segments,
        inputs,
        gain_attn,
        query_t,
        key_t,
        value_t,
        out_weight,
    ]
    attention_args = [pltpu.with_memory_space_constraint(a, pltpu.HBM) for a in attention_args]
    outs = run(
        bind(attention_kernel, members),
        shares_sds(BF16, F32)
        + [sds((length, width), BF16)]
        + [sds((length, cols), BF16)] * 3
        + [sds((heads, length, length), F32), sds((length, cols), BF16)],
        attention_args,
        [pltpu.VMEM((length, width), F32), pltpu.VMEM((8, 2 * length), F32)]
        + [pltpu.VMEM(a.shape, a.dtype) for a in attention_args]
        + [pltpu.SemaphoreType.DMA((len(attention_args),))],
        name="attention",
        space=pltpu.HBM,
    )
    attended = exchange(outs[:members])
    normed, q, k, v, probs, mixed = outs[members:]

    hidden, normed_two = run(
        bind(hidden_kernel, members),
        [sds((share, width), F32), sds((share, width), BF16)],
        [gain_two_row] + attended,
        name="hidden",
    )
    up, down = run(
        fetch_kernel,
        [sds(expert_up.shape, BF16), sds(expert_down.shape, BF16)],
        [pltpu.with_memory_space_constraint(a, pltpu.HBM) for a in (expert_up, expert_down)],
        [pltpu.SemaphoreType.DMA((2,))],
        name="fetch",
        space=pltpu.HBM,
        after=[normed_two],
    )
    normed_two = spread(normed_two)

    slots = EXPERTS * CAP
    outs = run(
        bind(expert_kernel, members),
        shares_sds(BF16)
        + [sds((slots, width), BF16)] * 2
        + [sds((slots, hidden_units), BF16)] * 2
        + [sds((slots, width), BF16), sds((EXPERTS, width), F32), sds((share, width), BF16)],
        [where_to, cotangent, router_t, up, down] + normed_two,
        [
            pltpu.VMEM((length, width), BF16),
            pltpu.VMEM((slots, width), BF16),
            pltpu.VMEM((length, width), F32),
        ],
        name="expert",
    )
    back_rows = exchange(outs[:members])
    slot_rows, buffer, active, grad_before, grad_expert, grad_router, dy_share = outs[members:]

    def split_sds(rows, columns):
        return [sds((chips, rows, columns), BF16)] * 2

    def merge_sds(rows, columns):
        return [sds((2, rows, columns), F32), sds((2, rows, columns), BF16)]

    expert_grads = run(
        bind(expert_grad_kernel, split),
        (split_sds(part, 4 * hidden_units) if split else [sds((width, 4 * hidden_units), F32)])
        + [sds((2 * share, width), BF16)] * 2,
        [where_to, buffer, active, grad_before, grad_expert, slot_rows],
        [pltpu.VMEM((width, hidden_units), F32), pltpu.VMEM((length, width), F32)],
        name="expert_grads",
    )

    rows_kept, rows_sent = expert_grads[-2:]
    grad_hidden, grad_attended, grad_gain_expert = run(
        bind(hidden_back_kernel, members),
        [sds((share, width), F32), sds((share, width), BF16), sds((1, width), F32)],
        [hidden, dy_share, gain_two_row] + back_rows,
        name="hidden_back",
        after=expert_grads[-1:],
    )
    grad_attended = spread(grad_attended)

    expert_merged = []
    if split:
        expert_merged = run(
            merge_kernel,
            merge_sds(part, 4 * hidden_units),
            [expert_grads[0], swap(expert_grads[1], "dp", 1)],
            name="expert_merge",
        )
    own_rows, other_rows = run(
        pair_sum_kernel,
        [sds((share, width), F32), sds((share, width), BF16)],
        [rows_kept, swap(rows_sent, "tensor", 1)],
        name="pair_sum",
        after=expert_merged[:1],
    )
    crossed = []

    def tall_sds(dtype):
        return sds((share + GAIN_ROWS, width), dtype)

    outs = run(
        bind(attention_back_kernel, members),
        [tall_sds(F32)]
        + [tall_sds(BF16)] * (members - 1)
        + [
            sds((3, length, cols), BF16),
            sds((length, width), BF16),
            sds((heads, length, length), BF16),
        ],
        [inputs, probs, q, k, v, query_t, key_t, value_t, out_weight]
        + [grad_gain_expert, grad_router]
        + grad_attended,
        [pltpu.VMEM((length, width), F32)],
        name="attention_back",
        after=[own_rows, *expert_merged[:1]],
    )
    grad_normed = exchange(outs[:members])
    projections, attended_low, grad_scores = outs[members:]

    (output_share,) = run(
        output_kernel,
        [sds((share, width), BF16)],
        [hidden, own_rows, swap(other_rows, "tensor", 2)],
        name="output_share",
    )
    weight_cols = 4 * cols
    weight_grads = run(
        bind(weight_grad_kernel, split),
        (split_sds(part, weight_cols) if split else [sds((width, weight_cols), F32)])
        + [sds((8, width), F32)],
        [normed, projections, attended_low, mixed, grad_scores, bucket_wide],
        [pltpu.VMEM((width, weight_cols), F32)],
        name="weight_grads",
        after=[output_share],
    )

    if split:
        expert_own, expert_sent = run(
            expert_cross_kernel,
            [sds((part, 4 * hidden_units), F32), sds((part, 4 * hidden_units), BF16)],
            [expert_merged[0], swap_chips(expert_merged[1], 2, 4)],
            name="expert_cross",
            after=weight_grads[-1:],
        )
        crossing, weight_kept = run(
            cross_kernel,
            [
                sds((part + part // 2, 4 * hidden_units), BF16),
                sds((2, part, weight_cols), F32),
            ],
            [expert_sent, weight_grads[0], swap(weight_grads[1], "dp", 1)],
            name="cross",
        )
        crossed = [weight_kept]
    grad_share, small = run(
        bind(input_back_kernel, members),
        [sds((share, width), BF16), sds((8, width), F32)],
        [inputs, gain_row, grad_hidden, weight_grads[-1]]
        + grad_normed,
        name="input_back",
        after=crossed,
    )
    row_parts = spread(grad_share)
    (output_pair,) = run(
        pair_kernel,
        [sds((2 * share, width), BF16)],
        [output_share, swap(output_share, "tensor", 2)],
        name="output_pair",
        after=[small],
    )
    row_parts += [output_pair, swap(output_pair, "tensor", 1)]
    if split:
        (small,) = run(
            add_kernel,
            [sds(small.shape, F32)],
            [small, swap(small, "dp", 1)],
            name="small_sum",
        )
    if split:
        crossing = swap_chips(crossing, 4, 2)
        grad_expert_up, grad_expert_down = run(
            expert_final_kernel,
            [sds((EXPERTS, part, hidden_units), F32), sds((EXPERTS, part, hidden_units), F32)],
            [expert_own, crossing],
            name="expert_final", out=None,
        )
        grad_expert_down = grad_expert_down.transpose(0, 2, 1)
        weight_own, weight_sent = run(
            weight_cross_kernel,
            [
                sds((part + SMALL_ROWS, weight_cols), F32),
                sds((part + SMALL_ROWS, weight_cols), BF16),
            ],
            [weight_kept, crossing, small, swap_chips(small, 4, 2)],
            name="weight_cross",
            after=row_parts[1:members],
        )
        per = part // members
        done = [pltpu.with_memory_space_constraint(grad_expert_up, pltpu.HBM)]
        (
            output,
            grad_inputs,
            grad_query_weight,
            grad_key_weight,
            grad_value_weight,
            grad_out_weight,
            grad_gain_attn,
            grad_gain_expert,
            grad_router,
            grad_table,
        ) = run(
            bind(finish_kernel, members),
            [sds((length, width), BF16)] * 2
            + [sds((part, cols), F32)] * 3
            + [sds((cols, part), F32), sds((1, per), F32), sds((1, per), F32)]
            + [sds((EXPERTS, per), F32), sds((heads, bucket_count), F32)],
            [weight_own, swap_chips(weight_sent, 2, 4)] + row_parts,
            name="finish",
            out=None,
            after=done,
        )
        grad_table = grad_table.T
        grad_router = grad_router.T
        grad_gain_attn = grad_gain_attn.reshape(per)
        grad_gain_expert = grad_gain_expert.reshape(per)
    else:

        def scatter(values, axes, dimension):
            return lax.psum_scatter(values, axes, scatter_dimension=dimension, tiled=True)

        def pick(values):
            at = lax.axis_index("tensor") * (part // members)
            return lax.dynamic_slice_in_dim(scatter(values, "dp", 0), at, part // members)

        grads = expert_grads[0].reshape(width, EXPERTS, 2, hidden_units)
        grad_expert_up = scatter(grads[:, :, 0].transpose(1, 0, 2), "dp", 1)
        grad_expert_down = scatter(grads[:, :, 1].transpose(1, 2, 0), "dp", 2)
        grads = weight_grads[0]
        grad_query_weight = scatter(grads[:, 0:cols], "dp", 0)
        grad_key_weight = scatter(grads[:, cols : 2 * cols], "dp", 0)
        grad_value_weight = scatter(grads[:, 2 * cols : 3 * cols], "dp", 0)
        grad_out_weight = scatter(grads[:, 3 * cols :].T, "dp", 1)
        grad_table = lax.psum(small[TABLE_ROW : TABLE_ROW + heads, :bucket_count].T, "dp")
        grad_gain_attn = pick(small[0])
        grad_gain_expert = pick(small[1])
        grad_router = pick(small[2:TABLE_ROW].T)
        output, grad_inputs = run(
            rows_kernel, [sds((length, width), BF16)] * 2, row_parts, name="rows", out=None
        )
    return (
        output,
        grad_inputs,
        grad_gain_attn,
        grad_table,
        grad_query_weight,
        grad_key_weight,
        grad_value_weight,
        grad_out_weight,
        grad_gain_expert,
        grad_router,
        grad_expert_up,
        grad_expert_down,
    )


def solution(mesh):
    return jax.shard_map(
        shards,
        mesh=mesh,
        in_specs=(
            P("dp", None),
            P("dp", None),
            P(),
            P("dp"),
            P("dp"),
            P(),
            P(None, "tensor"),
            P(None, "tensor"),
            P(None, "tensor"),
            P(None, "tensor"),
            P("tensor", None),
            P(),
            P(),
            P(None, None, "tensor"),
            P(None, "tensor", None),
            P("dp", None),
        ),
        out_specs=(
            P("dp", None),
            P("dp", None),
            P(("dp", "tensor")),
            P(None, "tensor"),
            P("dp", "tensor"),
            P("dp", "tensor"),
            P("dp", "tensor"),
            P("tensor", "dp"),
            P(("dp", "tensor")),
            P(("dp", "tensor"), None),
            P(None, "dp", "tensor"),
            P(None, "tensor", "dp"),
        ),
        check_vma=False,
    )
```
